128 devices in a mesh: pipe: 2 (over y_lo), dp: 32 (over z, x, core), mp: 2 (over y_hi).
Axes of the slice: x: 4, y: 4 (y_hi: 2, y_lo: 2; y = y_hi * 2 + y_lo), z: 4, core: 2. Of those that a mesh axis runs over, the one named last changes fastest.
Arguments:
- radar_tokens: bfloat16 [2, 16384, 768], P(None, 'dp'), may hold values from -6 to 6
- optical_tokens: bfloat16 [2, 16384, 768], P(None, 'dp'), may hold values from -6 to 6
- out_cotangent: bfloat16 [2, 16384, 768], P(None, 'dp'), may hold values from -6 to 6
- tile_sides: int32 [2, 96], P(None, 'dp'), may hold values from 0 to 20, as said below
- norm1_gain: float32 [2, 768], P('pipe'), may hold values from 0.5 to 1.5
- norm1_bias: float32 [2, 768], P('pipe'), may hold values from -3 to 3
- qkv_weight: bfloat16 [2, 768, 3, 768], P('pipe', None, None, 'mp'), may hold values from -0.21875 to 0.21875
- attn_weight: bfloat16 [2, 768, 768], P('pipe', 'mp'), may hold values from -0.4375 to 0.4375
- attn_bias: float32 [2, 768], P('pipe'), may hold values from -3 to 3
- norm2_gain: float32 [2, 768], P('pipe'), may hold values from 0.5 to 1.5
- norm2_bias: float32 [2, 768], P('pipe'), may hold values from -3 to 3
- up_weight: bfloat16 [2, 768, 3072], P('pipe', None, 'mp'), may hold values from -0.21875 to 0.21875
- up_bias: float32 [2, 3072], P('pipe'), may hold values from -3 to 3
- down_weight: bfloat16 [2, 3072, 768], P('pipe', 'mp'), may hold values from -0.109375 to 0.109375
- down_bias: float32 [2, 768], P('pipe'), may hold values from -3 to 3
- query_gain: float32 [768], replicated, may hold values from 0.5 to 1.5
- query_bias: float32 [768], replicated, may hold values from -3 to 3
- cross_query: bfloat16 [768, 768], P(None, 'mp'), may hold values from -0.21875 to 0.21875
- cross_keyval: bfloat16 [768, 2, 768], P(None, None, 'mp'), may hold values from -0.21875 to 0.21875
- cross_weight: bfloat16 [768, 768], P('mp'), may hold values from -0.4375 to 0.4375
- cross_bias: float32 [768], replicated, may hold values from -3 to 3
Outputs:
- joined_out: float32 [2, 16384, 768], P(None, ('dp', 'mp'), 'pipe')
- radar_grad: float32 [2, 16384, 768], P(None, ('dp', 'mp'), 'pipe')
- optical_grad: float32 [2, 16384, 768], P(None, ('dp', 'mp'), 'pipe')
- grad_norm1_gain: float32 [2, 768], P('pipe')
- grad_norm1_bias: float32 [2, 768], P('pipe')
- grad_qkv_weight: float32 [2, 768, 3, 768], P('pipe', 'dp', None, 'mp')
- grad_attn_weight: float32 [2, 768, 768], P('pipe', 'mp', 'dp')
- grad_attn_bias: float32 [2, 768], P('pipe')
- grad_norm2_gain: float32 [2, 768], P('pipe')
- grad_norm2_bias: float32 [2, 768], P('pipe')
- grad_up_weight: float32 [2, 768, 3072], P('pipe', 'dp', 'mp')
- grad_up_bias: float32 [2, 3072], P('pipe')
- grad_down_weight: float32 [2, 3072, 768], P('pipe', 'mp', 'dp')
- grad_down_bias: float32 [2, 768], P('pipe')
- grad_query_gain: float32 [768], replicated
- grad_query_bias: float32 [768], replicated
- grad_cross_query: float32 [768, 768], P(('pipe', 'dp'), 'mp')
- grad_cross_keyval: float32 [768, 2, 768], P(('pipe', 'dp'), None, 'mp')
- grad_cross_weight: float32 [768, 768], P('mp', ('pipe', 'dp'))
- grad_cross_bias: float32 [768], replicated
The draws below stay inside these ranges and needn't reach their ends.
Inputs may be any that keep to these rules, and one draw needn't show every extreme that they name: `tile_sides`: each buffer of one device and micro-batch lists 3 sides, nonzero ones (12, 15 or 20) first and 0 for unused places; a buffer holds one to three tiles, 369 to 450 patches of its 512 rows.
All inputs are finite; a program needn't handle non-finite values.
Results may differ from the reference program's by a relative error of at most 0.024.
Values may be sent and summed in bfloat16 or wider, within the bound.
A program may use at most 320 MiB of HBM per device.

```python
import jax
import jax.numpy as jnp
from jax import lax

D = 768
H = 12
HS = 64
FF = 3072
ROWS = 512
SLOTS = 3
MICRO = 2
N_PIPE = 2
N_DP = 32


def draw_tile_sides(key, part):
    key = jax.random.fold_in(key, 7)
    patterns = jnp.array([[20, 0, 0], [15, 15, 0], [12, 12, 12], [15, 12, 0], [12, 15, 0]], dtype=jnp.int32)
    pattern_index = jax.random.randint(key, (MICRO, N_DP), 0, 5)
    pattern_index = pattern_index.at[0, 0].set(1)
    pattern_index = pattern_index.at[MICRO - 1, N_DP - 1].set(0)
    chosen = patterns[pattern_index]
    return chosen.reshape(MICRO, N_DP * SLOTS).astype(jnp.int32)


def shard_levels(rng, extent, split, low, top_value):
    factor_of = 1.0
    for dim, parts in split:
        heights = jax.random.uniform(jax.random.fold_in(jax.random.fold_in(rng, 6), dim), (parts,), jnp.float32, low / len(split), top_value / len(split))
        factor_of = factor_of * jnp.repeat(jnp.exp(heights), extent[dim] // parts).reshape((-1,) + (1,) * (len(extent) - 1 - dim))
    return factor_of


def centred(key, dims, deviation, limit, shards=(), held_as=jnp.bfloat16):
    entries = jax.random.normal(key, dims, jnp.float32) * deviation
    if len(shards) > 0:
        entries = shard_levels(key, dims, shards, -0.22, 0.18) * entries
    return jnp.clip(entries, min=-limit, max=limit).astype(held_as)


def setup_inputs(seed: int = 0) -> dict:
    arg_keys = jax.random.split(jax.random.key(seed), 22)
    radar_tokens = centred(arg_keys[0], (MICRO, N_DP * ROWS, D), 1.0, 6.0, ((1, 32),))
    optical_tokens = centred(arg_keys[1], (MICRO, N_DP * ROWS, D), 1.0, 6.0, ((1, 32),))
    out_cotangent = centred(arg_keys[2], (MICRO, N_DP * ROWS, D), 1.0, 6.0, ((1, 32),))
    tile_sides = draw_tile_sides(jax.random.fold_in(arg_keys[21], 71), 0)
    norm1_gain = jnp.clip(1.0 + 0.1 * jax.random.normal(arg_keys[4], (N_PIPE, D), jnp.float32), 0.5, 1.5)
    norm1_bias = centred(arg_keys[5], (N_PIPE, D), 0.3, 3.0, ((0, 2),), jnp.float32)
    qkv_weight = centred(arg_keys[6], (N_PIPE, D, 3, D), D ** -0.5, 0.21875, ((0, 2), (3, 2)))
    attn_weight = centred(arg_keys[7], (N_PIPE, D, D), (D // 4) ** -0.5, 0.4375, ((0, 2), (1, 2)))
    attn_bias = centred(arg_keys[8], (N_PIPE, D), 0.3, 3.0, ((0, 2),), jnp.float32)
    norm2_gain = jnp.clip(1.0 + 0.1 * jax.random.normal(arg_keys[9], (N_PIPE, D), jnp.float32), 0.5, 1.5)
    norm2_bias = centred(arg_keys[10], (N_PIPE, D), 0.3, 3.0, ((0, 2),), jnp.float32)
    up_weight = centred(arg_keys[11], (N_PIPE, D, FF), D ** -0.5, 0.21875, ((0, 2), (2, 2)))
    up_bias = centred(arg_keys[12], (N_PIPE, FF), 0.3, 3.0, ((0, 2),), jnp.float32)
    down_weight = centred(arg_keys[13], (N_PIPE, FF, D), FF ** -0.5, 0.109375, ((0, 2), (1, 2)))
    down_bias = centred(arg_keys[14], (N_PIPE, D), 0.3, 3.0, ((0, 2),), jnp.float32)
    query_gain = jnp.clip(1.0 + 0.1 * jax.random.normal(arg_keys[15], (D,), jnp.float32), 0.5, 1.5)
    query_bias = centred(arg_keys[16], (D,), 0.3, 3.0, (), jnp.float32)
    cross_query = centred(arg_keys[17], (D, D), D ** -0.5, 0.21875, ((1, 2),))
    cross_keyval = centred(arg_keys[18], (D, 2, D), D ** -0.5, 0.21875, ((2, 2),))
    cross_weight = centred(arg_keys[19], (D, D), (D // 4) ** -0.5, 0.4375, ((0, 2),))
    cross_bias = centred(arg_keys[20], (D,), 0.3, 3.0, (), jnp.float32)
    return {"radar_tokens": radar_tokens, "optical_tokens": optical_tokens, "out_cotangent": out_cotangent, "tile_sides": tile_sides, "norm1_gain": norm1_gain, "norm1_bias": norm1_bias, "qkv_weight": qkv_weight, "attn_weight": attn_weight, "attn_bias": attn_bias, "norm2_gain": norm2_gain, "norm2_bias": norm2_bias, "up_weight": up_weight, "up_bias": up_bias, "down_weight": down_weight, "down_bias": down_bias, "query_gain": query_gain, "query_bias": query_bias, "cross_query": cross_query, "cross_keyval": cross_keyval, "cross_weight": cross_weight, "cross_bias": cross_bias}


@jax.custom_vjp
def low(v):
    return lax.optimization_barrier(v.astype(jnp.bfloat16)).astype(jnp.float32)

@jax.custom_vjp
def low_back(v):
    return v

def low_keep(v):
    return (low(v), None)

def low_pass(kept, grad):
    return (grad,)

def back_keep(v):
    return (v, None)

def back_low(kept, grad):
    return (low(grad),)
low.defvjp(low_keep, low_pass)
low_back.defvjp(back_keep, back_low)
EPSILON = 1e-05
MASKED = -1e+30
PRECISE = lax.Precision.HIGHEST

def geometry(tile_sizes, row_count):
    slot_count = tile_sizes.shape[0]
    counts = (tile_sizes * tile_sizes).astype(jnp.int32)
    endings = jnp.cumsum(counts).astype(jnp.int32)
    starting = (endings - counts).astype(jnp.int32)
    position = jnp.arange(row_count, dtype=jnp.int32)
    member = lax.optimization_barrier(jnp.sum((position[:, None] >= endings[None, :]).astype(jnp.int32), axis=1)).astype(jnp.int32)
    start_table = jnp.concatenate([starting, endings[slot_count - 1:]]).astype(jnp.int32)
    side_table = jnp.concatenate([jnp.maximum(tile_sizes, 1), jnp.ones((1,), jnp.int32)]).astype(jnp.int32)
    picked = member[:, None] == jnp.arange(slot_count + 1, dtype=jnp.int32)[None, :]
    first_place = lax.optimization_barrier(jnp.sum(jnp.where(picked, start_table[None, :], 0), axis=1)).astype(jnp.int32)
    tile_side = lax.optimization_barrier(jnp.sum(jnp.where(picked, side_table[None, :], 0), axis=1)).astype(jnp.int32)
    offset = position - first_place
    row_place = (offset // tile_side).astype(jnp.float32)
    col_place = (offset % tile_side).astype(jnp.float32)
    validity = (member < slot_count).astype(jnp.float32)
    return (member, row_place, col_place, validity)

def alibi_bias(member, row_place, col_place, slopes):
    row_gap = row_place[:, None] - row_place[None, :]
    col_gap = col_place[:, None] - col_place[None, :]
    distance = jnp.sqrt(row_gap * row_gap + col_gap * col_gap)
    same_tile = member[:, None] == member[None, :]
    return jnp.where(same_tile[None, :, :], -slopes[:, None, None] * distance[None, :, :], MASKED)

def normalize(values, gain_vector, bias_vector):
    centered = values - lax.optimization_barrier(jnp.mean(values, axis=-1, keepdims=True))
    inverse = lax.rsqrt(lax.optimization_barrier(jnp.mean(centered * centered, axis=-1, keepdims=True)) + EPSILON)
    return centered * inverse * gain_vector + bias_vector

def attention(queries, keys_in, values_in, score_bias):
    scores = jnp.einsum('qhd,khd->hqk', queries, keys_in, precision=PRECISE) * HS ** (-0.5) + score_bias
    weights = low(jax.nn.softmax(low_back(scores), axis=-1))
    return jnp.einsum('hqk,khd->qhd', weights, values_in, precision=PRECISE)

def self_block(hidden_x, layer_weights, layer_index, score_bias):
    row_count = hidden_x.shape[0]
    normal = low(normalize(hidden_x, layer_weights['norm1_gain'][layer_index], layer_weights['norm1_bias'][layer_index]))
    projected = low_back(low(jnp.einsum('rd,dce->rce', normal, layer_weights['qkv_weight'][layer_index], precision=PRECISE)))
    head_parts = projected.reshape(row_count, 3, H, HS)
    merged = attention(head_parts[:, 0], head_parts[:, 1], head_parts[:, 2], score_bias).reshape(row_count, D)
    merged = low_back(low(merged))
    branch = jnp.dot(merged, layer_weights['attn_weight'][layer_index], precision=PRECISE) + layer_weights['attn_bias'][layer_index]
    return hidden_x + low_back(branch)

def cross_block(hidden_x, context, cross_weights, score_bias):
    row_count = hidden_x.shape[0]
    normal = low(normalize(hidden_x, cross_weights['query_gain'], cross_weights['query_bias']))
    queries = low_back(low(jnp.dot(normal, cross_weights['cross_query'], precision=PRECISE)))
    pair_values = low_back(low(jnp.einsum('rd,dce->rce', context, cross_weights['cross_keyval'], precision=PRECISE)))
    pair_heads = pair_values.reshape(row_count, 2, H, HS)
    merged = attention(queries.reshape(row_count, H, HS), pair_heads[:, 0], pair_heads[:, 1], score_bias).reshape(row_count, D)
    merged = low_back(low(merged))
    branch = jnp.dot(merged, cross_weights['cross_weight'], precision=PRECISE) + cross_weights['cross_bias']
    return hidden_x + low_back(branch)

def feed_block(hidden_x, layer_weights, layer_index):
    normal = low(normalize(hidden_x, layer_weights['norm2_gain'][layer_index], layer_weights['norm2_bias'][layer_index]))
    hidden = low_back(jnp.dot(normal, layer_weights['up_weight'][layer_index], precision=PRECISE) + layer_weights['up_bias'][layer_index])
    unit_values = low(jax.nn.gelu(hidden, approximate=False))
    branch = jnp.dot(unit_values, layer_weights['down_weight'][layer_index], precision=PRECISE) + layer_weights['down_bias'][layer_index]
    return hidden_x + low_back(branch)

def forward_buffer(layer_weights, cross_weights, radar, optical, score_bias, validity):
    row_mask = validity[:, None]
    context = low(optical * row_mask)
    radar_out = feed_block(self_block(radar * row_mask, layer_weights, 0, score_bias), layer_weights, 0)
    joining_in = low_back(low(radar_out))
    middle = self_block(joining_in, layer_weights, 1, score_bias)
    middle = cross_block(middle, context, cross_weights, score_bias)
    return feed_block(middle, layer_weights, 1) * row_mask

def reference(radar_tokens, optical_tokens, out_cotangent, tile_sides, norm1_gain, norm1_bias, qkv_weight, attn_weight, attn_bias, norm2_gain, norm2_bias, up_weight, up_bias, down_weight, down_bias, query_gain, query_bias, cross_query, cross_keyval, cross_weight, cross_bias):
    layer_weights = dict(norm1_gain=norm1_gain.astype(jnp.float32), norm1_bias=norm1_bias.astype(jnp.float32), qkv_weight=qkv_weight.astype(jnp.float32), attn_weight=attn_weight.astype(jnp.float32), attn_bias=attn_bias.astype(jnp.float32), norm2_gain=norm2_gain.astype(jnp.float32), norm2_bias=norm2_bias.astype(jnp.float32), up_weight=up_weight.astype(jnp.float32), up_bias=up_bias.astype(jnp.float32), down_weight=down_weight.astype(jnp.float32), down_bias=down_bias.astype(jnp.float32))
    cross_weights = dict(query_gain=query_gain.astype(jnp.float32), query_bias=query_bias.astype(jnp.float32), cross_query=cross_query.astype(jnp.float32), cross_keyval=cross_keyval.astype(jnp.float32), cross_weight=cross_weight.astype(jnp.float32), cross_bias=cross_bias.astype(jnp.float32))
    buffers = MICRO * N_DP
    radar = radar_tokens.reshape(buffers, ROWS, D)
    optical = optical_tokens.reshape(buffers, ROWS, D)
    cotangent = out_cotangent.reshape(buffers, ROWS, D)
    tile_sizes = tile_sides.reshape(buffers, SLOTS)
    slopes = jnp.exp2(-8.0 * (jnp.arange(H) + 1).astype(jnp.float32) / H)

    def visit_buffer(totals, buffer_items):
        radar_one, optical_one, cotangent_one, sizes_one = buffer_items
        member, row_place, col_place, validity = geometry(sizes_one, ROWS)
        score_bias = alibi_bias(member, row_place, col_place, slopes)

        def run_layers(layer_in, cross_in, radar_in, optical_in):
            return forward_buffer(layer_in, cross_in, radar_in, optical_in, score_bias, validity)
        outputs, pullback = jax.vjp(run_layers, layer_weights, cross_weights, radar_one.astype(jnp.float32), optical_one.astype(jnp.float32))
        grad_layer, grad_cross, grad_radar, grad_optical = pullback(cotangent_one.astype(jnp.float32))
        totals = jax.tree.map(jnp.add, totals, (grad_layer, grad_cross))
        return (totals, (outputs, grad_radar, grad_optical))
    zero_sums = jax.tree.map(jnp.zeros_like, (layer_weights, cross_weights))
    totals, (joined, radar_grad, optical_grad) = lax.scan(visit_buffer, zero_sums, (radar, optical, cotangent, tile_sizes))
    grad_layer, grad_cross = totals
    shape_out = (MICRO, N_DP * ROWS, D)
    return (joined.reshape(shape_out), radar_grad.reshape(shape_out), optical_grad.reshape(shape_out), grad_layer['norm1_gain'], grad_layer['norm1_bias'], grad_layer['qkv_weight'], grad_layer['attn_weight'], grad_layer['attn_bias'], grad_layer['norm2_gain'], grad_layer['norm2_bias'], grad_layer['up_weight'], grad_layer['up_bias'], grad_layer['down_weight'], grad_layer['down_bias'], grad_cross['query_gain'], grad_cross['query_bias'], grad_cross['cross_query'], grad_cross['cross_keyval'], grad_cross['cross_weight'], grad_cross['cross_bias'])
```

```python
import jax
import jax.numpy as jnp
from jax import lax
from jax.experimental import pallas as pl
from jax.experimental.pallas import tpu as pltpu
from jax.sharding import PartitionSpec as P

H = 12
HS = 64
D = 768
FF = 3072
R = 512
HALF = D // 2
EPSILON = 1e-05
BF = jnp.bfloat16
F32 = jnp.float32
ANY = pl.BlockSpec(memory_space=pl.ANY)
VM = pl.BlockSpec(memory_space=pltpu.VMEM)
SM = pl.BlockSpec(memory_space=pltpu.SMEM)
MESH = pl.DeviceIdType.MESH
BIG = 60 * 1024 * 1024


def shape(dims, kind):
    return jax.ShapeDtypeStruct(dims, kind)


def geometry(tile_sizes, row_count):
    slot_count = tile_sizes.shape[0]
    counts = tile_sizes * tile_sizes
    endings = jnp.cumsum(counts)
    starting = endings - counts
    position = jnp.arange(row_count, dtype=jnp.int32)
    member = jnp.sum((position[:, None] >= endings[None, :]).astype(jnp.int32), axis=1)
    start_table = jnp.concatenate([starting, endings[slot_count - 1 :]])
    side_table = jnp.concatenate([jnp.maximum(tile_sizes, 1), jnp.ones((1,), jnp.int32)])
    picked = member[:, None] == jnp.arange(slot_count + 1, dtype=jnp.int32)[None, :]
    first_place = jnp.sum(jnp.where(picked, start_table[None, :], 0), axis=1)
    tile_side = jnp.sum(jnp.where(picked, side_table[None, :], 0), axis=1)
    offset = position - first_place
    row_place = (offset // tile_side).astype(F32)
    col_place = (offset % tile_side).astype(F32)
    validity = (member < slot_count).astype(F32)
    return jnp.stack([member.astype(F32), row_place, col_place, validity])


class Links:
    def __init__(self, send_sems, recv_sems):
        self.send_sems, self.recv_sems = send_sems, recv_sems
        self.used = 0
        self.started = []

    def send(self, source, target, device):
        copy = pltpu.make_async_remote_copy(
            src_ref=source,
            dst_ref=target,
            send_sem=self.send_sems.at[self.used],
            recv_sem=self.recv_sems.at[self.used],
            device_id=device,
            device_id_type=MESH,
        )
        self.used += 1
        copy.start()
        self.started.append(copy)
        return copy

    def drain(self):
        for copy in self.started:
            copy.wait_send()
        self.started = []


class Place:
    def __init__(self):
        dp = lax.axis_index("dp")
        self.pipe = lax.axis_index("pipe")
        self.mp = lax.axis_index("mp")
        self.core = lax.rem(dp, 2)
        chip = dp // 2
        self.x = lax.rem(chip, 4)
        self.z = chip // 4

    def at(self, z, x, core):
        return {"dp": (z * 4 + x) * 2 + core}

    def step_x(self, by):
        return self.at(self.z, lax.rem(self.x + by, 4), self.core)

    def step_z(self, by):
        return self.at(lax.rem(self.z + by, 4), self.x, self.core)

    def sibling(self):
        return self.at(self.z, self.x, 1 - self.core)

    def partner(self):
        return {"mp": 1 - self.mp}

    def greet(self, devices):
        barrier = pltpu.get_barrier_semaphore()
        for device in devices:
            pl.semaphore_signal(barrier, inc=1, device_id=device, device_id_type=MESH)
        pl.semaphore_wait(barrier, len(devices))


def gather_kernel(piece, out, send_sems, recv_sems):
    here = Place()
    c, x, z = here.core, here.x, here.z
    right, left = here.step_x(1), here.step_x(3)
    up, down = here.step_z(1), here.step_z(3)
    xl, xr = lax.rem(x + 3, 4), lax.rem(x + 1, 4)
    zd, zu = lax.rem(z + 3, 4), lax.rem(z + 1, 4)
    here.greet([right, left, up, down, here.sibling(), here.partner()])
    links = Links(send_sems, recv_sems)
    a, b = pl.ds(0, 48), pl.ds(48, 48)
    a0, a1 = pl.ds(0, 32), pl.ds(32, 16)
    b0, b1 = pl.ds(48, 32), pl.ds(80, 16)

    def stages(g):
        waiting = []

        def wait():
            for copy in waiting:
                copy.wait_recv()
            waiting.clear()

        def go(view, device):
            waiting.append(links.send(view, view, device))

        def stage0():
            waiting.append(links.send(piece.at[g], out.at[g, z, x, c], here.partner()))

        def stage1():
            wait()
            go(out.at[g, z, x, c, a], right)
            go(out.at[g, z, x, c, a], left)
            go(out.at[g, z, x, c, b], up)
            go(out.at[g, z, x, c, b], down)

        def stage2():
            wait()
            go(out.at[g, z, xl, c, a0], right)
            go(out.at[g, z, xr, c, a1], left)
            go(out.at[g, zd, x, c, b0], up)
            go(out.at[g, zu, x, c, b1], down)

        def stage3():
            wait()
            go(out.at[g, z, :, c, a], up)
            go(out.at[g, z, :, c, a], down)
            go(out.at[g, :, x, c, b], right)
            go(out.at[g, :, x, c, b], left)

        def stage4():
            wait()
            go(out.at[g, zd, pl.ds(0, 2), c, a], up)
            go(out.at[g, zu, pl.ds(2, 2), c, a], down)
            go(out.at[g, pl.ds(0, 2), xl, c, b], right)
            go(out.at[g, pl.ds(2, 2), xr, c, b], left)

        def stage5():
            wait()
            go(out.at[g, :, :, c], here.sibling())

        return [stage0, stage1, stage2, stage3, stage4, stage5, wait]

    def run(groups):
        plans = [stages(g) for g in groups]
        for t in range(len(groups) + 6):
            for i, plan in enumerate(plans):
                if 0 <= t - i < 7:
                    plan[t - i]()

    run([0, 1, 2])
    links.drain()

    @pl.when(here.pipe == 1)
    def _():
        run([3])
        links.drain()


def gather_weights(piece):
    return pl.pallas_call(
        gather_kernel,
        out_shape=shape((4, 4, 4, 2, 96, 384), BF),
        in_specs=[ANY],
        out_specs=ANY,
        scratch_shapes=[pltpu.SemaphoreType.DMA((72,)), pltpu.SemaphoreType.DMA((72,))],
        compiler_params=pltpu.CompilerParams(collective_id=0, has_side_effects=True),
    )(piece)


def scatter_kernel(gff, gat, vec, off, oat, ovec, *scratch):
    here = Place()
    names = list(scratch)
    sems, names = names[:3], names[3:]
    here.greet(
        [
            here.step_x(1),
            here.step_x(3),
            here.step_z(1),
            here.step_z(3),
            here.sibling(),
            here.partner(),
            here.step_x(2),
            here.step_z(2),
        ]
    )
    links = Links(sems[0], sems[1])
    vbuf = names[0]
    vec_steps = vector_stages(here, links, vec, vbuf, ovec)
    first = scatter_stages(here, links, sems[2], 0, gff, off, names[1:11])
    second = scatter_stages(here, links, sems[2], 1, gat, oat, names[11:21])
    for t in range(len(first) + 1):
        if t < len(first):
            first[t]()
        if 1 <= t < len(second) + 1:
            second[t - 1]()
        if t < len(vec_steps):
            vec_steps[t]()
    links.drain()


def cross_scatter_kernel(gcr, ocr, *scratch):
    here = Place()
    names = list(scratch)
    sems, names = names[:3], names[3:]
    here.greet(
        [
            here.step_x(1),
            here.step_x(3),
            here.step_z(1),
            here.step_z(3),
            here.sibling(),
            here.partner(),
        ]
    )
    links = Links(sems[0], sems[1])
    for stage in scatter_stages(here, links, sems[2], 0, gcr, ocr, names):
        stage()
    links.drain()


def vector_stages(here, links, vec, vbuf, ovec):
    x, z = here.x, here.z
    flip_x1 = here.at(z, x + 1 - 2 * lax.rem(x, 2), here.core)
    flip_z1 = here.at(z + 1 - 2 * lax.rem(z, 2), x, here.core)
    order = [here.sibling(), flip_x1, here.step_x(2), flip_z1, here.step_z(2), here.partner()]
    waiting = []

    def begin(i):
        def stage():
            if i == 0:
                ovec[...] = vec[...]
            else:
                copy = waiting.pop()
                copy.wait()
                links.started = [other for other in links.started if other is not copy]
                ovec[...] = ovec[...] + vbuf[i - 1]
            if i < len(order):
                waiting.append(links.send(ovec, vbuf.at[i], order[i]))

        return stage

    return [begin(i) for i in range(len(order) + 1)]


def scatter_scratch(cols):
    half, quarter = cols // 2, cols // 4
    return [
        pltpu.VMEM((4, 4, 48, cols), BF),
        pltpu.VMEM((4, 4, 48, cols), BF),
        pltpu.VMEM((2, 2, 2, 48, half), BF),
        pltpu.VMEM((2, 2, 4, 48, half), BF),
        pltpu.VMEM((2, 4, 48, half), BF),
        pltpu.VMEM((2, 2, 48, quarter), BF),
        pltpu.VMEM((2, 2, 48, half), BF),
        pltpu.VMEM((2, 48, half), BF),
        pltpu.VMEM((48, half), BF),
        pltpu.VMEM((2, 24, half), F32),
    ]


def scatter_stages(here, links, local_sems, at, grads, out, buffers):
    own, other, far, near, mid, far2, near2, late, mated, last = buffers
    cols = own.shape[-1]
    half, quarter = cols // 2, cols // 4
    c, x, z, m = here.core, here.x, here.z, here.mp
    xs = [x, lax.rem(x + 1, 4), lax.rem(x + 2, 4), lax.rem(x + 3, 4)]
    zs = [z, lax.rem(z + 1, 4), lax.rem(z + 2, 4), lax.rem(z + 3, 4)]
    lanes = [pl.ds(0, half), pl.ds(half, half)]
    low, high = pl.ds(0, 2), pl.ds(2, 2)
    ahead = [here.step_x(1), here.step_z(1)]
    behind = [here.step_x(3), here.step_z(3)]
    order = [2, 1, 3, 0]
    exchanged = {}
    kept = {}

    def block(ref, way, j):
        if way == 0:
            return ref.at[:, xs[j], :, lanes[0]]
        return ref.at[zs[j], :, :, lanes[1]]

    def part(ref, way, j, span):
        if way == 0:
            return ref.at[span, xs[j], :, lanes[0]]
        return ref.at[zs[j], span, :, lanes[1]]

    def start():
        kept["local"] = pltpu.make_async_copy(grads.at[c], own, local_sems.at[at])
        kept["local"].start()
        for j in order:
            for way in range(2):
                exchanged[way, j] = links.send(
                    block(grads.at[1 - c], way, j), block(other, way, j), here.sibling()
                )

    def add_other(way, j):
        exchanged[way, j].wait_recv()
        mine, theirs = block(own, way, j), block(other, way, j)
        for i in range(4):
            mine[i] = mine[i] + theirs[i]

    def ring_one():
        kept["local"].wait()
        for way in range(2):
            add_other(way, 2)
            kept["a", way] = links.send(part(own, way, 2, low), far.at[way, 0], ahead[way])
            kept["b", way] = links.send(part(own, way, 2, high), far.at[way, 1], behind[way])
        for way in range(2):
            add_other(way, 1)
            kept["c", way] = links.send(
                part(own, way, 1, high), near.at[way, 0, high], ahead[way]
            )
            add_other(way, 3)
            kept["d", way] = links.send(part(own, way, 3, low), near.at[way, 1, low], behind[way])
        for way in range(2):
            add_other(way, 0)

    def ring_two():
        for way in range(2):
            kept["a", way].wait_recv()
            target = part(own, way, 1, low)
            for i in range(2):
                target[i] = target[i] + far[way, 0, i]
            kept["e", way] = links.send(target, near.at[way, 0, low], ahead[way])
            kept["b", way].wait_recv()
            target = part(own, way, 3, high)
            for i in range(2):
                target[i] = target[i] + far[way, 1, i]
            kept["f", way] = links.send(target, near.at[way, 1, high], behind[way])

    def ring_three():
        for way in range(2):
            turn = 1 - way
            places = zs if way == 0 else xs
            for key in "cdef":
                kept[key, way].wait_recv()
            mine = block(own, way, 0)
            for i in range(4):
                mid[way, i] = (
                    mine[i].astype(F32) + near[way, 0, i].astype(F32) + near[way, 1, i].astype(F32)
                ).astype(BF)
            fore, aft = pl.ds(0, quarter), pl.ds(quarter, quarter)
            kept["g", way] = links.send(
                mid.at[way, places[2], :, fore], far2.at[way, 0], ahead[turn]
            )
            kept["h", way] = links.send(
                mid.at[way, places[2], :, aft], far2.at[way, 1], behind[turn]
            )
            kept["i", way] = links.send(
                mid.at[way, places[1], :, aft], near2.at[way, 0, :, aft], ahead[turn]
            )
            kept["j", way] = links.send(
                mid.at[way, places[3], :, fore], near2.at[way, 1, :, fore], behind[turn]
            )

    def ring_four():
        for way in range(2):
            turn = 1 - way
            places = zs if way == 0 else xs
            fore, aft = pl.ds(0, quarter), pl.ds(quarter, quarter)
            kept["g", way].wait_recv()
            target = mid.at[way, places[1], :, fore]
            target[...] = target[...] + far2[way, 0]
            kept["k", way] = links.send(target, near2.at[way, 0, :, fore], ahead[turn])
            kept["h", way].wait_recv()
            target = mid.at[way, places[3], :, aft]
            target[...] = target[...] + far2[way, 1]
            kept["l", way] = links.send(target, near2.at[way, 1, :, aft], behind[turn])

    def to_partner():
        for way in range(2):
            places = zs if way == 0 else xs
            for key in "ijkl":
                kept[key, way].wait_recv()
            late[way] = (
                mid[way, places[0]].astype(F32)
                + near2[way, 0].astype(F32)
                + near2[way, 1].astype(F32)
            ).astype(BF)
        kept["m"] = links.send(late.at[1 - m], mated, here.partner())

    def to_sibling():
        kept["m"].wait_recv()
        total = late[m].astype(F32) + mated[...].astype(F32)
        last[0] = jnp.where(c == 0, total[24:], total[:24])
        out[c] = jnp.where(c == 0, total[:24], total[24:])
        kept["n"] = links.send(last.at[0], last.at[1], here.sibling())

    def finish():
        kept["n"].wait_recv()
        out[1 - c] = last[1]

    return [start, ring_one, ring_two, ring_three, ring_four, to_partner, to_sibling, finish]


def scatter_grads(gff, gat, vec):
    return pl.pallas_call(
        scatter_kernel,
        out_shape=(shape((2, 24, 1536), F32), shape((2, 24, 768), F32), shape((16, D), F32)),
        in_specs=[ANY, ANY, VM],
        out_specs=(VM, VM, VM),
        scratch_shapes=[
            pltpu.SemaphoreType.DMA((80,)),
            pltpu.SemaphoreType.DMA((80,)),
            pltpu.SemaphoreType.DMA((2,)),
            pltpu.VMEM((6, 16, D), F32),
        ]
        + scatter_scratch(3072)
        + scatter_scratch(1536),
        compiler_params=pltpu.CompilerParams(
            collective_id=1, has_side_effects=True, vmem_limit_bytes=BIG
        ),
    )(gff.reshape(2, 4, 4, 48, 3072), gat.reshape(2, 4, 4, 48, 1536), vec)


def scatter_cross(gcr):
    return pl.pallas_call(
        cross_scatter_kernel,
        out_shape=shape((2, 24, 768), F32),
        in_specs=[ANY],
        out_specs=VM,
        scratch_shapes=[
            pltpu.SemaphoreType.DMA((40,)),
            pltpu.SemaphoreType.DMA((40,)),
            pltpu.SemaphoreType.DMA((2,)),
        ]
        + scatter_scratch(1536),
        compiler_params=pltpu.CompilerParams(
            collective_id=2, has_side_effects=True, vmem_limit_bytes=BIG
        ),
    )(gcr)


def mm(a, b):
    return lax.dot_general(a, b, (((1,), (0,)), ((), ())), preferred_element_type=F32)


def mmt(a, b):
    return lax.dot_general(a, b, (((1,), (1,)), ((), ())), preferred_element_type=F32)


def tmm(a, b):
    return lax.dot_general(a, b, (((0,), (0,)), ((), ())), preferred_element_type=F32)


def normalize(values):
    centered = values - jnp.mean(values, axis=-1, keepdims=True)
    inverse = lax.rsqrt(jnp.mean(centered * centered, axis=-1, keepdims=True) + EPSILON)
    return centered * inverse, inverse


def norm_grad(upstream, normed, inverse, gain):
    scaled = upstream * gain
    return inverse * (
        scaled
        - jnp.mean(scaled, axis=-1, keepdims=True)
        - normed * jnp.mean(scaled * normed, axis=-1, keepdims=True)
    )


def distances(geo_rows, geo_cols, dist):
    rows = geo_cols[...]
    gap_r = rows[:, 1:2] - geo_rows[1:2, :]
    gap_c = rows[:, 2:3] - geo_rows[2:3, :]
    apart = jnp.sqrt(gap_r * gap_r + gap_c * gap_c)
    dist[...] = jnp.where(rows[:, 0:1] == geo_rows[0:1, :], apart, 1e30)


def head_lanes():
    lane = lax.broadcasted_iota(jnp.int32, (1, 128), 1)
    first = (lane < HS).astype(F32)
    return first.astype(BF), (1.0 - first).astype(BF), first > 0.5


def attend(q_at, k_at, v_at, o_at, lse, dist, slopes):
    m0, m1, in_first = head_lanes()
    lane = lax.broadcasted_iota(jnp.int32, (1, 128), 1)
    lse_lanes = lse["lanes"]
    lse_lanes[...] = jnp.zeros_like(lse_lanes)

    def pair(i, carry):
        q, k, v = q_at(i)[...], k_at(i)[...], v_at(i)[...]
        q = q * jnp.asarray(0.125, BF)
        halves = []
        for j, keep in enumerate((m0, m1)):
            s = mmt(q * keep, k) - slopes[2 * i + j] * dist[...]
            top = jnp.max(s, axis=-1, keepdims=True)
            raised = jnp.exp(s - top)
            total = jnp.sum(raised, axis=-1, keepdims=True)
            w = (raised * (1.0 / total)).astype(BF)
            halves.append(mm(w, v))
            lse_lanes[...] = jnp.where(lane == 2 * i + j, top + jnp.log(total), lse_lanes[...])
        o_at(i)[...] = jnp.where(in_first, halves[0], halves[1]).astype(BF)
        return carry

    lax.fori_loop(0, H // 2, pair, 0)
    lse["rows"][...] = lse_lanes[...].T[:16]


def attend_grad(q_at, k_at, v_at, do_at, lse_rows, dist, slopes):
    m0, m1, in_first = head_lanes()

    def pair(i, carry):
        q, k, v, do = q_at(i)[...], k_at(i)[...], v_at(i)[...], do_at(i)[...]
        q = q * jnp.asarray(0.125, BF)
        dqs, dks, dvs = [], [], []
        for j, keep in enumerate((m0, m1)):
            h = 2 * i + j
            s = mmt(k, q * keep) - slopes[h] * dist[...]
            p = jnp.exp(s - lse_rows[pl.ds(h, 1), :])
            dvs.append(mm(p.astype(BF), do))
            t = p * mmt(v, do * keep)
            ds = (t - p * jnp.sum(t, axis=0, keepdims=True)).astype(BF)
            dks.append(mm(ds, q))
            dqs.append(tmm(ds, k))
        q_at(i)[...] = (jnp.where(in_first, dqs[0], dqs[1]) * 0.125).astype(BF)
        k_at(i)[...] = jnp.where(in_first, dks[0], dks[1]).astype(BF)
        v_at(i)[...] = jnp.where(in_first, dvs[0], dvs[1]).astype(BF)
        return carry

    lax.fori_loop(0, H // 2, pair, 0)


def lanes_of(ref, first):
    return lambda i: ref.at[:, pl.ds(pl.multiple_of(first + i * 128, 128), 128)]


class Loads:
    def __init__(self, sems):
        self.sems = sems
        self.used = 0

    def start(self, pairs):
        copies = []
        for source, target in pairs:
            copies.append(pltpu.make_async_copy(source, target, self.sems.at[self.used]))
            self.used += 1
        for copy in copies:
            copy.start()
        return copies


def wait_all(copies):
    for copy in copies:
        copy.wait()


def at_lanes(ref, first, size):
    return ref.at[:, pl.ds(pl.multiple_of(first, 128), size)]


def weight_pairs(own, gathered, kept):
    m = lax.axis_index("mp")
    o = 1 - m
    qkv, attn, up, down = own
    wqkv, wo, wup, wdn = kept
    g = gathered
    pairs_qkv = []
    for j in range(3):
        pairs_qkv.append((qkv.at[j], at_lanes(wqkv, j * D + m * HALF, HALF)))
        pairs_qkv.append((g.at[0, pl.ds(j * D, D)], at_lanes(wqkv, j * D + o * HALF, HALF)))
    pairs_o = [(attn, wo.at[pl.ds(m * HALF, HALF)])]
    pairs_up = [(up, at_lanes(wup, m * 1536, 1536))]
    pairs_dn = [(down, wdn.at[pl.ds(m * 1536, 1536)])]
    for b in range(2):
        lanes = pl.ds(b * HALF, HALF)
        pairs_o.append(
            (g.at[0, pl.ds(2304 + b * HALF, HALF)], wo.at[pl.ds(o * HALF, HALF), lanes])
        )
        pairs_dn.append((g.at[2, pl.ds(b * 1536, 1536)], wdn.at[pl.ds(o * 1536, 1536), lanes]))
    for b in range(4):
        pairs_up.append((g.at[1, pl.ds(b * D, D)], at_lanes(wup, o * 1536 + b * HALF, HALF)))
    return pairs_qkv, pairs_o, pairs_up, pairs_dn


def cross_pairs(own, gathered, kept):
    m = lax.axis_index("mp")
    o = 1 - m
    cq, kv, cw = own
    wcq, wkv, wcw = kept
    g = gathered
    pairs = [
        (cq, at_lanes(wcq, m * HALF, HALF)),
        (g.at[3, pl.ds(0, D)], at_lanes(wcq, o * HALF, HALF)),
        (cw, wcw.at[pl.ds(m * HALF, HALF)]),
    ]
    for j in range(2):
        pairs.append((kv.at[j], at_lanes(wkv, j * D + m * HALF, HALF)))
        pairs.append((g.at[3, pl.ds((j + 1) * D, D)], at_lanes(wkv, j * D + o * HALF, HALF)))
        pairs.append(
            (
                g.at[3, pl.ds(2304 + j * HALF, HALF)],
                wcw.at[pl.ds(o * HALF, HALF), pl.ds(j * HALF, HALF)],
            )
        )
    return pairs


LAYER_WEIGHTS = [((D, 3 * D), BF), ((D, D), BF), ((D, FF), BF), ((FF, D), BF)]
CROSS_WEIGHTS = [((D, D), BF), ((D, 2 * D), BF), ((D, D), BF)]
SAVED = [((R, 3 * D), BF), ((R, D), BF), ((16, R), F32), ((R, D), F32), ((R, FF), BF), ((R, FF), BF)]


def row(ref, i):
    return ref[i : i + 1, :]


def self_forward(x, vecs, weights, waits, saved, work, dist, slopes):
    wqkv, wo = weights[:2]
    qkv, o, lse_rows, x1 = saved[:4]
    normed, _ = normalize(x)
    work["a"][...] = (normed * row(vecs, 0) + row(vecs, 1)).astype(BF)
    wait_all(waits[0])
    for j in range(3):
        lanes = pl.ds(j * D, D)
        qkv[:, lanes] = mm(work["a"][...], wqkv[:, lanes]).astype(BF)
    attend(
        lanes_of(qkv, 0),
        lanes_of(qkv, D),
        lanes_of(qkv, 2 * D),
        lanes_of(o, 0),
        {"lanes": work["lanes"], "rows": lse_rows},
        dist,
        slopes,
    )
    wait_all(waits[1])
    x1[...] = x + mm(o[...], wo[...]) + row(vecs, 2)


def feed_forward(x2, vecs, weights, waits, g, gp, work):
    wup, wdn = weights[2:]
    normed, _ = normalize(x2[...])
    work["a"][...] = (normed * row(vecs, 3) + row(vecs, 4)).astype(BF)
    wait_all(waits[2])
    for j in range(4):
        lanes = pl.ds(j * D, D)
        u = mm(work["a"][...], wup[:, lanes]) + row(vecs, 6 + j)
        phi = 0.5 * (1.0 + lax.erf(u * 0.7071067811865476))
        g[:, lanes] = (u * phi).astype(BF)
        gp[:, lanes] = (phi + u * jnp.exp(-0.5 * u * u) * 0.3989422804014327).astype(BF)
        if j == 0:
            wait_all(waits[3])
        term = mm(g[:, lanes], wdn[lanes, :])
        work["acc"][...] = term if j == 0 else work["acc"][...] + term


class Staged:
    def __init__(self, buffers, sems):
        self.buffers, self.sems = buffers, sems
        self.count = buffers.shape[0]
        self.turn = 0
        self.flying = {}

    def put(self, value, targets):
        slot = self.turn % self.count
        self.turn += 1
        wait_all(self.flying.pop(slot, []))
        self.buffers[slot] = value
        copies = []
        for i, (first, size, target) in enumerate(targets):
            copy = pltpu.make_async_copy(
                self.buffers.at[slot, :, pl.ds(first, size)], target, self.sems.at[slot, i]
            )
            copy.start()
            copies.append(copy)
        self.flying[slot] = copies

    def drain(self):
        for copies in self.flying.values():
            wait_all(copies)
        self.flying = {}


def feed_backward(dy, x2, vecs, weights, waits, g, gp, gff, staged, vec_out, work):
    wup, wdn = weights[2:]
    e3 = dy.astype(BF)
    work["e"][...] = e3
    vec_out[5:6, :] = jnp.sum(e3.astype(F32), axis=0, keepdims=True)
    work["et"][...] = e3.T
    normed, inverse = normalize(x2[...])
    work["at"][...] = (normed * row(vecs, 3) + row(vecs, 4)).astype(BF).T
    wait_all(waits[2])
    wait_all(waits[3])
    for j in range(4):
        lanes = pl.ds(j * D, D)
        du = (mmt(work["e"][...], wdn[lanes, :]) * gp[:, lanes].astype(F32)).astype(BF)
        work["a"][...] = du
        vec_out[6 + j : 7 + j, :] = jnp.sum(du.astype(F32), axis=0, keepdims=True)
        staged.put(mm(work["et"][...], g[:, lanes]).astype(BF), [(0, D, gff.at[1, :, lanes])])
        staged.put(mm(work["at"][...], work["a"][...]).astype(BF), [(0, D, gff.at[0, :, lanes])])
        term = mmt(work["a"][...], wup[:, lanes])
        work["acc"][...] = term if j == 0 else work["acc"][...] + term
    dm = work["acc"][...]
    vec_out[3:4, :] = jnp.sum(dm * normed, axis=0, keepdims=True)
    vec_out[4:5, :] = jnp.sum(dm, axis=0, keepdims=True)
    work["acc"][...] = dy + norm_grad(dm, normed, inverse, row(vecs, 3))


def halves(target, which, first):
    return [
        (part * HALF, HALF, target.at[which, :, pl.ds(part * D + first, HALF)]) for part in range(2)
    ]


def self_backward(x, vecs, weights, waits, saved, gat, staged, vec_out, work, dist, slopes):
    wqkv, wo = weights[:2]
    qkv, o, lse_rows = saved[:3]
    e1 = work["acc"][...].astype(BF)
    work["e"][...] = e1
    vec_out[2:3, :] = jnp.sum(e1.astype(F32), axis=0, keepdims=True)
    work["et"][...] = e1.T
    staged.put(mm(work["et"][...], o[...]).astype(BF), halves(gat, 1, HALF))
    wait_all(waits[1])
    work["a"][...] = mmt(work["e"][...], wo[...]).astype(BF)
    attend_grad(
        lanes_of(qkv, 0),
        lanes_of(qkv, D),
        lanes_of(qkv, 2 * D),
        lanes_of(work["a"], 0),
        lse_rows,
        dist,
        slopes,
    )
    normed, inverse = normalize(x)
    work["at"][...] = (normed * row(vecs, 0) + row(vecs, 1)).astype(BF).T
    wait_all(waits[0])
    da = None
    for j, target in enumerate([(0, 0), (0, HALF), (1, 0)]):
        lanes = pl.ds(j * D, D)
        staged.put(mm(work["at"][...], qkv[:, lanes]).astype(BF), halves(gat, *target))
        term = mmt(qkv[:, lanes], wqkv[:, lanes])
        da = term if j == 0 else da + term
    vec_out[0:1, :] = jnp.sum(da * normed, axis=0, keepdims=True)
    vec_out[1:2, :] = jnp.sum(da, axis=0, keepdims=True)
    work["acc"][...] = work["acc"][...] + norm_grad(da, normed, inverse, row(vecs, 0))


WORK = [
    ((R, D), BF),
    ((128, R), F32),
    ((R, 128), F32),
    ((R, D), F32),
    ((R, D), BF),
    ((D, R), BF),
    ((D, R), BF),
    ((R, R), F32),
]


def work_of(refs):
    return dict(a=refs[0], lanes=refs[2], acc=refs[3], e=refs[4], et=refs[5], at=refs[6])


def vmem(shapes):
    return [pltpu.VMEM(dims, kind) for dims, kind in shapes]


def first_forward_kernel(x_in, geo_r, geo_c, vecs, slopes, qkv, attn, up, down, gathered, *refs):
    y_out, saved, refs = refs[0], refs[1:7], refs[7:]
    weights, work_refs, sems = refs[:4], refs[4:12], refs[12]
    work, dist = work_of(work_refs), work_refs[7]
    loads = Loads(sems)
    waits = [loads.start(p) for p in weight_pairs((qkv, attn, up, down), gathered, weights)]
    distances(geo_r, geo_c, dist)
    x = x_in[...].astype(F32) * geo_c[:, 3:4]
    self_forward(x, vecs, weights, waits, saved, work, dist, slopes)
    x1, g, gp = saved[3:]
    feed_forward(x1, vecs, weights, waits, g, gp, work)
    y_out[...] = (x1[...] + work["acc"][...] + row(vecs, 5)).astype(BF)


def first_forward(x, geo_r, geo_c, vecs, slopes, own, gathered):
    return pl.pallas_call(
        first_forward_kernel,
        out_shape=[shape((R, D), BF)] + [shape(*s) for s in SAVED],
        in_specs=[VM, VM, VM, VM, SM] + [ANY] * 5,
        out_specs=[VM] * 7,
        scratch_shapes=vmem(LAYER_WEIGHTS + WORK) + [pltpu.SemaphoreType.DMA((20,))],
        compiler_params=pltpu.CompilerParams(vmem_limit_bytes=BIG),
    )(x, geo_r, geo_c, vecs, slopes, *own, gathered)


def first_backward_kernel(
    dy_in, x_in, geo_r, geo_c, vecs, slopes, qkv, attn, up, down, gathered, *refs
):
    saved, refs = refs[:6], refs[6:]
    dx_out, gff, gat, vec_out, refs = refs[0], refs[1], refs[2], refs[3], refs[4:]
    weights, work_refs, staging, sems, stage_sems = refs[:4], refs[4:12], refs[12], refs[13], refs[14]
    work, dist = work_of(work_refs), work_refs[7]
    loads = Loads(sems)
    waits = [loads.start(p) for p in weight_pairs((qkv, attn, up, down), gathered, weights)]
    staged = Staged(staging, stage_sems)
    distances(geo_r, geo_c, dist)
    vec_out[...] = jnp.zeros_like(vec_out)
    x1, g, gp = saved[3:]
    feed_backward(
        dy_in[...].astype(F32), x1, vecs, weights, waits, g, gp, gff, staged, vec_out, work
    )
    x = x_in[...].astype(F32) * geo_c[:, 3:4]
    self_backward(x, vecs, weights, waits, saved, gat, staged, vec_out, work, dist, slopes)
    dx_out[...] = work["acc"][...] * geo_c[:, 3:4]
    staged.drain()


def first_backward(dy, x, geo_r, geo_c, vecs, slopes, own, gathered, saved):
    return pl.pallas_call(
        first_backward_kernel,
        out_shape=[
            shape((R, D), F32),
            shape((2, D, FF), BF),
            shape((2, D, 2 * D), BF),
            shape((16, D), F32),
        ],
        in_specs=[VM, VM, VM, VM, VM, SM] + [ANY] * 5 + [VM] * 6,
        out_specs=[VM, ANY, ANY, VM],
        input_output_aliases={},
        scratch_shapes=vmem(LAYER_WEIGHTS + WORK)
        + [
            pltpu.VMEM((3, D, D), BF),
            pltpu.SemaphoreType.DMA((20,)),
            pltpu.SemaphoreType.DMA((3, 2)),
        ],
        compiler_params=pltpu.CompilerParams(vmem_limit_bytes=BIG),
    )(dy, x, geo_r, geo_c, vecs, slopes, *own, gathered, *saved)


def second_kernel(
    x_in, ctx_in, cot_in, geo_r, geo_c, vecs, slopes, qkv, attn, up, down, cq, kv, cw, gathered, *refs
):
    joined, dx_out, optical, gff, gat, gcr, vec_out = refs[:7]
    refs = refs[7:]
    weights, cross, saved, refs = refs[:4], refs[4:7], refs[7:13], refs[13:]
    query, pairs, merged, lse_cross, x2, refs = refs[0], refs[1], refs[2], refs[3], refs[4], refs[5:]
    work_refs, ctx, staging, sems, stage_sems = refs[:8], refs[8], refs[9], refs[10], refs[11]
    work, dist = work_of(work_refs), work_refs[7]
    wcq, wkv, wcw = cross
    loads = Loads(sems)
    groups = weight_pairs((qkv, attn, up, down), gathered, weights)
    waits = [loads.start(groups[0]), loads.start(groups[1])]
    cross_wait = loads.start(cross_pairs((cq, kv, cw), gathered, cross))
    waits += [loads.start(groups[2]), loads.start(groups[3])]
    staged = Staged(staging, stage_sems)
    distances(geo_r, geo_c, dist)
    valid = geo_c[:, 3:4]
    vec_out[...] = jnp.zeros_like(vec_out)
    ctx[...] = (ctx_in[...].astype(F32) * valid).astype(BF)
    x = x_in[...].astype(F32)
    self_forward(x, vecs, weights, waits, saved, work, dist, slopes)
    x1, g, gp = saved[3:]
    normed, _ = normalize(x1[...])
    work["a"][...] = (normed * row(vecs, 10) + row(vecs, 11)).astype(BF)
    wait_all(cross_wait)
    query[...] = mm(work["a"][...], wcq[...]).astype(BF)
    for j in range(2):
        lanes = pl.ds(j * D, D)
        pairs[:, lanes] = mm(ctx[...], wkv[:, lanes]).astype(BF)
    attend(
        lanes_of(query, 0),
        lanes_of(pairs, 0),
        lanes_of(pairs, D),
        lanes_of(merged, 0),
        {"lanes": work["lanes"], "rows": lse_cross},
        dist,
        slopes,
    )
    x2[...] = x1[...] + mm(merged[...], wcw[...]) + row(vecs, 12)
    feed_forward(x2, vecs, weights, waits, g, gp, work)
    joined[...] = (x2[...] + work["acc"][...] + row(vecs, 5)) * valid

    none = [[], [], [], []]
    dy = cot_in[...].astype(F32) * valid
    feed_backward(dy, x2, vecs, weights, none, g, gp, gff, staged, vec_out, work)
    e2 = work["acc"][...].astype(BF)
    work["e"][...] = e2
    vec_out[12:13, :] = jnp.sum(e2.astype(F32), axis=0, keepdims=True)
    work["et"][...] = e2.T
    staged.put(mm(work["et"][...], merged[...]).astype(BF), halves(gcr, 1, HALF))
    work["a"][...] = mmt(work["e"][...], wcw[...]).astype(BF)
    attend_grad(
        lanes_of(query, 0),
        lanes_of(pairs, 0),
        lanes_of(pairs, D),
        lanes_of(work["a"], 0),
        lse_cross,
        dist,
        slopes,
    )
    normed, inverse = normalize(x1[...])
    work["at"][...] = (normed * row(vecs, 10) + row(vecs, 11)).astype(BF).T
    work["et"][...] = ctx[...].T
    staged.put(mm(work["at"][...], query[...]).astype(BF), halves(gcr, 0, 0))
    back = None
    for j, target in enumerate([(0, HALF), (1, 0)]):
        lanes = pl.ds(j * D, D)
        staged.put(mm(work["et"][...], pairs[:, lanes]).astype(BF), halves(gcr, *target))
        term = mmt(pairs[:, lanes], wkv[:, lanes])
        back = term if j == 0 else back + term
    optical[...] = back * valid
    dc = mmt(query[...], wcq[...])
    vec_out[10:11, :] = jnp.sum(dc * normed, axis=0, keepdims=True)
    vec_out[11:12, :] = jnp.sum(dc, axis=0, keepdims=True)
    work["acc"][...] = work["acc"][...] + norm_grad(dc, normed, inverse, row(vecs, 10))
    self_backward(x, vecs, weights, none, saved, gat, staged, vec_out, work, dist, slopes)
    dx_out[...] = work["acc"][...].astype(BF)
    staged.drain()


def second_layer(x, ctx, cot, geo_r, geo_c, vecs, slopes, own, cross_own, gathered):
    extra = [((R, D), BF), ((R, 2 * D), BF), ((R, D), BF), ((16, R), F32), ((R, D), F32)]
    return pl.pallas_call(
        second_kernel,
        out_shape=[
            shape((R, D), F32),
            shape((R, D), BF),
            shape((R, D), F32),
            shape((2, D, FF), BF),
            shape((2, D, 2 * D), BF),
            shape((2, D, 2 * D), BF),
            shape((16, D), F32),
        ],
        in_specs=[VM] * 6 + [SM] + [ANY] * 8,
        out_specs=[VM, VM, VM, ANY, ANY, ANY, VM],
        scratch_shapes=vmem(LAYER_WEIGHTS + CROSS_WEIGHTS + SAVED + extra + WORK)
        + [
            pltpu.VMEM((R, D), BF),
            pltpu.VMEM((2, D, D), BF),
            pltpu.SemaphoreType.DMA((32,)),
            pltpu.SemaphoreType.DMA((2, 2)),
        ],
        compiler_params=pltpu.CompilerParams(vmem_limit_bytes=BIG),
    )(x, ctx, cot, geo_r, geo_c, vecs, slopes, *own, *cross_own, gathered)


def pieces(own, cross_own, index):
    qkv, attn, up, down = own
    cq, kv, cw = cross_own

    def cut(array, first_row, first_col):
        return lax.dynamic_slice(array, (first_row, first_col), (96, HALF))

    late = jnp.maximum(index - 24, 0)
    early = jnp.minimum(index, 23)

    def mixed(stacked, tail):
        return jnp.where(
            index < 24,
            cut(stacked, early * 96, 0),
            cut(tail, (late % 4) * 96, (late // 4) * HALF),
        )

    first = mixed(qkv.reshape(3 * D, HALF), attn)
    second = cut(up, (index % 8) * 96, (index // 8) * HALF)
    third = cut(down, (index % 16) * 96, (index // 16) * HALF)
    stacked = jnp.concatenate([cq[None], kv]).reshape(3 * D, HALF)
    fourth = mixed(stacked, cw)
    return jnp.stack([first, second, third, fourth])


def to_others(array, source):
    m = lax.axis_index("mp")
    half_rows = R // 2
    array = array.astype(BF)

    def cut(part, section):
        return lax.dynamic_slice(array, (part * half_rows, section * HALF), (half_rows, HALF))

    def over(value, pairs):
        return lax.ppermute(value, ("pipe", "mp"), pairs)

    def number(pipe, part):
        return pipe * 2 + part

    s, t = source, 1 - source
    same = over(cut(1 - m, s), [(number(s, i), number(s, 1 - i)) for i in range(2)])
    straight = over(cut(m, t), [(number(s, i), number(t, i)) for i in range(2)])
    crossed = over(cut(1 - m, t), [(number(s, i), number(t, 1 - i)) for i in range(2)])
    return same, straight, crossed


def placed(array, sent, source):
    same, straight, crossed = sent
    m = lax.axis_index("mp")
    here = lax.axis_index("pipe") == source
    own = lax.dynamic_slice(array, (m * (R // 2), source * HALF), (R // 2, HALF))
    mine = jnp.where(here, own, straight.astype(F32))
    others = jnp.where(here, same, crossed).astype(F32)
    swap = m == 1
    return jnp.stack([jnp.where(swap, others, mine), jnp.where(swap, mine, others)])


def local(
    radar_tokens,
    optical_tokens,
    out_cotangent,
    tile_sides,
    norm1_gain,
    norm1_bias,
    qkv_weight,
    attn_weight,
    attn_bias,
    norm2_gain,
    norm2_bias,
    up_weight,
    up_bias,
    down_weight,
    down_bias,
    query_gain,
    query_bias,
    cross_query,
    cross_keyval,
    cross_weight,
    cross_bias,
):
    m = lax.axis_index("mp")
    pipe = lax.axis_index("pipe")
    dp = lax.axis_index("dp")
    joining = pipe == 1

    def mine(stacked):
        return lax.dynamic_index_in_dim(stacked, m, 0, keepdims=False)

    own = (qkv_weight[0].transpose(1, 0, 2), attn_weight[0], up_weight[0], down_weight[0])
    cross_own = (cross_query, cross_keyval.transpose(1, 0, 2), cross_weight)
    gathered = gather_weights(pieces(own, cross_own, dp)).reshape(4, 3072, HALF)
    geo = geometry(mine(tile_sides), R)
    geo_r = jnp.concatenate([geo, jnp.zeros((4, R), F32)])
    geo_c = geo_r.T
    slopes = jnp.exp2(-8.0 * (jnp.arange(H, dtype=jnp.int32) + 1).astype(F32) / H)
    vecs = jnp.concatenate(
        [
            norm1_gain,
            norm1_bias,
            attn_bias,
            norm2_gain,
            norm2_bias,
            down_bias,
            up_bias.reshape(4, D),
            query_gain[None],
            query_bias[None],
            cross_bias[None],
            jnp.zeros((3, D), F32),
        ]
    )
    radar, optical, cotangent = mine(radar_tokens), mine(optical_tokens), mine(out_cotangent)

    def blank(shapes):
        return [jnp.zeros(dims, kind) for dims, kind in shapes]

    forward = lax.cond(
        joining,
        lambda: blank([((R, D), BF)] + SAVED),
        lambda: list(first_forward(radar, geo_r, geo_c, vecs, slopes, own, gathered)),
    )
    y0, saved = forward[0], forward[1:]
    arrived = lax.ppermute(y0, "pipe", [(0, 1)])
    grad_shapes = [((2, D, FF), BF), ((2, D, 2 * D), BF)]
    joined, dx1, back, gff1, gat1, gcr, vec1 = lax.cond(
        joining,
        lambda: list(
            second_layer(
                arrived, optical, cotangent, geo_r, geo_c, vecs, slopes, own, cross_own, gathered
            )
        ),
        lambda: blank(
            [((R, D), F32), ((R, D), BF), ((R, D), F32)]
            + grad_shapes
            + [((2, D, 2 * D), BF), ((16, D), F32)]
        ),
    )
    returned = lax.ppermute(dx1, "pipe", [(1, 0)])
    sent_joined = to_others(joined, 1)
    sent_back = to_others(back, 1)
    radar_back, gff, gat, vec = lax.cond(
        joining,
        lambda: [jnp.zeros((R, D), F32), gff1, gat1, vec1],
        lambda: list(
            first_backward(returned, radar, geo_r, geo_c, vecs, slopes, own, gathered, saved)
        ),
    )
    chunks = gcr.reshape(2, 2, 16, 2, 12, 2 * D).transpose(0, 2, 3, 1, 4, 5)
    chunks = chunks.reshape(2, 4, 4, 48, 2 * D)
    sent_radar = to_others(radar_back, 0)
    off, oat, ovec = scatter_grads(gff, gat, vec)
    return (
        placed(joined, sent_joined, 1),
        placed(radar_back, sent_radar, 0),
        placed(back, sent_back, 1),
    ) + finish_grads(off, oat, ovec, chunks, joining)


def finish_grads(off, oat, ovec, chunks, joining):
    ocr = scatter_cross(chunks)
    sent = lax.ppermute((ocr[:, :12], ovec[10:13]), "pipe", [(1, 0)])
    ocr = jnp.where(joining, ocr[:, 12:], sent[0])
    cross_vec = jnp.where(joining, ovec[10:13], sent[1])
    q, k = oat[0, :, :HALF], oat[0, :, HALF:]
    v, attn = oat[1, :, :HALF], oat[1, :, HALF:]
    cq, ck = ocr[0, :, :HALF], ocr[0, :, HALF:]
    cv, cw = ocr[1, :, :HALF], ocr[1, :, HALF:]
    return (
        ovec[0:1],
        ovec[1:2],
        jnp.stack([q, k, v], axis=1)[None],
        attn.T[None],
        ovec[2:3],
        ovec[3:4],
        ovec[4:5],
        off[0][None],
        ovec[6:10].reshape(1, FF),
        off[1].T[None],
        ovec[5:6],
        cross_vec[0],
        cross_vec[1],
        cq,
        jnp.stack([ck, cv], axis=1),
        cw.T,
        cross_vec[2],
    )


def solution(mesh):
    in_specs = (
        P(None, "dp", None),
        P(None, "dp", None),
        P(None, "dp", None),
        P(None, "dp"),
        P("pipe", None),
        P("pipe", None),
        P("pipe", None, None, "mp"),
        P("pipe", "mp", None),
        P("pipe", None),
        P("pipe", None),
        P("pipe", None),
        P("pipe", None, "mp"),
        P("pipe", None),
        P("pipe", "mp", None),
        P("pipe", None),
        P(),
        P(),
        P(None, "mp"),
        P(None, None, "mp"),
        P("mp", None),
        P(),
    )
    out_specs = (
        P(None, ("dp", "mp"), "pipe"),
        P(None, ("dp", "mp"), "pipe"),
        P(None, ("dp", "mp"), "pipe"),
        P("pipe", None),
        P("pipe", None),
        P("pipe", "dp", None, "mp"),
        P("pipe", "mp", "dp"),
        P("pipe", None),
        P("pipe", None),
        P("pipe", None),
        P("pipe", "dp", "mp"),
        P("pipe", None),
        P("pipe", "mp", "dp"),
        P("pipe", None),
        P(),
        P(),
        P(("pipe", "dp"), "mp"),
        P(("pipe", "dp"), None, "mp"),
        P("mp", ("pipe", "dp")),
        P(),
    )
    return jax.shard_map(local, mesh=mesh, in_specs=in_specs, out_specs=out_specs, check_vma=False)
```

```python
import jax
import jax.numpy as jnp
from jax import lax
from jax.experimental import pallas as pl
from jax.experimental.pallas import tpu as pltpu
from jax.sharding import PartitionSpec as P

H = 12
HS = 64
D = 768
FF = 3072
R = 512
HALF = D // 2
HIDDEN = FF // 2
SLOTS = 3
EPSILON = 1e-05
BF = jnp.bfloat16
F32 = jnp.float32
ANY = pl.BlockSpec(memory_space=pl.ANY)
VM = pl.BlockSpec(memory_space=pltpu.VMEM)
SM = pl.BlockSpec(memory_space=pltpu.SMEM)
MESH = pl.DeviceIdType.MESH
BIG = 61 * 1024 * 1024


def shape(dims, kind):
    return jax.ShapeDtypeStruct(dims, kind)


def vmem(shapes):
    return [pltpu.VMEM(dims, kind) for dims, kind in shapes]


def dma(count):
    return pltpu.SemaphoreType.DMA((count,))


class Place:
    def __init__(self):
        dp = lax.axis_index("dp")
        self.dp = dp
        self.pipe = lax.axis_index("pipe")
        self.m = lax.axis_index("mp")
        self.o = 1 - self.m
        self.core = lax.rem(dp, 2)
        self.twin = 1 - self.core
        chip = dp // 2
        self.x = lax.rem(chip, 4)
        self.z = chip // 4
        self.xs = [self.x] + [lax.rem(self.x + i, 4) for i in (1, 2, 3)]
        self.zs = [self.z] + [lax.rem(self.z + i, 4) for i in (1, 2, 3)]
        self.along_x = [self.at(self.z, x, self.core) for x in self.xs]
        self.along_z = [self.at(z, self.x, self.core) for z in self.zs]
        self.flip_x = self.at(self.z, self.x + 1 - 2 * lax.rem(self.x, 2), self.core)
        self.flip_z = self.at(self.z + 1 - 2 * lax.rem(self.z, 2), self.x, self.core)
        self.sibling = self.at(self.z, self.x, self.twin)
        self.partner = {"mp": self.o}
        self.section = {"pipe": 1 - self.pipe}
        self.crossed = {"pipe": 1 - self.pipe, "mp": self.o}
        self.ring = [self.along_x[1], self.along_x[3], self.along_z[1], self.along_z[3]]
        self.first = self.pipe == 0
        self.second = self.pipe == 1

    def at(self, z, x, core):
        return {"dp": (z * 4 + x) * 2 + core}

    def signal(self, devices):
        barrier = pltpu.get_barrier_semaphore()
        for device in devices:
            pl.semaphore_signal(barrier, inc=1, device_id=device, device_id_type=MESH)

    def await_all(self, devices):
        pl.semaphore_wait(pltpu.get_barrier_semaphore(), len(devices))


def remote(source, target, sems, i, device):
    return pltpu.make_async_remote_copy(
        src_ref=source,
        dst_ref=target,
        send_sem=sems[0].at[i],
        recv_sem=sems[1].at[i],
        device_id=device,
        device_id_type=MESH,
    )


class Links:
    def __init__(self, *sems):
        self.sems = sems
        self.used = 0

    def prepare(self, source, target, device):
        copy = remote(source, target, self.sems, self.used, device)
        self.used += 1
        return copy


class Loads:
    def __init__(self, sems):
        self.sems = sems
        self.used = 0

    def start(self, *pairs):
        copies = []
        for source, target in pairs:
            copies.append(pltpu.make_async_copy(source, target, self.sems.at[self.used]))
            self.used += 1
        for copy in copies:
            copy.start()
        return copies


def wait_all(copies):
    for copy in copies:
        copy.wait()


def lanes_at(first, size):
    return pl.ds(pl.multiple_of(first, 128), size)


def rows_at(first, size):
    return pl.ds(pl.multiple_of(first, 16), size)


class Gather:
    def __init__(self, here, links, out, g, sources):
        c, x, z = here.core, here.x, here.z
        right, left, up, down = here.ring
        xr, xl, zu, zd = here.xs[1], here.xs[3], here.zs[1], here.zs[3]
        a, b = pl.ds(0, 48), pl.ds(48, 48)
        low, high = pl.ds(0, 2), pl.ds(2, 2)
        at = links.used
        self.begins = [
            (condition, remote(source, out.at[g, z, x, c], links.sems, at, here.partner))
            for condition, source in sources
        ]
        links.used = at + 1

        def same(view, device):
            return links.prepare(view, view, device)

        self.steps = [
            [self.begins[-1][1]],
            [
                same(out.at[g, z, x, c, a], right),
                same(out.at[g, z, x, c, a], left),
                same(out.at[g, z, x, c, b], up),
                same(out.at[g, z, x, c, b], down),
            ],
            [
                same(out.at[g, z, xl, c, pl.ds(0, 32)], right),
                same(out.at[g, z, xr, c, pl.ds(32, 16)], left),
                same(out.at[g, zd, x, c, pl.ds(48, 32)], up),
                same(out.at[g, zu, x, c, pl.ds(80, 16)], down),
            ],
            [
                same(out.at[g, z, :, c, a], up),
                same(out.at[g, z, :, c, a], down),
                same(out.at[g, :, x, c, b], right),
                same(out.at[g, :, x, c, b], left),
            ],
            [
                same(out.at[g, zd, low, c, a], up),
                same(out.at[g, zu, high, c, a], down),
                same(out.at[g, low, xl, c, b], right),
                same(out.at[g, high, xr, c, b], left),
            ],
            [same(out.at[g, :, :, c], here.sibling)],
            [],
        ]

    def begin(self):
        for condition, copy in self.begins:
            if condition is None:
                copy.start()
            else:
                pl.when(condition)(copy.start)

    def stage(self, i):
        if 1 <= i < len(self.steps):
            for copy in self.steps[i - 1]:
                copy.wait_recv()
            for copy in self.steps[i]:
                copy.start()

    def drain(self):
        for step in self.steps:
            for copy in step:
                copy.wait_send()


def vector_stages(here, links, vec, vbuf, total):
    order = [
        here.sibling,
        here.flip_x,
        here.along_x[2],
        here.flip_z,
        here.along_z[2],
        here.partner,
    ]
    copies = [links.prepare(total, vbuf.at[i], device) for i, device in enumerate(order)]

    def begin(i):
        def stage():
            if i == 0:
                total[...] = vec[...]
            else:
                copies[i - 1].wait()
                total[...] = total[...] + vbuf[i - 1]
            if i < len(order):
                copies[i].start()

        return stage

    return [begin(i) for i in range(len(order) + 1)]


def scatter_scratch(cols):
    half, quarter = cols // 2, cols // 4
    return [
        pltpu.VMEM((4, 4, 48, cols), BF),
        pltpu.VMEM((2, 2, 2, 48, half), BF),
        pltpu.VMEM((2, 2, 4, 48, half), BF),
        pltpu.VMEM((2, 4, 48, half), BF),
        pltpu.VMEM((2, 2, 48, quarter), BF),
        pltpu.VMEM((2, 2, 48, half), BF),
        pltpu.VMEM((2, 48, half), BF),
        pltpu.VMEM((48, half), BF),
        pltpu.VMEM((2, 24, half), F32),
    ]


def scatter_stages(here, links, local_sem, grads, out, own, buffers):
    other, far, near, mid, far2, near2, late, mated, last = buffers
    cols = own.shape[-1]
    half, quarter = cols // 2, cols // 4
    c, twin, m, o = here.core, here.twin, here.m, here.o
    xs, zs = here.xs, here.zs
    lanes = [pl.ds(0, half), pl.ds(half, half)]
    low, high = pl.ds(0, 2), pl.ds(2, 2)
    fore, aft = pl.ds(0, quarter), pl.ds(quarter, quarter)
    ahead = [here.along_x[1], here.along_z[1]]
    behind = [here.along_x[3], here.along_z[3]]

    def block(ref, way, j):
        if way == 0:
            return ref.at[:, xs[j], :, lanes[0]]
        return ref.at[zs[j], :, :, lanes[1]]

    def part(ref, way, j, span):
        if way == 0:
            return ref.at[span, xs[j], :, lanes[0]]
        return ref.at[zs[j], span, :, lanes[1]]

    def places(way):
        return zs if way == 0 else xs

    order = [(way, j) for j in (2, 1, 3, 0) for way in range(2)]
    local = pltpu.make_async_copy(grads.at[c], own, local_sem)
    exchange = {
        (way, j): links.prepare(
            block(grads.at[twin], way, j), block(other, way, j), here.sibling
        )
        for way, j in order
    }
    one, two, three, four = [], [], [], []
    for way in range(2):
        turn = 1 - way
        at = places(way)
        one.append(
            [
                links.prepare(part(own, way, 2, low), far.at[way, 0], ahead[way]),
                links.prepare(part(own, way, 2, high), far.at[way, 1], behind[way]),
                links.prepare(part(own, way, 1, high), near.at[way, 0, high], ahead[way]),
                links.prepare(part(own, way, 3, low), near.at[way, 1, low], behind[way]),
            ]
        )
        two.append(
            [
                links.prepare(part(own, way, 1, low), near.at[way, 0, low], ahead[way]),
                links.prepare(part(own, way, 3, high), near.at[way, 1, high], behind[way]),
            ]
        )
        three.append(
            [
                links.prepare(mid.at[way, at[2], :, fore], far2.at[way, 0], ahead[turn]),
                links.prepare(mid.at[way, at[2], :, aft], far2.at[way, 1], behind[turn]),
                links.prepare(mid.at[way, at[1], :, aft], near2.at[way, 0, :, aft], ahead[turn]),
                links.prepare(
                    mid.at[way, at[3], :, fore], near2.at[way, 1, :, fore], behind[turn]
                ),
            ]
        )
        four.append(
            [
                links.prepare(mid.at[way, at[1], :, fore], near2.at[way, 0, :, fore], ahead[turn]),
                links.prepare(mid.at[way, at[3], :, aft], near2.at[way, 1, :, aft], behind[turn]),
            ]
        )
    mating = links.prepare(late.at[o], mated, here.partner)
    ending = links.prepare(last.at[0], last.at[1], here.sibling)

    def start():
        local.start()
        for key in order:
            exchange[key].start()

    def add_other(way, j):
        exchange[way, j].wait_recv()
        mine, theirs = block(own, way, j), block(other, way, j)
        for i in range(4):
            mine[i] = mine[i] + theirs[i]

    def ring_one():
        local.wait()
        for way in range(2):
            add_other(way, 2)
            one[way][0].start()
            one[way][1].start()
        for way in range(2):
            add_other(way, 1)
            one[way][2].start()
            add_other(way, 3)
            one[way][3].start()
        for way in range(2):
            add_other(way, 0)

    def ring_two():
        for way in range(2):
            one[way][0].wait_recv()
            target = part(own, way, 1, low)
            for i in range(2):
                target[i] = target[i] + far[way, 0, i]
            two[way][0].start()
            one[way][1].wait_recv()
            target = part(own, way, 3, high)
            for i in range(2):
                target[i] = target[i] + far[way, 1, i]
            two[way][1].start()

    def ring_three():
        for way in range(2):
            for copy in one[way][2:] + two[way]:
                copy.wait_recv()
            mine = block(own, way, 0)
            for i in range(4):
                mid[way, i] = (
                    mine[i].astype(F32) + near[way, 0, i].astype(F32) + near[way, 1, i].astype(F32)
                ).astype(BF)
            for copy in three[way]:
                copy.start()

    def ring_four():
        for way in range(2):
            at = places(way)
            three[way][0].wait_recv()
            target = mid.at[way, at[1], :, fore]
            target[...] = target[...] + far2[way, 0]
            four[way][0].start()
            three[way][1].wait_recv()
            target = mid.at[way, at[3], :, aft]
            target[...] = target[...] + far2[way, 1]
            four[way][1].start()

    def to_partner():
        for way in range(2):
            for copy in three[way][2:] + four[way]:
                copy.wait_recv()
            late[way] = (
                mid[way, places(way)[0]].astype(F32)
                + near2[way, 0].astype(F32)
                + near2[way, 1].astype(F32)
            ).astype(BF)
        mating.start()

    def to_sibling():
        mating.wait_recv()
        total = late[m].astype(F32) + mated[...].astype(F32)
        last[0] = jnp.where(c == 0, total[24:], total[:24])
        out[c] = jnp.where(c == 0, total[:24], total[24:])
        ending.start()

    def finish():
        ending.wait_recv()
        out[twin] = last[1]
        for key in order:
            exchange[key].wait_send()
        for step in one + two + three + four:
            for copy in step:
                copy.wait_send()
        mating.wait_send()
        ending.wait_send()

    return [start, ring_one, ring_two, ring_three, ring_four, to_partner, to_sibling, finish]


def own_scratch(cols):
    return [pltpu.VMEM((4, 4, 48, cols), BF)]


def mm(a, b):
    return lax.dot_general(a, b, (((1,), (0,)), ((), ())), preferred_element_type=F32)


def mmt(a, b):
    return lax.dot_general(a, b, (((1,), (1,)), ((), ())), preferred_element_type=F32)


def tmm(a, b):
    return lax.dot_general(a, b, (((0,), (0,)), ((), ())), preferred_element_type=F32)


def normalize(values):
    centered = values - jnp.mean(values, axis=-1, keepdims=True)
    inverse = lax.rsqrt(jnp.mean(centered * centered, axis=-1, keepdims=True) + EPSILON)
    return centered * inverse, inverse


def norm_grad(upstream, normed, inverse, gain):
    scaled = upstream * gain
    return inverse * (
        scaled
        - jnp.mean(scaled, axis=-1, keepdims=True)
        - normed * jnp.mean(scaled * normed, axis=-1, keepdims=True)
    )


class Geometry:
    def __init__(self, tiles, m, places):
        starts, member = [0], jnp.zeros_like(places)
        for slot in range(SLOTS):
            side = tiles[m, slot]
            starts.append(starts[-1] + side * side)
            member = member + (places >= starts[-1]).astype(jnp.int32)
        first, side = jnp.zeros_like(places), jnp.ones_like(places)
        for slot in range(SLOTS):
            here = member == slot
            first = jnp.where(here, starts[slot], first)
            side = jnp.where(here, jnp.maximum(tiles[m, slot], 1), side)
        first = jnp.where(member == SLOTS, starts[SLOTS], first)
        offset = (places - first).astype(F32)
        side = side.astype(F32)
        self.row = jnp.floor((offset + 0.5) / side)
        self.col = offset - self.row * side
        self.member = member
        self.valid = (member < SLOTS).astype(F32)


def distances(tiles, m, dist, valid):
    down = Geometry(tiles, m, lax.broadcasted_iota(jnp.int32, (R, 1), 0))
    along = Geometry(tiles, m, lax.broadcasted_iota(jnp.int32, (1, R), 1))
    gap_r = down.row - along.row
    gap_c = down.col - along.col
    apart = jnp.sqrt(gap_r * gap_r + gap_c * gap_c)
    dist[...] = jnp.where(down.member == along.member, apart, 1e30)
    valid[...] = jnp.broadcast_to(down.valid, (R, 128))


def head_lanes():
    lane = lax.broadcasted_iota(jnp.int32, (1, 128), 1)
    first = (lane < HS).astype(F32)
    return first.astype(BF), (1.0 - first).astype(BF), first > 0.5, lane


class Heads:
    def __init__(self, q, k, v, o, dist, slopes, lse_lanes, lse_rows):
        self.q, self.k, self.v, self.o = q, k, v, o
        self.dist, self.slopes = dist, slopes
        self.lse_lanes, self.lse_rows = lse_lanes, lse_rows

    def at(self, place, i):
        ref, first = place
        return ref.at[:, lanes_at(first + i * 128, 128)]

    def forward(self, i):
        m0, m1, in_first, lane = head_lanes()
        q, k, v = self.at(self.q, i)[...], self.at(self.k, i)[...], self.at(self.v, i)[...]
        q = q * jnp.asarray(0.125, BF)
        parts = []
        lse = self.lse_lanes
        for j, keep in enumerate((m0, m1)):
            s = mmt(q * keep, k) - self.slopes[2 * i + j] * self.dist[...]
            top = jnp.max(s, axis=-1, keepdims=True)
            raised = jnp.exp(s - top)
            total = jnp.sum(raised, axis=-1, keepdims=True)
            w = (raised * (1.0 / total)).astype(BF)
            parts.append(mm(w, v))
            lse[...] = jnp.where(lane == 2 * i + j, top + jnp.log(total), lse[...])
        self.at(self.o, i)[...] = jnp.where(in_first, parts[0], parts[1]).astype(BF)

    def backward(self, i):
        m0, m1, in_first, lane = head_lanes()
        q, k, v = self.at(self.q, i)[...], self.at(self.k, i)[...], self.at(self.v, i)[...]
        do = self.at(self.o, i)[...]
        q = q * jnp.asarray(0.125, BF)
        dqs, dks, dvs = [], [], []
        for j, keep in enumerate((m0, m1)):
            h = 2 * i + j
            s = mmt(k, q * keep) - self.slopes[h] * self.dist[...]
            p = jnp.exp(s - self.lse_rows[pl.ds(h, 1), :])
            dvs.append(mm(p.astype(BF), do))
            t = p * mmt(v, do * keep)
            ds = (t - p * jnp.sum(t, axis=0, keepdims=True)).astype(BF)
            dks.append(mm(ds, q))
            dqs.append(tmm(ds, k))
        self.at(self.q, i)[...] = (jnp.where(in_first, dqs[0], dqs[1]) * 0.125).astype(BF)
        self.at(self.k, i)[...] = jnp.where(in_first, dks[0], dks[1]).astype(BF)
        self.at(self.v, i)[...] = jnp.where(in_first, dvs[0], dvs[1]).astype(BF)

    def each(self, what, first, last):
        def step(i, carry):
            what(i)
            return carry

        lax.fori_loop(first, last, step, 0)

    def finish(self):
        self.lse_rows[...] = self.lse_lanes[...].T[:16]


class Staged:
    def __init__(self, buffers, sems):
        self.buffers, self.sems = buffers, sems
        self.count = buffers.shape[0]
        self.turn = 0
        self.flying = {}

    def put(self, value, targets):
        slot = self.turn % self.count
        self.turn += 1
        wait_all(self.flying.pop(slot, []))
        self.buffers[slot] = value.reshape(self.buffers.shape[1:])
        copies = []
        for i, (first, size, target) in enumerate(targets):
            copy = pltpu.make_async_copy(
                self.buffers.at[slot, :, :, :, pl.ds(first, size)], target, self.sems.at[slot, i]
            )
            copy.start()
            copies.append(copy)
        self.flying[slot] = copies

    def drain(self):
        for copies in self.flying.values():
            wait_all(copies)
        self.flying = {}


def halves(target, which, first):
    return [
        (part * HALF, HALF, target.at[which, :, :, :, pl.ds(part * D + first, HALF)]) for part in range(2)
    ]


class Vectors:
    def __init__(self, refs):
        (
            self.norm1_gain,
            self.norm1_bias,
            self.attn_bias,
            self.norm2_gain,
            self.norm2_bias,
            self.up_bias,
            self.down_bias,
            self.query_gain,
            self.query_bias,
            self.cross_bias,
        ) = refs


def column_sums(values):
    return jnp.sum(values.astype(F32), axis=0, keepdims=True)


def scaled_norm(values, gain, bias):
    normed, _ = normalize(values)
    return (normed * gain[...] + bias[...]).astype(BF)


LAYER_WEIGHTS = [
    ((4, 2, 96, 3 * D), BF),
    ((2, 2, 2, 96, D), BF),
    ((4, 2, 96, FF), BF),
    ((2, 2, 4, 2, 96, D), BF),
]
CROSS_WEIGHTS = [((4, 2, 96, D), BF), ((4, 2, 96, 2 * D), BF), ((2, 2, 2, 96, D), BF)]
CHUNKED = [
    ((4, 4, 48, 3 * D), BF),
    ((2, 2, 2, 96, D), BF),
    ((4, 4, 48, FF), BF),
    ((2, 2, 4, 2, 96, D), BF),
]
SAVED = [((R, 3 * D), BF), ((R, D), BF), ((16, R), F32), ((R, D), F32), ((R, FF), BF), ((R, FF), BF)]
EXTRA = [((R, D), BF), ((R, 2 * D), BF), ((R, D), BF), ((16, R), F32), ((R, D), F32)]
WORK = [
    ((R, D), BF),
    ((R, 128), F32),
    ((R, D), F32),
    ((D, R), BF),
    ((D, R), BF),
    ((R, R), F32),
    ((R, 128), F32),
]


def flat(ref, lanes=None):
    value = ref[...] if lanes is None else ref[..., lanes]
    return value.reshape(-1, value.shape[-1])


def down_chunk(wdn, j):
    return flat(wdn.at[j // 2, j % 2])


def column_chunks():
    return [pl.ds(j * D, D) for j in range(4)]


def hidden_units(u):
    phi = 0.5 * (1.0 + lax.erf(u * 0.7071067811865476))
    return u * phi, phi + u * jnp.exp(-0.5 * u * u) * 0.3989422804014327


def forward_kernel(*refs):
    here = Place()
    tiles, slopes, radar, optical, cotangent = refs[:5]
    vecs = Vectors(refs[5:15])
    qkv_own, attn_own, up_own, down_own, cq_own, kv_own, cw_own = refs[15:22]
    refs = refs[22:]
    gathered, arrived = refs[:2]
    saved_out, refs = refs[2:8], refs[8:]
    gff, gat, gcr, vec_out, joined_own, back_own, joined_all, back_all = refs[:8]
    refs = refs[8:]
    wqkv, wo, wup, wdn, wcq, wkv, wcw = refs[:7]
    saved, refs = refs[7:13], refs[13:]
    qkv, o, lse_rows, x1, g, gp = saved
    query, pairs, merged, lse_cross, x2 = refs[:5]
    a, lse_lanes, acc, et, at, dist, valid = refs[5:12]
    xin, ctx, cot, e1, e2, out_bf, staging = refs[12:19]
    link_send, link_recv, near_send, near_recv, load_sems, save_sems, stage_sems = refs[19:]
    m, oth = here.m, here.o
    first, second = pl.when(here.first), pl.when(here.second)

    peers = here.ring + [here.sibling, here.partner, here.section]
    here.signal(peers)
    loads = Loads(load_sems)
    heads = Heads((qkv, 0), (qkv, D), (qkv, 2 * D), (o, 0), dist, slopes, lse_lanes, lse_rows)
    cross = Heads(
        (query, 0), (pairs, 0), (pairs, D), (merged, 0), dist, slopes, lse_lanes, lse_cross
    )
    own_qkv = loads.start(
        *[(qkv_own.at[j], wqkv.at[:, :, :, lanes_at(j * D + m * HALF, HALF)]) for j in range(3)]
    )
    own_rest = loads.start(
        (attn_own, wo.at[m]),
        (up_own, wup.at[:, :, :, lanes_at(m * HIDDEN, HIDDEN)]),
        (down_own, wdn.at[m]),
    )
    token_loads = loads.start((optical.at[m], ctx), (cotangent.at[m], cot))
    cross_own = loads.start(
        (cq_own, wcq.at[:, :, :, lanes_at(m * HALF, HALF)]), (cw_own, wcw.at[m])
    )

    i = here.dp
    links = Links(link_send, link_recv)
    block, inner = i // 8, (lax.rem(i // 2, 4), lax.rem(i, 2))
    tail_lanes = lanes_at(lax.rem(i // 4, 2) * HALF, HALF)
    tail = (lax.rem(i // 2, 2), inner[1], slice(None), tail_lanes)
    part = lax.rem(block, 3)
    kv_part = lax.rem(block + 1, 2)

    @second
    def _():
        for j in range(2):
            wkv[:, :, :, lanes_at(j * D + m * HALF, HALF)] = kv_own[:, j, :].reshape(4, 2, 96, HALF)

    here.await_all(peers)
    in_head, in_query = i < 24, i < 8
    in_tail, in_pairs = i >= 24, jnp.logical_and(i >= 8, i < 24)
    kv_lanes = lanes_at(kv_part * D + m * HALF, HALF)
    rest = slice(None)
    down_piece = (lax.rem(block, 2),) + inner + (rest, lanes_at((i // 16) * HALF, HALF))
    gathers = [
        Gather(here, links, gathered, g, sources)
        for g, sources in enumerate(
            [
                [(in_head, qkv_own.at[(part,) + inner]), (in_tail, attn_own.at[tail])],
                [(None, up_own.at[inner + (rest, lanes_at(block * HALF, HALF))])],
                [(None, down_own.at[down_piece])],
                [
                    (in_query, cq_own.at[inner]),
                    (in_pairs, wkv.at[inner + (rest, kv_lanes)]),
                    (in_tail, cw_own.at[tail]),
                ],
            ]
        )
    ]
    for gather in gathers[:3]:
        gather.begin()

    @second
    def _():
        wait_all(cross_own)
        gathers[3].begin()

    def tick(t):
        for j in range(3):
            gathers[j].stage(t - j)
        second(lambda: gathers[3].stage(t - 3))

    distances(tiles, m, dist, valid)

    @first
    def _():
        lse_lanes[...] = jnp.zeros_like(lse_lanes)
        copy = pltpu.make_async_copy(radar.at[m], xin, save_sems.at[6])
        copy.start()
        copy.wait()
        x = xin[...].astype(F32) * valid[:, :1]
        a[...] = scaled_norm(x, vecs.norm1_gain, vecs.norm1_bias)
        wait_all(own_qkv)

    def project(j, part):
        lanes = lanes_at(j * D + part * HALF, HALF)
        qkv[:, lanes] = mm(a[...], flat(wqkv, lanes)).astype(BF)

    tick(1)
    first(lambda: project(0, m))
    tick(2)

    @first
    def _():
        project(1, m)
        project(2, m)

    tick(3)
    first(lambda: heads.forward(m * 3))
    tick(4)
    first(lambda: heads.forward(m * 3 + 1))
    tick(5)
    first(lambda: heads.forward(m * 3 + 2))
    tick(6)
    other_one = loads.start(
        *[
            (gathered.at[0, j], wqkv.at[:, :, :, lanes_at(j * D + oth * HALF, HALF)])
            for j in range(3)
        ],
        *[
            (gathered.at[0, 3, pl.ds(2 * j, 2)], wo.at[oth, :, :, :, pl.ds(j * HALF, HALF)])
            for j in range(2)
        ],
    )
    tick(7)

    @first
    def _():
        wait_all(other_one[:3])
        for j in range(3):
            project(j, oth)

    tick(8)
    other_up = loads.start(
        *[
            (gathered.at[1, j], wup.at[:, :, :, lanes_at(oth * HIDDEN + j * HALF, HALF)])
            for j in range(4)
        ]
    )
    other_down = loads.start(
        *[
            (
                gathered.at[2, pl.ds(2 * j, 2)],
                wdn.at[oth, :, :, :, :, pl.ds(j * HALF, HALF)],
            )
            for j in range(2)
        ]
    )

    def feed_forward(source, rows):
        a[rows] = scaled_norm(source[rows], vecs.norm2_gain, vecs.norm2_bias)
        for j, lanes in enumerate(column_chunks()):
            u = mm(a[rows], flat(wup, lanes)) + vecs.up_bias[:, lanes]
            unit, slope = hidden_units(u)
            g[rows, lanes] = unit.astype(BF)
            gp[rows, lanes] = slope.astype(BF)
            term = mm(g[rows, lanes], down_chunk(wdn, j))
            acc[rows] = term if j == 0 else acc[rows] + term

    near = (near_send, near_recv)
    blocks = [pl.ds(0, R // 2), pl.ds(R // 2, R // 2)]
    forth = [remote(out_bf.at[b], xin.at[b], near, i, here.section) for i, b in enumerate(blocks)]
    back = [
        remote(out_bf.at[b], arrived.at[b], near, 2 + i, here.section)
        for i, b in enumerate(blocks)
    ]

    @first
    def _():
        heads.each(heads.forward, oth * 3, oth * 3 + 3)
        heads.finish()
        saves = [
            pltpu.make_async_copy(source, target, save_sems.at[i])
            for i, (source, target) in enumerate(zip(saved, saved_out))
        ]
        for copy in saves[:3]:
            copy.start()
        wait_all(own_rest)
        wait_all(other_one[3:])
        x = xin[...].astype(F32) * valid[:, :1]
        x1[...] = x + mm(o[...], flat(wo)) + vecs.attn_bias[...]
        saves[3].start()
        wait_all(other_up)
        wait_all(other_down)
        for rows, copy in zip(blocks, forth):
            feed_forward(x1, rows)
            out_bf[rows] = (x1[rows] + acc[rows] + vecs.down_bias[...]).astype(BF)
            copy.start()
        for copy in saves[4:]:
            copy.start()
        wait_all(saves)
        wait_all(token_loads)
        wait_all(cross_own)
        for copy in forth:
            copy.wait_send()
        for copy in back:
            copy.wait_recv()

    @second
    def _():
        gathers[3].stage(6)
        pairs_cross = [(gathered.at[3, 0], wcq.at[:, :, :, lanes_at(oth * HALF, HALF)])]
        for j in range(2):
            pairs_cross += [
                (gathered.at[3, j + 1], wkv.at[:, :, :, lanes_at(j * D + oth * HALF, HALF)]),
                (
                    gathered.at[3, 3, pl.ds(2 * j, 2)],
                    wcw.at[oth, :, :, :, pl.ds(j * HALF, HALF)],
                ),
            ]
        other_cross = loads.start(*pairs_cross)
        for copies in (own_qkv, own_rest, other_one, other_up, other_down):
            wait_all(copies)
        wait_all(token_loads)
        wait_all(other_cross)
        keep = valid[:, :1]
        ctx[...] = (ctx[...].astype(F32) * keep).astype(BF)
        cot[...] = (cot[...].astype(F32) * keep).astype(BF)
        for j in range(2):
            lanes = pl.ds(j * D, D)
            pairs[:, lanes] = mm(ctx[...], flat(wkv, lanes)).astype(BF)
        lse_lanes[...] = jnp.zeros_like(lse_lanes)
        for copy in forth:
            copy.wait_recv()
        a[...] = scaled_norm(xin[...].astype(F32), vecs.norm1_gain, vecs.norm1_bias)
        for j in range(3):
            lanes = pl.ds(j * D, D)
            qkv[:, lanes] = mm(a[...], flat(wqkv, lanes)).astype(BF)
        heads.each(heads.forward, 0, H // 2)
        heads.finish()
        x1[...] = xin[...].astype(F32) + mm(o[...], flat(wo)) + vecs.attn_bias[...]
        a[...] = scaled_norm(x1[...], vecs.query_gain, vecs.query_bias)
        query[...] = mm(a[...], flat(wcq)).astype(BF)
        cross.each(cross.forward, 0, H // 2)
        cross.finish()
        x2[...] = x1[...] + mm(merged[...], flat(wcw)) + vecs.cross_bias[...]
        feed_forward(x2, pl.ds(0, R))
        acc[...] = (x2[...] + acc[...] + vecs.down_bias[...]) * keep
        joined_own[...] = acc[rows_at(m * (R // 2), R // 2), pl.ds(HALF, HALF)]
        joined_all[...] = acc[...].astype(BF)

        for j, lanes in enumerate(column_chunks()):
            gp[:, lanes] = (mmt(cot[...], down_chunk(wdn, j)) * gp[:, lanes].astype(F32)).astype(BF)
            term = mmt(gp[:, lanes], flat(wup, lanes))
            acc[...] = term if j == 0 else acc[...] + term
        vec_out[...] = jnp.zeros_like(vec_out)
        dm = acc[...]
        normed, inverse = normalize(x2[...])
        vec_out[3:4, :] = column_sums(dm * normed)
        vec_out[4:5, :] = column_sums(dm)
        acc[...] = cot[...].astype(F32) + norm_grad(dm, normed, inverse, vecs.norm2_gain[...])
        e2[...] = acc[...].astype(BF)
        a[...] = mmt(e2[...], flat(wcw)).astype(BF)
        cross_back = Heads(
            (query, 0), (pairs, 0), (pairs, D), (a, 0), dist, slopes, lse_lanes, lse_cross
        )
        cross_back.each(cross_back.backward, 0, H // 2)
        dc = mmt(query[...], flat(wcq))
        normed, inverse = normalize(x1[...])
        vec_out[10:11, :] = column_sums(dc * normed)
        vec_out[11:12, :] = column_sums(dc)
        acc[...] = acc[...] + norm_grad(dc, normed, inverse, vecs.query_gain[...])
        e1[...] = acc[...].astype(BF)
        a[...] = mmt(e1[...], flat(wo)).astype(BF)
        self_back = Heads(
            (qkv, 0), (qkv, D), (qkv, 2 * D), (a, 0), dist, slopes, lse_lanes, lse_rows
        )
        self_back.each(self_back.backward, 0, H // 2)
        sums = []
        for rows, copy in zip(blocks, back):
            da = mmt(qkv[rows], flat(wqkv))
            normed, inverse = normalize(xin[rows].astype(F32))
            sums.append((column_sums(da * normed), column_sums(da)))
            out_bf[rows] = (
                acc[rows] + norm_grad(da, normed, inverse, vecs.norm1_gain[...])
            ).astype(BF)
            copy.start()
        vec_out[0:1, :] = sums[0][0] + sums[1][0]
        vec_out[1:2, :] = sums[0][1] + sums[1][1]

        staged = Staged(staging, stage_sems)
        acc[...] = mmt(pairs[...], flat(wkv)) * keep
        back_own[...] = acc[rows_at(m * (R // 2), R // 2), pl.ds(HALF, HALF)]
        back_all[...] = acc[...].astype(BF)
        permute = chunk_order()
        et[...] = mmt(permute, e2[...]).astype(BF)
        staged.put(mm(et[...], merged[...]).astype(BF), halves(gcr, 1, HALF))
        a[...] = scaled_norm(x1[...], vecs.query_gain, vecs.query_bias)
        et[...] = mmt(permute, a[...]).astype(BF)
        staged.put(mm(et[...], query[...]).astype(BF), halves(gcr, 0, 0))
        et[...] = mmt(permute, ctx[...]).astype(BF)
        for j, target in enumerate([(0, HALF), (1, 0)]):
            staged.put(mm(et[...], pairs[:, pl.ds(j * D, D)]).astype(BF), halves(gcr, *target))
        et[...] = cot[...].T
        a[...] = scaled_norm(x2[...], vecs.norm2_gain, vecs.norm2_bias)
        at[...] = a[...].T
        for j, lanes in enumerate(column_chunks()):
            vec_out[6 + j : 7 + j, :] = column_sums(gp[:, lanes])
            staged.put(mm(et[...], g[:, lanes]).astype(BF), [(0, D, gff.at[1, :, :, :, lanes])])
            staged.put(mm(at[...], gp[:, lanes]).astype(BF), [(0, D, gff.at[0, :, :, :, lanes])])
        vec_out[2:3, :] = column_sums(e1[...])
        vec_out[5:6, :] = column_sums(cot[...])
        vec_out[12:13, :] = column_sums(e2[...])
        et[...] = e1[...].T
        staged.put(mm(et[...], o[...]).astype(BF), halves(gat, 1, HALF))
        a[...] = scaled_norm(xin[...].astype(F32), vecs.norm1_gain, vecs.norm1_bias)
        at[...] = a[...].T
        for j, target in enumerate([(0, 0), (0, HALF), (1, 0)]):
            staged.put(mm(at[...], qkv[:, pl.ds(j * D, D)]).astype(BF), halves(gat, *target))
        staged.drain()
        for copy in back:
            copy.wait_send()
        gathers[3].drain()

    for gather in gathers[:3]:
        gather.drain()


def chunk_order():
    r = lax.broadcasted_iota(jnp.int32, (D, 1), 0).astype(F32)
    chunk = jnp.floor((r + 0.5) / 48.0)
    inner = r - chunk * 48.0
    core = (inner >= 24.0).astype(F32)
    inner = inner - 24.0 * core
    section = (inner >= 12.0).astype(F32)
    source = 384.0 * section + 24.0 * chunk + 12.0 * core + inner - 12.0 * section
    columns = lax.broadcasted_iota(jnp.int32, (D, D), 1).astype(F32)
    return (columns == source).astype(F32).astype(BF)


def forward(tiles, slopes, tokens, vecs, own):
    scratch = vmem(
        LAYER_WEIGHTS + CROSS_WEIGHTS + SAVED + EXTRA + WORK + [((R, D), BF)] * 6 + [((2, 4, 4, 48, D), BF)]
    )
    quarter = shape((R // 2, HALF), F32)
    return pl.pallas_call(
        forward_kernel,
        out_shape=[shape((4, 4, 4, 2, 96, HALF), BF), shape((R, D), BF)]
        + [shape(*s) for s in SAVED]
        + [shape((2, 4, 4, 48, n), BF) for n in (FF, 2 * D, 2 * D)]
        + [shape((16, D), F32), quarter, quarter, shape((R, D), BF), shape((R, D), BF)],
        in_specs=[SM, SM] + [ANY] * 3 + [VM] * 10 + [ANY] * 5 + [VM] + [ANY],
        out_specs=[ANY] * 11 + [VM] * 5,
        scratch_shapes=scratch
        + [dma(72), dma(72), dma(4), dma(4), dma(40), dma(7), pltpu.SemaphoreType.DMA((2, 2))],
        compiler_params=pltpu.CompilerParams(
            collective_id=0, has_side_effects=True, vmem_limit_bytes=BIG
        ),
    )(tiles, slopes, *tokens, *vecs, *own)


def backward_kernel(*refs):
    here = Place()
    tiles, slopes, radar, dy_in = refs[:4]
    vecs = Vectors(refs[4:14])
    qkv_own, attn_own, up_own, down_own, gathered, gathered48 = refs[14:20]
    saved_in, refs = refs[20:26], refs[26:]
    vec_in, joined_all, back_all, gcr = refs[:4]
    refs = refs[6:]
    gff, gat, off, oat, ocr, vec_total, vec_other, radar_own, quarters, ocr_other = refs[:10]
    refs = refs[10:]
    wqkv, wo, wup, wdn = refs[:4]
    saved, refs = refs[4:10], refs[10:]
    qkv, o, lse_rows, x1, g, gp = saved
    a, lse_lanes, acc, et, at, dist, valid = refs[:7]
    xin, out_bf, staging, vec, vbuf = refs[7:12]
    own_at, cross_sums = refs[12:14]
    ff_buffers, at_buffers, cross_buffers, refs = refs[14:23], refs[23:32], refs[32:41], refs[41:]
    link_send, link_recv, far_send, far_recv, load_sems, local_sems, stage_sems = refs
    m, oth = here.m, here.o
    first, second = pl.when(here.first), pl.when(here.second)
    peers = here.ring + [
        here.sibling,
        here.partner,
        here.along_x[2],
        here.along_z[2],
        here.section,
        here.crossed,
    ]
    here.signal(peers)
    loads = Loads(load_sems)
    links = Links(link_send, link_recv)
    far = (far_send, far_recv)
    staged = Staged(staging, stage_sems)
    heads = Heads((qkv, 0), (qkv, D), (qkv, 2 * D), (a, 0), dist, slopes, lse_lanes, lse_rows)
    chunks = column_chunks()

    @first
    def _():
        cotangent = loads.start((dy_in, out_bf))
        copies = loads.start(
            (down_own, wdn.at[m]),
            *[
                (gathered.at[2, pl.ds(2 * j, 2)], wdn.at[oth, :, :, :, :, pl.ds(j * HALF, HALF)])
                for j in range(2)
            ],
        )
        units = [
            loads.start((saved_in[5].at[:, c], gp.at[:, c]), (saved_in[4].at[:, c], g.at[j]))
            for j, c in enumerate(chunks[:2])
        ]
        early = loads.start((saved_in[3], x1), (radar.at[m], xin))
        copies_up = loads.start(
            (up_own, wup.at[:, :, :, lanes_at(m * HIDDEN, HIDDEN)]),
            *[
                (gathered48.at[1, j], wup.at[:, :, :, lanes_at(oth * HIDDEN + j * HALF, HALF)])
                for j in range(4)
            ],
        )
        units += [loads.start((saved_in[5].at[:, c], gp.at[:, c])) for c in chunks[2:]]
        late = loads.start(
            (saved_in[0], qkv),
            (saved_in[1], o),
            (saved_in[2], lse_rows),
            (attn_own, wo.at[m]),
            *[
                (gathered.at[0, 3, pl.ds(2 * j, 2)], wo.at[oth, :, :, :, pl.ds(j * HALF, HALF)])
                for j in range(2)
            ],
            *[
                (qkv_own.at[j], wqkv.at[:, :, :, lanes_at(j * D + m * HALF, HALF)])
                for j in range(3)
            ],
            *[
                (gathered48.at[0, j], wqkv.at[:, :, :, lanes_at(j * D + oth * HALF, HALF)])
                for j in range(3)
            ],
        )
        distances(tiles, m, dist, valid)
        vec[...] = jnp.zeros_like(vec)
        wait_all(cotangent)
        e3 = out_bf[...]
        vec[5:6, :] = column_sums(e3)
        et[...] = e3.T
        wait_all(early)
        a[...] = scaled_norm(x1[...], vecs.norm2_gain, vecs.norm2_bias)
        at[...] = a[...].T
        wait_all(copies)
        for j, lanes in enumerate(chunks):
            wait_all(units[j])
            du = (mmt(out_bf[...], down_chunk(wdn, j)) * gp[:, lanes].astype(F32)).astype(BF)
            gp[:, lanes] = du
            vec[6 + j : 7 + j, :] = column_sums(du)
            staged.put(mm(et[...], g[j % 2]).astype(BF), [(0, D, gff.at[1, :, :, :, lanes])])
            staged.put(mm(at[...], gp[:, lanes]).astype(BF), [(0, D, gff.at[0, :, :, :, lanes])])
            if j < 2:
                units[j + 2] += loads.start((saved_in[4].at[:, chunks[j + 2]], g.at[j]))
            if j == 0:
                wait_all(copies_up)
            term = mmt(gp[:, lanes], flat(wup, lanes))
            acc[...] = term if j == 0 else acc[...] + term
        wait_all(late)
        staged.drain()

    @second
    def _():
        vec[...] = vec_in[...]

    here.await_all(peers)
    ff = scatter_stages(here, links, local_sems.at[0], gff, off, wup, ff_buffers)
    mid = scatter_stages(here, links, local_sems.at[1], gat, oat, own_at, at_buffers)
    vec_steps = vector_stages(here, links, vec, vbuf, vec_total)
    own_cross = wqkv.at[:, :, :, pl.ds(0, 2 * D)]
    cross = scatter_stages(
        here, links, local_sems.at[2], gcr, cross_sums, own_cross, cross_buffers
    )

    def quarter_copies(source, kind):
        half_rows = R // 2
        mine, others = rows_at(m * half_rows, half_rows), rows_at(oth * half_rows, half_rows)
        sender, receiver = (0, 1) if kind == 2 else (1, 0)
        same = pl.ds(sender * HALF, HALF)
        over = pl.ds(receiver * HALF, HALF)
        return [
            remote(source.at[mine, over], quarters.at[kind, 0], far, 3 * kind, here.section),
            remote(source.at[others, over], quarters.at[kind, 1], far, 3 * kind + 1, here.crossed),
            remote(source.at[others, same], quarters.at[kind, 1], far, 3 * kind + 2, here.partner),
        ]

    sent = [quarter_copies(s, i) for i, s in enumerate((joined_all, back_all, out_bf))]
    cross_sent = remote(ocr.at[0], ocr_other, far, 9, here.section)
    vec_sent = remote(vec_total, vec_other, far, 10, here.section)

    @second
    def _():
        for copies in sent[:2]:
            for copy in copies:
                copy.start()
        cross[0]()

    ff[0]()
    second(cross[1])

    @first
    def _():
        dm = acc[...]
        normed, inverse = normalize(x1[...])
        vec[3:4, :] = column_sums(dm * normed)
        vec[4:5, :] = column_sums(dm)
        acc[...] = out_bf[...].astype(F32) + norm_grad(dm, normed, inverse, vecs.norm2_gain[...])
        e1 = acc[...].astype(BF)
        vec[2:3, :] = column_sums(e1)
        out_bf[...] = e1
        a[...] = mmt(out_bf[...], flat(wo)).astype(BF)

    ff[1]()

    @first
    def _():
        et[...] = out_bf[...].T
        staged.put(mm(et[...], o[...]).astype(BF), halves(gat, 1, HALF))
        heads.each(heads.backward, 0, 2)
        staged.drain()

    second(cross[2])
    ff[2]()
    second(cross[3])
    first(lambda: heads.each(heads.backward, 2, 4))
    ff[3]()
    second(cross[4])
    first(lambda: heads.each(heads.backward, 4, 6))
    ff[4]()
    second(cross[5])

    @first
    def _():
        x = xin[...].astype(F32) * valid[:, :1]
        a[...] = scaled_norm(x, vecs.norm1_gain, vecs.norm1_bias)
        at[...] = a[...].T
        for j, target in enumerate([(0, 0), (0, HALF), (1, 0)]):
            staged.put(mm(at[...], qkv[:, pl.ds(j * D, D)]).astype(BF), halves(gat, *target))
        staged.drain()

    mid[0]()
    ff[5]()
    second(cross[6])

    @first
    def _():
        da = mmt(qkv[...], flat(wqkv))
        normed, inverse = normalize(xin[...].astype(F32) * valid[:, :1])
        vec[0:1, :] = column_sums(da * normed)
        vec[1:2, :] = column_sums(da)
        acc[...] = (acc[...] + norm_grad(da, normed, inverse, vecs.norm1_gain[...])) * valid[:, :1]
        radar_own[...] = acc[rows_at(m * (R // 2), R // 2), pl.ds(0, HALF)]
        out_bf[...] = acc[...].astype(BF)
        for copy in sent[2]:
            copy.start()

    @second
    def _():
        cross[7]()
        for section in range(2):
            for which in range(2):
                ocr[section, which] = cross_sums[which][section * 12 : section * 12 + 12]
        cross_sent.start()

    mid[1]()
    vec_steps[0]()
    ff[6]()
    vec_steps[1]()
    mid[2]()
    vec_steps[2]()
    ff[7]()
    mid[3]()
    vec_steps[3]()
    mid[4]()
    vec_steps[4]()
    mid[5]()
    vec_steps[5]()
    mid[6]()
    vec_steps[6]()

    @second
    def _():
        vec_sent.start()

    mid[7]()

    @first
    def _():
        for copies in sent[:2]:
            copies[0].wait_recv()
            copies[1].wait_recv()
        sent[2][2].wait_recv()
        for copy in sent[2]:
            copy.wait_send()
        cross_sent.wait_recv()
        vec_sent.wait_recv()

    @second
    def _():
        sent[2][0].wait_recv()
        sent[2][1].wait_recv()
        for copies in sent[:2]:
            copies[2].wait_recv()
            for copy in copies:
                copy.wait_send()
        cross_sent.wait_send()
        vec_sent.wait_send()


def backward(tiles, slopes, radar, dy, vecs, own, gathered, saved, vec, quarters, gcr, gff, gat):
    scratch = vmem(
        CHUNKED
        + SAVED[:4]
        + [((2, R, D), BF)]
        + SAVED[5:]
        + WORK
        + [((R, D), BF)] * 2
        + [((2, 4, 4, 48, D), BF), ((16, D), F32), ((6, 16, D), F32)]
    )
    vector = shape((16, D), F32)
    qkv, attn, up, down = own
    return pl.pallas_call(
        backward_kernel,
        out_shape=[
            shape(gff.shape, BF),
            shape(gat.shape, BF),
            shape((2, 24, HIDDEN), F32),
            shape((2, 24, D), F32),
            shape((2, 2, 12, D), F32),
            vector,
            vector,
            shape((R // 2, HALF), F32),
            shape((3, 2, R // 2, HALF), BF),
            shape((2, 12, D), F32),
        ],
        in_specs=[SM, SM, ANY, ANY] + [VM] * 10 + [ANY] * 6 + [ANY] * 6 + [VM] + [ANY] * 5,
        out_specs=[ANY, ANY] + [VM] * 6 + [ANY, VM],
        input_output_aliases={30: 0, 31: 1},
        scratch_shapes=scratch
        + own_scratch(2 * D)
        + [pltpu.VMEM((2, 24, D), F32)]
        + scatter_scratch(FF)
        + scatter_scratch(2 * D)
        + scatter_scratch(2 * D)
        + [dma(112), dma(112), dma(11), dma(11), dma(40), dma(3), pltpu.SemaphoreType.DMA((2, 2))],
        compiler_params=pltpu.CompilerParams(
            collective_id=1, has_side_effects=True, vmem_limit_bytes=BIG
        ),
    )(
        tiles,
        slopes,
        radar,
        dy,
        *vecs,
        qkv.reshape(3, 4, 4, 48, HALF),
        attn,
        up.reshape(4, 4, 48, HIDDEN),
        down,
        gathered,
        gathered.reshape(4, 4, 4, 4, 48, HALF),
        *saved,
        vec,
        *quarters,
        gcr,
        gff,
        gat,
    )


def local(
    radar_tokens,
    optical_tokens,
    out_cotangent,
    tile_sides,
    norm1_gain,
    norm1_bias,
    qkv_weight,
    attn_weight,
    attn_bias,
    norm2_gain,
    norm2_bias,
    up_weight,
    up_bias,
    down_weight,
    down_bias,
    query_gain,
    query_bias,
    cross_query,
    cross_keyval,
    cross_weight,
    cross_bias,
):
    m = lax.axis_index("mp")
    joining = lax.axis_index("pipe") == 1
    slopes = jnp.exp2(-8.0 * (jnp.arange(H, dtype=jnp.int32) + 1).astype(F32) / H)
    vecs = (
        norm1_gain,
        norm1_bias,
        attn_bias,
        norm2_gain,
        norm2_bias,
        up_bias,
        down_bias,
        query_gain[None],
        query_bias[None],
        cross_bias[None],
    )
    own = (
        qkv_weight[0].transpose(1, 0, 2).reshape(3, 4, 2, 96, HALF),
        attn_weight.reshape(2, 2, 96, D),
        up_weight.reshape(4, 2, 96, HIDDEN),
        down_weight.reshape(2, 4, 2, 96, D),
    )
    cross_own = (
        cross_query.reshape(4, 2, 96, HALF),
        cross_keyval,
        cross_weight.reshape(2, 2, 96, D),
    )
    tokens = (radar_tokens, optical_tokens, out_cotangent)
    results = forward(
        tile_sides, slopes, tokens, vecs, own + cross_own
    )
    gathered, dy0 = results[:2]
    saved = results[2:8]
    gff, gat, gcr, vec, joined_own, back_own, joined_all, back_all = results[8:]
    outs = backward(
        tile_sides,
        slopes,
        radar_tokens,
        dy0,
        vecs,
        own,
        gathered,
        saved,
        vec,
        (joined_all, back_all),
        gcr,
        gff,
        gat,
    )
    _, _, off, oat, ocr, vec, vec_other, radar_own, quarters, ocr_other = outs

    def placed(own_quarter, kind, here):
        mine = jnp.where(here, own_quarter, quarters[kind, 0].astype(F32))
        others = quarters[kind, 1].astype(F32)
        swap = m == 1
        return jnp.stack([jnp.where(swap, others, mine), jnp.where(swap, mine, others)])

    crossed = jnp.where(joining, vec[10:13], vec_other[10:13])
    ocr = jnp.where(joining, ocr[1], ocr_other)
    q, k = oat[0, :, :HALF], oat[0, :, HALF:]
    v, attn = oat[1, :, :HALF], oat[1, :, HALF:]
    cq, ck = ocr[0, :, :HALF], ocr[0, :, HALF:]
    cv, cw = ocr[1, :, :HALF], ocr[1, :, HALF:]
    return (
        placed(joined_own, 0, joining),
        placed(radar_own, 2, jnp.logical_not(joining)),
        placed(back_own, 1, joining),
        vec[0:1],
        vec[1:2],
        jnp.stack([q, k, v], axis=1)[None],
        attn.T[None],
        vec[2:3],
        vec[3:4],
        vec[4:5],
        off[0][None],
        vec[6:10].reshape(1, FF),
        off[1].T[None],
        vec[5:6],
        crossed[0],
        crossed[1],
        cq,
        jnp.stack([ck, cv], axis=1),
        cw.T,
        crossed[2],
    )


def solution(mesh):
    in_specs = (
        P(None, "dp", None),
        P(None, "dp", None),
        P(None, "dp", None),
        P(None, "dp"),
        P("pipe", None),
        P("pipe", None),
        P("pipe", None, None, "mp"),
        P("pipe", "mp", None),
        P("pipe", None),
        P("pipe", None),
        P("pipe", None),
        P("pipe", None, "mp"),
        P("pipe", None),
        P("pipe", "mp", None),
        P("pipe", None),
        P(),
        P(),
        P(None, "mp"),
        P(None, None, "mp"),
        P("mp", None),
        P(),
    )
    out_specs = (
        P(None, ("dp", "mp"), "pipe"),
        P(None, ("dp", "mp"), "pipe"),
        P(None, ("dp", "mp"), "pipe"),
        P("pipe", None),
        P("pipe", None),
        P("pipe", "dp", None, "mp"),
        P("pipe", "mp", "dp"),
        P("pipe", None),
        P("pipe", None),
        P("pipe", None),
        P("pipe", "dp", "mp"),
        P("pipe", None),
        P("pipe", "mp", "dp"),
        P("pipe", None),
        P(),
        P(),
        P(("pipe", "dp"), "mp"),
        P(("pipe", "dp"), None, "mp"),
        P("mp", ("pipe", "dp")),
        P(),
    )
    return jax.shard_map(local, mesh=mesh, in_specs=in_specs, out_specs=out_specs, check_vma=False)
```

```python
import jax
import jax.numpy as jnp
from jax import lax
from jax.experimental import pallas as pl
from jax.experimental.pallas import tpu as pltpu
from jax.sharding import PartitionSpec as P

H = 12
HS = 64
D = 768
FF = 3072
R = 512
HALF = D // 2
HIDDEN = FF // 2
SLOTS = 3
EPSILON = 1e-05
BF = jnp.bfloat16
F32 = jnp.float32
ANY = pl.BlockSpec(memory_space=pl.ANY)
VM = pl.BlockSpec(memory_space=pltpu.VMEM)
SM = pl.BlockSpec(memory_space=pltpu.SMEM)
MESH = pl.DeviceIdType.MESH
BIG = 62 * 1024 * 1024


def shape(dims, kind):
    return jax.ShapeDtypeStruct(dims, kind)


def vmem(shapes):
    return [pltpu.VMEM(dims, kind) for dims, kind in shapes]


def dma(count):
    return pltpu.SemaphoreType.DMA((count,))


class Place:
    def __init__(self):
        dp = lax.axis_index("dp")
        self.dp = dp
        self.pipe = lax.axis_index("pipe")
        self.m = lax.axis_index("mp")
        self.o = 1 - self.m
        self.core = lax.rem(dp, 2)
        self.twin = 1 - self.core
        chip = dp // 2
        self.x = lax.rem(chip, 4)
        self.z = chip // 4
        self.xs = [self.x] + [lax.rem(self.x + i, 4) for i in (1, 2, 3)]
        self.zs = [self.z] + [lax.rem(self.z + i, 4) for i in (1, 2, 3)]
        self.along_x = [self.at(self.z, x, self.core) for x in self.xs]
        self.along_z = [self.at(z, self.x, self.core) for z in self.zs]
        self.sibling = self.at(self.z, self.x, self.twin)
        self.partner = {"mp": self.o}
        self.section = {"pipe": 1 - self.pipe}
        self.crossed = {"pipe": 1 - self.pipe, "mp": self.o}
        self.diagonal = dict(self.sibling, mp=self.o)
        self.ring = [self.along_x[1], self.along_x[3], self.along_z[1], self.along_z[3]]
        self.first = self.pipe == 0
        self.second = self.pipe == 1

    def at(self, z, x, core):
        return {"dp": (z * 4 + x) * 2 + core}

    def signal(self, devices):
        barrier = pltpu.get_barrier_semaphore()
        for device in devices:
            pl.semaphore_signal(barrier, inc=1, device_id=device, device_id_type=MESH)

    def await_all(self, devices):
        pl.semaphore_wait(pltpu.get_barrier_semaphore(), len(devices))


def remote(source, target, sems, i, device):
    return pltpu.make_async_remote_copy(
        src_ref=source,
        dst_ref=target,
        send_sem=sems[0].at[i],
        recv_sem=sems[1].at[i],
        device_id=device,
        device_id_type=MESH,
    )


class Links:
    def __init__(self, *sems):
        self.sems = sems
        self.used = 0

    def prepare(self, source, target, device):
        copy = remote(source, target, self.sems, self.used, device)
        self.used += 1
        return copy


class Loads:
    def __init__(self, sems):
        self.sems = sems
        self.used = 0

    def start(self, *pairs):
        copies = []
        for source, target in pairs:
            copies.append(pltpu.make_async_copy(source, target, self.sems.at[self.used]))
            self.used += 1
        for copy in copies:
            copy.start()
        return copies


def wait_all(copies):
    for copy in copies:
        copy.wait()


def lanes_at(first, size):
    return pl.ds(pl.multiple_of(first, 128), size)


def rows_at(first, size):
    return pl.ds(pl.multiple_of(first, 16), size)


class Gather:
    def __init__(self, here, links, out, g, sources):
        c, x, z = here.core, here.x, here.z
        xs, zs = here.xs, here.zs
        right, left, up, down = here.ring
        a, b = pl.ds(0, 48), pl.ds(48, 48)
        low, high = pl.ds(0, 2), pl.ds(2, 2)
        at = links.used
        self.begins = [
            (condition, remote(source, out.at[g, z, x, c], links.sems, at, here.partner))
            for condition, source in sources
        ]
        links.used = at + 1

        def same(view, device):
            return links.prepare(view, view, device)

        direct, early = [], []
        for j in (2, 1, 3):
            direct.append(same(out.at[g, z, x, c, a], here.along_x[j]))
            direct.append(same(out.at[g, z, x, c, b], here.along_z[j]))
        for j in (0, 1, 3):
            early.append(same(out.at[g, zs[j], :, c, a], here.sibling))
            early.append(same(out.at[g, :, xs[j], c, b], here.sibling))
        near = [
            same(out.at[g, z, :, c, a], up),
            same(out.at[g, z, :, c, a], down),
            same(out.at[g, :, x, c, b], right),
            same(out.at[g, :, x, c, b], left),
        ]
        relayed = [
            same(out.at[g, zs[3], low, c, a], up),
            same(out.at[g, zs[1], high, c, a], down),
            same(out.at[g, low, xs[3], c, b], right),
            same(out.at[g, high, xs[1], c, b], left),
        ]
        late = [
            same(out.at[g, zs[2], :, c, a], here.sibling),
            same(out.at[g, :, xs[2], c, b], here.sibling),
        ]
        first = [self.begins[-1][1]]
        self.waits = [[], first, direct, near, relayed, early + late]
        self.starts = [[], direct, near, relayed + early, late, []]
        self.all = first + direct + near + relayed + early + late

    def begin(self):
        for condition, copy in self.begins:
            if condition is None:
                copy.start()
            else:
                pl.when(condition)(copy.start)

    def stage(self, i):
        for copy in self.waits[i]:
            copy.wait_recv()
        for copy in self.starts[i]:
            copy.start()

    def drain(self):
        for copy in self.all:
            copy.wait_send()


def vector_stages(here, links, vec, vbuf, total):
    rounds = [[here.sibling], here.along_x[1:], here.along_z[1:], [here.partner]]
    copies, used = [], 0
    for devices in rounds:
        copies.append(
            [links.prepare(total, vbuf.at[used + i], d) for i, d in enumerate(devices)]
        )
        used += len(devices)

    def begin(i):
        def stage():
            if i == 0:
                total[...] = vec[...]
            else:
                first = sum(len(devices) for devices in rounds[: i - 1])
                for copy in copies[i - 1]:
                    copy.wait()
                value = total[...]
                for j in range(len(rounds[i - 1])):
                    value = value + vbuf[first + j]
                total[...] = value
            if i < len(rounds):
                for copy in copies[i]:
                    copy.start()

        return stage

    return [begin(i) for i in range(len(rounds) + 1)]


def scatter_scratch(cols):
    half = cols // 2
    return [
        pltpu.VMEM((4, 4, 48, cols), BF),
        pltpu.VMEM((2, 2, 2, 48, half), BF),
        pltpu.VMEM((2, 2, 4, 48, half), BF),
        pltpu.VMEM((2, 4, 48, half), BF),
        pltpu.VMEM((2, 3, 48, half), BF),
        pltpu.VMEM((2, 2, 24, half), F32),
        pltpu.VMEM((3, 24, half), F32),
    ]


def scatter_stages(here, links, local_sem, grads, out, own, buffers):
    other, far, near, mid, near2, late, last = buffers
    cols = own.shape[-1]
    half = cols // 2
    c, twin, m, o = here.core, here.twin, here.m, here.o
    xs, zs = here.xs, here.zs
    lanes = [pl.ds(0, half), pl.ds(half, half)]
    low, high = pl.ds(0, 2), pl.ds(2, 2)
    ahead = [here.along_x[1], here.along_z[1]]
    behind = [here.along_x[3], here.along_z[3]]

    def block(ref, way, j):
        if way == 0:
            return ref.at[:, xs[j], :, lanes[0]]
        return ref.at[zs[j], :, :, lanes[1]]

    def part(ref, way, j, span):
        if way == 0:
            return ref.at[span, xs[j], :, lanes[0]]
        return ref.at[zs[j], span, :, lanes[1]]

    def places(way):
        return zs if way == 0 else xs

    order = [(way, j) for j in (2, 1, 3, 0) for way in range(2)]
    local = pltpu.make_async_copy(grads.at[c], own, local_sem)
    exchange = {
        (way, j): links.prepare(
            block(grads.at[twin], way, j), block(other, way, j), here.sibling
        )
        for way, j in order
    }
    one, two, three = [], [], []
    for way in range(2):
        turn = 1 - way
        at = places(way)
        one.append(
            [
                links.prepare(part(own, way, 2, low), far.at[way, 0], ahead[way]),
                links.prepare(part(own, way, 2, high), far.at[way, 1], behind[way]),
                links.prepare(part(own, way, 1, high), near.at[way, 0, high], ahead[way]),
                links.prepare(part(own, way, 3, low), near.at[way, 1, low], behind[way]),
            ]
        )
        two.append(
            [
                links.prepare(part(own, way, 1, low), near.at[way, 0, low], ahead[way]),
                links.prepare(part(own, way, 3, high), near.at[way, 1, high], behind[way]),
            ]
        )
        axis = (here.along_x, here.along_z)[turn]
        three.append(
            [
                links.prepare(mid.at[way, at[j]], near2.at[way, j - 1], axis[j])
                for j in (2, 1, 3)
            ]
        )
    ending = [
        links.prepare(late.at[m, twin], last.at[0], here.sibling),
        links.prepare(late.at[o, c], last.at[1], here.partner),
        links.prepare(late.at[o, twin], last.at[2], here.diagonal),
    ]

    def start():
        local.start()
        for key in order:
            exchange[key].start()

    def add_other(way, j):
        exchange[way, j].wait_recv()
        mine, theirs = block(own, way, j), block(other, way, j)
        for i in range(4):
            mine[i] = mine[i] + theirs[i]

    def ring_one():
        local.wait()
        for way in range(2):
            add_other(way, 2)
            one[way][0].start()
            one[way][1].start()
        for way in range(2):
            add_other(way, 1)
            one[way][2].start()
            add_other(way, 3)
            one[way][3].start()
        for way in range(2):
            add_other(way, 0)

    def ring_two():
        for way in range(2):
            one[way][0].wait_recv()
            target = part(own, way, 1, low)
            for i in range(2):
                target[i] = target[i] + far[way, 0, i]
            two[way][0].start()
            one[way][1].wait_recv()
            target = part(own, way, 3, high)
            for i in range(2):
                target[i] = target[i] + far[way, 1, i]
            two[way][1].start()

    def ring_three():
        for way in range(2):
            for copy in one[way][2:] + two[way]:
                copy.wait_recv()
            mine = block(own, way, 0)
            for i in range(4):
                mid[way, i] = (
                    mine[i].astype(F32) + near[way, 0, i].astype(F32) + near[way, 1, i].astype(F32)
                ).astype(BF)
            for copy in three[way]:
                copy.start()

    def to_owners():
        for way in range(2):
            for copy in three[way]:
                copy.wait_recv()
            total = mid[way, places(way)[0]].astype(F32)
            for j in range(3):
                total = total + near2[way, j].astype(F32)
            late[way, 0] = total[:24]
            late[way, 1] = total[24:]
        for copy in ending:
            copy.start()

    def finish():
        for copy in ending:
            copy.wait_recv()
        out[c] = late[m, c] + last[1]
        out[twin] = last[0] + last[2]
        for key in order:
            exchange[key].wait_send()
        for step in one + two + three + [ending]:
            for copy in step:
                copy.wait_send()

    return [start, ring_one, ring_two, ring_three, to_owners, finish]


def own_scratch(cols):
    return [pltpu.VMEM((4, 4, 48, cols), BF)]


def mm(a, b):
    return lax.dot_general(a, b, (((1,), (0,)), ((), ())), preferred_element_type=F32)


def mmt(a, b):
    return lax.dot_general(a, b, (((1,), (1,)), ((), ())), preferred_element_type=F32)


def tmm(a, b):
    return lax.dot_general(a, b, (((0,), (0,)), ((), ())), preferred_element_type=F32)


def normalize(values):
    centered = values - jnp.mean(values, axis=-1, keepdims=True)
    inverse = lax.rsqrt(jnp.mean(centered * centered, axis=-1, keepdims=True) + EPSILON)
    return centered * inverse, inverse


def norm_grad(upstream, normed, inverse, gain):
    scaled = upstream * gain
    return inverse * (
        scaled
        - jnp.mean(scaled, axis=-1, keepdims=True)
        - normed * jnp.mean(scaled * normed, axis=-1, keepdims=True)
    )


class Geometry:
    def __init__(self, tiles, m, places):
        starts, member = [0], jnp.zeros_like(places)
        for slot in range(SLOTS):
            side = tiles[m, slot]
            starts.append(starts[-1] + side * side)
            member = member + (places >= starts[-1]).astype(jnp.int32)
        first, side = jnp.zeros_like(places), jnp.ones_like(places)
        for slot in range(SLOTS):
            here = member == slot
            first = jnp.where(here, starts[slot], first)
            side = jnp.where(here, jnp.maximum(tiles[m, slot], 1), side)
        first = jnp.where(member == SLOTS, starts[SLOTS], first)
        offset = (places - first).astype(F32)
        side = side.astype(F32)
        self.row = jnp.floor((offset + 0.5) / side)
        self.col = offset - self.row * side
        self.member = member
        self.valid = (member < SLOTS).astype(F32)


def distances(tiles, m, dist, valid):
    down = Geometry(tiles, m, lax.broadcasted_iota(jnp.int32, (R, 1), 0))
    along = Geometry(tiles, m, lax.broadcasted_iota(jnp.int32, (1, R), 1))
    gap_r = down.row - along.row
    gap_c = down.col - along.col
    apart = jnp.sqrt(gap_r * gap_r + gap_c * gap_c)
    dist[...] = jnp.where(down.member == along.member, apart, 1e30)
    valid[...] = jnp.broadcast_to(down.valid, (R, 128))


def head_lanes():
    lane = lax.broadcasted_iota(jnp.int32, (1, 128), 1)
    first = (lane < HS).astype(F32)
    return first.astype(BF), (1.0 - first).astype(BF), first > 0.5, lane


class Heads:
    def __init__(self, q, k, v, o, dist, slopes, lse_lanes, lse_rows):
        self.q, self.k, self.v, self.o = q, k, v, o
        self.dist, self.slopes = dist, slopes
        self.lse_lanes, self.lse_rows = lse_lanes, lse_rows

    def at(self, place, i):
        ref, first = place
        return ref.at[:, lanes_at(first + i * 128, 128)]

    def forward(self, i):
        m0, m1, in_first, lane = head_lanes()
        q, k, v = self.at(self.q, i)[...], self.at(self.k, i)[...], self.at(self.v, i)[...]
        q = q * jnp.asarray(0.125, BF)
        parts = []
        lse = self.lse_lanes
        for j, keep in enumerate((m0, m1)):
            s = mmt(q * keep, k) - self.slopes[2 * i + j] * self.dist[...]
            top = jnp.max(s, axis=-1, keepdims=True)
            raised = jnp.exp(s - top)
            total = jnp.sum(raised, axis=-1, keepdims=True)
            parts.append(mm(raised.astype(BF), v) * (1.0 / total))
            lse[...] = jnp.where(lane == 2 * i + j, top + jnp.log(total), lse[...])
        self.at(self.o, i)[...] = jnp.where(in_first, parts[0], parts[1]).astype(BF)

    def backward(self, i):
        m0, m1, in_first, lane = head_lanes()
        q, k, v = self.at(self.q, i)[...], self.at(self.k, i)[...], self.at(self.v, i)[...]
        do = self.at(self.o, i)[...]
        q = q * jnp.asarray(0.125, BF)
        dqs, dks, dvs = [], [], []
        for j, keep in enumerate((m0, m1)):
            h = 2 * i + j
            s = mmt(k, q * keep) - self.slopes[h] * self.dist[...]
            p = jnp.exp(s - self.lse_rows[pl.ds(h, 1), :])
            dvs.append(mm(p.astype(BF), do))
            ds = (p * (mmt(v, do * keep) - self.inner[pl.ds(h, 1), :])).astype(BF)
            dks.append(mm(ds, q))
            dqs.append(tmm(ds, k))
        self.at(self.q, i)[...] = (jnp.where(in_first, dqs[0], dqs[1]) * 0.125).astype(BF)
        self.at(self.k, i)[...] = jnp.where(in_first, dks[0], dks[1]).astype(BF)
        self.at(self.v, i)[...] = jnp.where(in_first, dvs[0], dvs[1]).astype(BF)

    def prepare(self, merged, inner):
        ref, _ = self.o
        self.inner = inner
        head = lax.broadcasted_iota(jnp.int32, (16, D), 0)
        lane = lax.broadcasted_iota(jnp.int32, (16, D), 1)
        of_head = ((lane >= head * HS) & (lane < head * HS + HS)).astype(F32).astype(BF)
        product = ref[...].astype(F32) * merged[...].astype(F32)
        high = product.astype(BF)
        low = (product - high.astype(F32)).astype(BF)
        inner[...] = mmt(of_head, high) + mmt(of_head, low)

    def each(self, what, first, last):
        def step(i, carry):
            what(i)
            return carry

        lax.fori_loop(first, last, step, 0)

    def finish(self):
        self.lse_rows[...] = self.lse_lanes[...].T[:16]


class Staged:
    def __init__(self, buffers, sems):
        self.buffers, self.sems = buffers, sems
        self.count = buffers.shape[0]
        self.turn = 0
        self.flying = {}

    def put(self, value, targets):
        slot = self.turn % self.count
        self.turn += 1
        wait_all(self.flying.pop(slot, []))
        self.buffers[slot] = value.reshape(self.buffers.shape[1:])
        copies = []
        for i, (first, size, target) in enumerate(targets):
            copy = pltpu.make_async_copy(
                self.buffers.at[slot, :, :, :, pl.ds(first, size)], target, self.sems.at[slot, i]
            )
            copy.start()
            copies.append(copy)
        self.flying[slot] = copies

    def drain(self):
        for copies in self.flying.values():
            wait_all(copies)
        self.flying = {}


def halves(target, which, first):
    return [
        (part * HALF, HALF, target.at[which, :, :, :, pl.ds(part * D + first, HALF)]) for part in range(2)
    ]


class Vectors:
    def __init__(self, refs):
        (
            self.norm1_gain,
            self.norm1_bias,
            self.attn_bias,
            self.norm2_gain,
            self.norm2_bias,
            self.up_bias,
            self.down_bias,
            self.query_gain,
            self.query_bias,
            self.cross_bias,
        ) = list(refs[:7]) + [refs[7].at[pl.ds(i, 1)] for i in range(3)]


def column_sums(values):
    return jnp.sum(values.astype(F32), axis=0, keepdims=True)


def scaled_norm(values, gain, bias):
    normed, _ = normalize(values)
    return (normed * gain[...] + bias[...]).astype(BF)


LAYER_WEIGHTS = [
    ((4, 2, 96, 3 * D), BF),
    ((2, 2, 2, 96, D), BF),
    ((4, 2, 96, FF), BF),
    ((2, 2, 4, 2, 96, D), BF),
]
CROSS_WEIGHTS = [((4, 2, 96, D), BF), ((4, 2, 96, 2 * D), BF), ((2, 2, 2, 96, D), BF)]
CHUNKED = [
    ((4, 4, 48, 3 * D), BF),
    ((2, 2, 2, 96, D), BF),
    ((4, 4, 48, FF), BF),
    ((2, 2, 4, 2, 96, D), BF),
]
SAVED = [((R, 3 * D), BF), ((R, D), BF), ((16, R), F32), ((R, D), F32), ((R, FF), BF), ((R, FF), BF)]
EXTRA = [((R, D), BF), ((R, 2 * D), BF), ((R, D), BF), ((16, R), F32), ((R, D), F32)]
WORK = [
    ((R, D), BF),
    ((R, 128), F32),
    ((R, D), F32),
    ((D, R), BF),
    ((D, R), BF),
    ((R, R), F32),
    ((R, 128), F32),
    ((16, R), F32),
]


def flat(ref, lanes=None):
    value = ref[...] if lanes is None else ref[..., lanes]
    return value.reshape(-1, value.shape[-1])


def down_chunk(wdn, j):
    return flat(wdn.at[j // 2, j % 2])


def column_chunks():
    return [pl.ds(j * D, D) for j in range(4)]


def hidden_units(u):
    phi = 0.5 * (1.0 + lax.erf(u * 0.7071067811865476))
    return u * phi, phi + u * jnp.exp(-0.5 * u * u) * 0.3989422804014327


def forward_kernel(*refs):
    here = Place()
    tiles, slopes, radar, optical, cotangent = refs[:5]
    vecs = Vectors(refs[5:13])
    qkv_own, attn_own, up_own, down_own, cq_own, kv_own, cw_own = refs[13:20]
    refs = refs[20:]
    gathered, arrived = refs[:2]
    saved_out, refs = refs[2:8], refs[8:]
    gff, gat, gcr, vec_out, joined_own, back_own, joined_all, back_all = refs[:8]
    refs = refs[8:]
    wqkv, wo, wup, wdn, wcq, wkv, wcw = refs[:7]
    saved, refs = refs[7:13], refs[13:]
    qkv, o, lse_rows, x1, g, gp = saved
    query, pairs, merged, lse_cross, x2 = refs[:5]
    a, lse_lanes, acc, et, at, dist, valid, inner = refs[5:13]
    xin, ctx, cot, e1, e2, out_bf, staging = refs[13:20]
    link_send, link_recv, near_send, near_recv, load_sems, save_sems, stage_sems = refs[20:]
    m, oth = here.m, here.o
    first, second = pl.when(here.first), pl.when(here.second)

    peers = here.along_x[1:] + here.along_z[1:] + [here.sibling, here.partner, here.section]
    here.signal(peers)
    loads = Loads(load_sems)
    heads = Heads((qkv, 0), (qkv, D), (qkv, 2 * D), (o, 0), dist, slopes, lse_lanes, lse_rows)
    cross = Heads(
        (query, 0), (pairs, 0), (pairs, D), (merged, 0), dist, slopes, lse_lanes, lse_cross
    )
    own_qkv = loads.start(
        *[(qkv_own.at[j], wqkv.at[:, :, :, lanes_at(j * D + m * HALF, HALF)]) for j in range(3)]
    )
    own_rest = loads.start(
        (attn_own, wo.at[m]),
        (up_own, wup.at[:, :, :, lanes_at(m * HIDDEN, HIDDEN)]),
        (down_own, wdn.at[m]),
    )
    token_loads = loads.start((optical.at[m], ctx), (cotangent.at[m], cot))
    cross_own = loads.start(
        (cq_own, wcq.at[:, :, :, lanes_at(m * HALF, HALF)]), (cw_own, wcw.at[m])
    )

    i = here.dp
    links = Links(link_send, link_recv)
    block, within = i // 8, (lax.rem(i // 2, 4), lax.rem(i, 2))
    tail_lanes = lanes_at(lax.rem(i // 4, 2) * HALF, HALF)
    tail = (lax.rem(i // 2, 2), within[1], slice(None), tail_lanes)
    part = lax.rem(block, 3)
    kv_part = lax.rem(block + 1, 2)

    @second
    def _():
        for j in range(2):
            wkv[:, :, :, lanes_at(j * D + m * HALF, HALF)] = kv_own[:, j, :].reshape(4, 2, 96, HALF)

    in_head, in_query = i < 24, i < 8
    in_tail, in_pairs = i >= 24, jnp.logical_and(i >= 8, i < 24)
    kv_lanes = lanes_at(kv_part * D + m * HALF, HALF)
    rest = slice(None)
    down_piece = (lax.rem(block, 2),) + within + (rest, lanes_at((i // 16) * HALF, HALF))
    gathers = [
        Gather(here, links, gathered, g, sources)
        for g, sources in enumerate(
            [
                [(in_head, qkv_own.at[(part,) + within]), (in_tail, attn_own.at[tail])],
                [(None, up_own.at[within + (rest, lanes_at(block * HALF, HALF))])],
                [(None, down_own.at[down_piece])],
                [
                    (in_query, cq_own.at[within]),
                    (in_pairs, wkv.at[within + (rest, kv_lanes)]),
                    (in_tail, cw_own.at[tail]),
                ],
            ]
        )
    ]
    distances(tiles, m, dist, valid)

    def project(j, part):
        lanes = lanes_at(j * D + part * HALF, HALF)
        qkv[:, lanes] = mm(a[...], flat(wqkv, lanes)).astype(BF)

    @first
    def _():
        lse_lanes[...] = jnp.zeros_like(lse_lanes)
        copy = pltpu.make_async_copy(radar.at[m], xin, save_sems.at[6])
        copy.start()
        copy.wait()
        x = xin[...].astype(F32) * valid[:, :1]
        a[...] = scaled_norm(x, vecs.norm1_gain, vecs.norm1_bias)
        wait_all(own_qkv)
        for j in range(3):
            project(j, m)

    here.await_all(peers)
    for gather in gathers[:3]:
        gather.begin()

    @second
    def _():
        wait_all(cross_own)
        gathers[3].begin()

    def stage(i):
        for gather in gathers[:3]:
            gather.stage(i)
        second(lambda: gathers[3].stage(i))

    for j in range(3):
        first(lambda: heads.forward(m * 3 + j))
        stage(j + 1)
    stage(4)
    gathers[0].stage(5)
    other_one = loads.start(
        *[
            (gathered.at[0, j], wqkv.at[:, :, :, lanes_at(j * D + oth * HALF, HALF)])
            for j in range(3)
        ],
        *[
            (gathered.at[0, 3, pl.ds(2 * j, 2)], wo.at[oth, :, :, :, pl.ds(j * HALF, HALF)])
            for j in range(2)
        ],
    )

    @first
    def _():
        wait_all(other_one[:3])
        for j in range(3):
            project(j, oth)

    gathers[1].stage(5)
    gathers[2].stage(5)
    other_up = loads.start(
        *[
            (gathered.at[1, j], wup.at[:, :, :, lanes_at(oth * HIDDEN + j * HALF, HALF)])
            for j in range(4)
        ]
    )
    other_down = loads.start(
        *[
            (
                gathered.at[2, pl.ds(2 * j, 2)],
                wdn.at[oth, :, :, :, :, pl.ds(j * HALF, HALF)],
            )
            for j in range(2)
        ]
    )

    def feed_forward(source, rows):
        a[rows] = scaled_norm(source[rows], vecs.norm2_gain, vecs.norm2_bias)
        for j, lanes in enumerate(column_chunks()):
            u = mm(a[rows], flat(wup, lanes)) + vecs.up_bias[:, lanes]
            unit, slope = hidden_units(u)
            g[rows, lanes] = unit.astype(BF)
            gp[rows, lanes] = slope.astype(BF)
            term = mm(g[rows, lanes], down_chunk(wdn, j))
            acc[rows] = term if j == 0 else acc[rows] + term

    near = (near_send, near_recv)
    blocks = [pl.ds(0, R // 2), pl.ds(R // 2, R // 2)]
    forth = [remote(out_bf.at[b], xin.at[b], near, i, here.section) for i, b in enumerate(blocks)]
    back = [
        remote(out_bf.at[b], arrived.at[b], near, 2 + i, here.section)
        for i, b in enumerate(blocks)
    ]

    @first
    def _():
        heads.each(heads.forward, oth * 3, oth * 3 + 3)
        heads.finish()
        saves = [
            pltpu.make_async_copy(source, target, save_sems.at[i])
            for i, (source, target) in enumerate(zip(saved, saved_out))
        ]
        for copy in saves[:3]:
            copy.start()
        wait_all(own_rest)
        wait_all(other_one[3:])
        x = xin[...].astype(F32) * valid[:, :1]
        x1[...] = x + mm(o[...], flat(wo)) + vecs.attn_bias[...]
        saves[3].start()
        wait_all(other_up)
        wait_all(other_down)
        for rows, copy in zip(blocks, forth):
            feed_forward(x1, rows)
            out_bf[rows] = (x1[rows] + acc[rows] + vecs.down_bias[...]).astype(BF)
            copy.start()
        for copy in saves[4:]:
            copy.start()
        wait_all(saves)
        wait_all(token_loads)
        wait_all(cross_own)
        for copy in forth:
            copy.wait_send()
        for copy in back:
            copy.wait_recv()

    @second
    def _():
        gathers[3].stage(5)
        pairs_cross = [(gathered.at[3, 0], wcq.at[:, :, :, lanes_at(oth * HALF, HALF)])]
        for j in range(2):
            pairs_cross += [
                (gathered.at[3, j + 1], wkv.at[:, :, :, lanes_at(j * D + oth * HALF, HALF)]),
                (
                    gathered.at[3, 3, pl.ds(2 * j, 2)],
                    wcw.at[oth, :, :, :, pl.ds(j * HALF, HALF)],
                ),
            ]
        other_cross = loads.start(*pairs_cross)
        for copies in (own_qkv, own_rest, other_one, other_up, other_down):
            wait_all(copies)
        wait_all(token_loads)
        wait_all(other_cross)
        keep = valid[:, :1]
        ctx[...] = (ctx[...].astype(F32) * keep).astype(BF)
        cot[...] = (cot[...].astype(F32) * keep).astype(BF)
        for j in range(2):
            lanes = pl.ds(j * D, D)
            pairs[:, lanes] = mm(ctx[...], flat(wkv, lanes)).astype(BF)
        lse_lanes[...] = jnp.zeros_like(lse_lanes)
        for copy in forth:
            copy.wait_recv()
        a[...] = scaled_norm(xin[...].astype(F32), vecs.norm1_gain, vecs.norm1_bias)
        for j in range(3):
            lanes = pl.ds(j * D, D)
            qkv[:, lanes] = mm(a[...], flat(wqkv, lanes)).astype(BF)
        heads.each(heads.forward, 0, H // 2)
        heads.finish()
        x1[...] = xin[...].astype(F32) + mm(o[...], flat(wo)) + vecs.attn_bias[...]
        a[...] = scaled_norm(x1[...], vecs.query_gain, vecs.query_bias)
        query[...] = mm(a[...], flat(wcq)).astype(BF)
        cross.each(cross.forward, 0, H // 2)
        cross.finish()
        x2[...] = x1[...] + mm(merged[...], flat(wcw)) + vecs.cross_bias[...]
        feed_forward(x2, pl.ds(0, R))
        acc[...] = (x2[...] + acc[...] + vecs.down_bias[...]) * keep
        joined_own[...] = acc[rows_at(m * (R // 2), R // 2), pl.ds(HALF, HALF)]
        joined_all[...] = acc[...].astype(BF)

        for j, lanes in enumerate(column_chunks()):
            gp[:, lanes] = (mmt(cot[...], down_chunk(wdn, j)) * gp[:, lanes].astype(F32)).astype(BF)
            term = mmt(gp[:, lanes], flat(wup, lanes))
            acc[...] = term if j == 0 else acc[...] + term
        vec_out[...] = jnp.zeros_like(vec_out)
        dm = acc[...]
        normed, inverse = normalize(x2[...])
        vec_out[3:4, :] = column_sums(dm * normed)
        vec_out[4:5, :] = column_sums(dm)
        acc[...] = cot[...].astype(F32) + norm_grad(dm, normed, inverse, vecs.norm2_gain[...])
        e2[...] = acc[...].astype(BF)
        a[...] = mmt(e2[...], flat(wcw)).astype(BF)
        cross_back = Heads(
            (query, 0), (pairs, 0), (pairs, D), (a, 0), dist, slopes, lse_lanes, lse_cross
        )
        cross_back.prepare(merged, inner)
        cross_back.each(cross_back.backward, 0, H // 2)
        dc = mmt(query[...], flat(wcq))
        normed, inverse = normalize(x1[...])
        vec_out[10:11, :] = column_sums(dc * normed)
        vec_out[11:12, :] = column_sums(dc)
        acc[...] = acc[...] + norm_grad(dc, normed, inverse, vecs.query_gain[...])
        e1[...] = acc[...].astype(BF)
        a[...] = mmt(e1[...], flat(wo)).astype(BF)
        self_back = Heads(
            (qkv, 0), (qkv, D), (qkv, 2 * D), (a, 0), dist, slopes, lse_lanes, lse_rows
        )
        self_back.prepare(o, inner)
        self_back.each(self_back.backward, 0, H // 2)
        sums = []
        for rows, copy in zip(blocks, back):
            da = mmt(qkv[rows], flat(wqkv))
            normed, inverse = normalize(xin[rows].astype(F32))
            sums.append((column_sums(da * normed), column_sums(da)))
            out_bf[rows] = (
                acc[rows] + norm_grad(da, normed, inverse, vecs.norm1_gain[...])
            ).astype(BF)
            copy.start()
        vec_out[0:1, :] = sums[0][0] + sums[1][0]
        vec_out[1:2, :] = sums[0][1] + sums[1][1]

        staged = Staged(staging, stage_sems)
        acc[...] = mmt(pairs[...], flat(wkv)) * keep
        back_own[...] = acc[rows_at(m * (R // 2), R // 2), pl.ds(HALF, HALF)]
        back_all[...] = acc[...].astype(BF)
        permute = chunk_order()
        et[...] = mmt(permute, e2[...]).astype(BF)
        staged.put(mm(et[...], merged[...]).astype(BF), halves(gcr, 1, HALF))
        a[...] = scaled_norm(x1[...], vecs.query_gain, vecs.query_bias)
        et[...] = mmt(permute, a[...]).astype(BF)
        staged.put(mm(et[...], query[...]).astype(BF), halves(gcr, 0, 0))
        et[...] = mmt(permute, ctx[...]).astype(BF)
        for j, target in enumerate([(0, HALF), (1, 0)]):
            staged.put(mm(et[...], pairs[:, pl.ds(j * D, D)]).astype(BF), halves(gcr, *target))
        et[...] = cot[...].T
        a[...] = scaled_norm(x2[...], vecs.norm2_gain, vecs.norm2_bias)
        at[...] = a[...].T
        for j, lanes in enumerate(column_chunks()):
            vec_out[6 + j : 7 + j, :] = column_sums(gp[:, lanes])
            staged.put(mm(et[...], g[:, lanes]).astype(BF), [(0, D, gff.at[1, :, :, :, lanes])])
            staged.put(mm(at[...], gp[:, lanes]).astype(BF), [(0, D, gff.at[0, :, :, :, lanes])])
        vec_out[2:3, :] = column_sums(e1[...])
        vec_out[5:6, :] = column_sums(cot[...])
        vec_out[12:13, :] = column_sums(e2[...])
        et[...] = e1[...].T
        staged.put(mm(et[...], o[...]).astype(BF), halves(gat, 1, HALF))
        a[...] = scaled_norm(xin[...].astype(F32), vecs.norm1_gain, vecs.norm1_bias)
        at[...] = a[...].T
        for j, target in enumerate([(0, 0), (0, HALF), (1, 0)]):
            staged.put(mm(at[...], qkv[:, pl.ds(j * D, D)]).astype(BF), halves(gat, *target))
        staged.drain()
        for copy in back:
            copy.wait_send()
        gathers[3].drain()

    for gather in gathers[:3]:
        gather.drain()


def chunk_order():
    r = lax.broadcasted_iota(jnp.int32, (D, 1), 0).astype(F32)
    chunk = jnp.floor((r + 0.5) / 48.0)
    inner = r - chunk * 48.0
    core = (inner >= 24.0).astype(F32)
    inner = inner - 24.0 * core
    section = (inner >= 12.0).astype(F32)
    source = 384.0 * section + 24.0 * chunk + 12.0 * core + inner - 12.0 * section
    columns = lax.broadcasted_iota(jnp.int32, (D, D), 1).astype(F32)
    return (columns == source).astype(F32).astype(BF)


def forward(tiles, slopes, tokens, vecs, own):
    scratch = vmem(
        LAYER_WEIGHTS + CROSS_WEIGHTS + SAVED + EXTRA + WORK + [((R, D), BF)] * 6 + [((2, 4, 4, 48, D), BF)]
    )
    quarter = shape((R // 2, HALF), F32)
    return pl.pallas_call(
        forward_kernel,
        out_shape=[shape((4, 4, 4, 2, 96, HALF), BF), shape((R, D), BF)]
        + [shape(*s) for s in SAVED]
        + [shape((2, 4, 4, 48, n), BF) for n in (FF, 2 * D, 2 * D)]
        + [shape((16, D), F32), quarter, quarter, shape((R, D), BF), shape((R, D), BF)],
        in_specs=[SM, SM] + [ANY] * 3 + [VM] * 8 + [ANY] * 5 + [VM] + [ANY],
        out_specs=[ANY] * 11 + [VM] * 5,
        scratch_shapes=scratch
        + [dma(92), dma(92), dma(4), dma(4), dma(40), dma(7), pltpu.SemaphoreType.DMA((2, 2))],
        compiler_params=pltpu.CompilerParams(
            collective_id=0, has_side_effects=True, vmem_limit_bytes=BIG
        ),
    )(tiles, slopes, *tokens, *vecs, *own)


def backward_kernel(*refs):
    here = Place()
    tiles, slopes, radar, dy_in = refs[:4]
    vecs = Vectors(refs[4:12])
    qkv_own, attn_own, up_own, down_own, gathered, gathered48 = refs[12:18]
    saved_in, refs = refs[18:24], refs[24:]
    vec_in, joined_all, back_all, gcr = refs[:4]
    refs = refs[6:]
    gff, gat, off, oat, ocr, vec_total, vec_other, radar_own, quarters, ocr_other = refs[:10]
    refs = refs[10:]
    wqkv, wo, wup, wdn = refs[:4]
    saved, refs = refs[4:10], refs[10:]
    qkv, o, lse_rows, x1, g, gp = saved
    a, lse_lanes, acc, et, at, dist, valid, inner = refs[:8]
    xin, out_bf, staging, vec, vbuf = refs[8:13]
    own_at, cross_sums = refs[13:15]
    ff_buffers, at_buffers, cross_buffers, refs = refs[15:22], refs[22:29], refs[29:36], refs[36:]
    link_send, link_recv, far_send, far_recv, load_sems, local_sems, stage_sems = refs
    m, oth = here.m, here.o
    first, second = pl.when(here.first), pl.when(here.second)
    peers = here.ring + [
        here.sibling,
        here.partner,
        here.diagonal,
        here.along_x[2],
        here.along_z[2],
        here.section,
        here.crossed,
    ]
    here.signal(peers)
    loads = Loads(load_sems)
    links = Links(link_send, link_recv)
    far = (far_send, far_recv)
    staged = Staged(staging, stage_sems)
    heads = Heads((qkv, 0), (qkv, D), (qkv, 2 * D), (a, 0), dist, slopes, lse_lanes, lse_rows)
    chunks = column_chunks()

    @first
    def _():
        cotangent = loads.start((dy_in, out_bf))
        copies = loads.start(
            (down_own, wdn.at[m]),
            *[
                (gathered.at[2, pl.ds(2 * j, 2)], wdn.at[oth, :, :, :, :, pl.ds(j * HALF, HALF)])
                for j in range(2)
            ],
        )
        units = [
            loads.start((saved_in[5].at[:, c], gp.at[:, c]), (saved_in[4].at[:, c], g.at[j]))
            for j, c in enumerate(chunks[:2])
        ]
        early = loads.start((saved_in[3], x1), (radar.at[m], xin))
        copies_up = loads.start(
            (up_own, wup.at[:, :, :, lanes_at(m * HIDDEN, HIDDEN)]),
            *[
                (gathered48.at[1, j], wup.at[:, :, :, lanes_at(oth * HIDDEN + j * HALF, HALF)])
                for j in range(4)
            ],
        )
        units += [loads.start((saved_in[5].at[:, c], gp.at[:, c])) for c in chunks[2:]]
        late = loads.start(
            (saved_in[0], qkv),
            (saved_in[1], o),
            (saved_in[2], lse_rows),
            (attn_own, wo.at[m]),
            *[
                (gathered.at[0, 3, pl.ds(2 * j, 2)], wo.at[oth, :, :, :, pl.ds(j * HALF, HALF)])
                for j in range(2)
            ],
            *[
                (qkv_own.at[j], wqkv.at[:, :, :, lanes_at(j * D + m * HALF, HALF)])
                for j in range(3)
            ],
            *[
                (gathered48.at[0, j], wqkv.at[:, :, :, lanes_at(j * D + oth * HALF, HALF)])
                for j in range(3)
            ],
        )
        distances(tiles, m, dist, valid)
        vec[...] = jnp.zeros_like(vec)
        wait_all(cotangent)
        e3 = out_bf[...]
        vec[5:6, :] = column_sums(e3)
        et[...] = e3.T
        wait_all(early)
        a[...] = scaled_norm(x1[...], vecs.norm2_gain, vecs.norm2_bias)
        at[...] = a[...].T
        wait_all(copies)
        for j, lanes in enumerate(chunks):
            wait_all(units[j])
            du = (mmt(out_bf[...], down_chunk(wdn, j)) * gp[:, lanes].astype(F32)).astype(BF)
            gp[:, lanes] = du
            vec[6 + j : 7 + j, :] = column_sums(du)
            staged.put(mm(et[...], g[j % 2]).astype(BF), [(0, D, gff.at[1, :, :, :, lanes])])
            staged.put(mm(at[...], gp[:, lanes]).astype(BF), [(0, D, gff.at[0, :, :, :, lanes])])
            if j < 2:
                units[j + 2] += loads.start((saved_in[4].at[:, chunks[j + 2]], g.at[j]))
            if j == 0:
                wait_all(copies_up)
            term = mmt(gp[:, lanes], flat(wup, lanes))
            acc[...] = term if j == 0 else acc[...] + term
        wait_all(late)
        staged.drain()

    @second
    def _():
        vec[...] = vec_in[...]

    here.await_all(peers)
    ff = scatter_stages(here, links, local_sems.at[0], gff, off, wup, ff_buffers)
    mid = scatter_stages(here, links, local_sems.at[1], gat, oat, own_at, at_buffers)
    vec_steps = vector_stages(here, links, vec, vbuf, vec_total)
    own_cross = wqkv.at[:, :, :, pl.ds(0, 2 * D)]
    cross = scatter_stages(
        here, links, local_sems.at[2], gcr, cross_sums, own_cross, cross_buffers
    )

    def quarter_copies(source, kind):
        half_rows = R // 2
        mine, others = rows_at(m * half_rows, half_rows), rows_at(oth * half_rows, half_rows)
        sender, receiver = (0, 1) if kind == 2 else (1, 0)
        same = pl.ds(sender * HALF, HALF)
        over = pl.ds(receiver * HALF, HALF)
        return [
            remote(source.at[mine, over], quarters.at[kind, 0], far, 3 * kind, here.section),
            remote(source.at[others, over], quarters.at[kind, 1], far, 3 * kind + 1, here.crossed),
            remote(source.at[others, same], quarters.at[kind, 1], far, 3 * kind + 2, here.partner),
        ]

    sent = [quarter_copies(s, i) for i, s in enumerate((joined_all, back_all, out_bf))]
    cross_sent = remote(ocr.at[0], ocr_other, far, 9, here.section)
    vec_sent = remote(vec_total, vec_other, far, 10, here.section)

    @second
    def _():
        for copies in sent[:2]:
            for copy in copies:
                copy.start()
        cross[0]()

    ff[0]()
    second(cross[1])

    @first
    def _():
        dm = acc[...]
        normed, inverse = normalize(x1[...])
        vec[3:4, :] = column_sums(dm * normed)
        vec[4:5, :] = column_sums(dm)
        acc[...] = out_bf[...].astype(F32) + norm_grad(dm, normed, inverse, vecs.norm2_gain[...])
        e1 = acc[...].astype(BF)
        vec[2:3, :] = column_sums(e1)
        out_bf[...] = e1
        a[...] = mmt(out_bf[...], flat(wo)).astype(BF)
        heads.prepare(o, inner)

    ff[1]()

    @first
    def _():
        et[...] = out_bf[...].T
        staged.put(mm(et[...], o[...]).astype(BF), halves(gat, 1, HALF))
        heads.each(heads.backward, 0, 2)
        staged.drain()

    second(cross[2])
    ff[2]()
    second(cross[3])
    first(lambda: heads.each(heads.backward, 2, 4))
    ff[3]()
    second(cross[4])
    first(lambda: heads.each(heads.backward, 4, 6))
    ff[4]()
    second(cross[5])

    @first
    def _():
        x = xin[...].astype(F32) * valid[:, :1]
        a[...] = scaled_norm(x, vecs.norm1_gain, vecs.norm1_bias)
        at[...] = a[...].T
        for j, target in enumerate([(0, 0), (0, HALF), (1, 0)]):
            staged.put(mm(at[...], qkv[:, pl.ds(j * D, D)]).astype(BF), halves(gat, *target))
        staged.drain()

    mid[0]()

    @first
    def _():
        da = mmt(qkv[...], flat(wqkv))
        normed, inverse = normalize(xin[...].astype(F32) * valid[:, :1])
        vec[0:1, :] = column_sums(da * normed)
        vec[1:2, :] = column_sums(da)
        acc[...] = (acc[...] + norm_grad(da, normed, inverse, vecs.norm1_gain[...])) * valid[:, :1]
        radar_own[...] = acc[rows_at(m * (R // 2), R // 2), pl.ds(0, HALF)]
        out_bf[...] = acc[...].astype(BF)
        for copy in sent[2]:
            copy.start()

    @second
    def _():
        for section in range(2):
            for which in range(2):
                ocr[section, which] = cross_sums[which][section * 12 : section * 12 + 12]
        cross_sent.start()

    vec_steps[0]()
    mid[1]()
    vec_steps[1]()
    ff[5]()
    mid[2]()
    vec_steps[2]()
    mid[3]()
    vec_steps[3]()
    mid[4]()
    vec_steps[4]()

    @second
    def _():
        vec_sent.start()

    mid[5]()

    @first
    def _():
        for copies in sent[:2]:
            copies[0].wait_recv()
            copies[1].wait_recv()
        sent[2][2].wait_recv()
        for copy in sent[2]:
            copy.wait_send()
        cross_sent.wait_recv()
        vec_sent.wait_recv()

    @second
    def _():
        sent[2][0].wait_recv()
        sent[2][1].wait_recv()
        for copies in sent[:2]:
            copies[2].wait_recv()
            for copy in copies:
                copy.wait_send()
        cross_sent.wait_send()
        vec_sent.wait_send()


def backward(tiles, slopes, radar, dy, vecs, own, gathered, saved, vec, quarters, gcr, gff, gat):
    scratch = vmem(
        CHUNKED
        + SAVED[:4]
        + [((2, R, D), BF)]
        + SAVED[5:]
        + WORK
        + [((R, D), BF)] * 2
        + [((2, 4, 4, 48, D), BF), ((16, D), F32), ((8, 16, D), F32)]
    )
    vector = shape((16, D), F32)
    qkv, attn, up, down = own
    return pl.pallas_call(
        backward_kernel,
        out_shape=[
            shape(gff.shape, BF),
            shape(gat.shape, BF),
            shape((2, 24, HIDDEN), F32),
            shape((2, 24, D), F32),
            shape((2, 2, 12, D), F32),
            vector,
            vector,
            shape((R // 2, HALF), F32),
            shape((3, 2, R // 2, HALF), BF),
            shape((2, 12, D), F32),
        ],
        in_specs=[SM, SM, ANY, ANY] + [VM] * 8 + [ANY] * 6 + [ANY] * 6 + [VM] + [ANY] * 5,
        out_specs=[ANY, ANY] + [VM] * 6 + [ANY, VM],
        input_output_aliases={28: 0, 29: 1},
        scratch_shapes=scratch
        + own_scratch(2 * D)
        + [pltpu.VMEM((2, 24, D), F32)]
        + scatter_scratch(FF)
        + scatter_scratch(2 * D)
        + scatter_scratch(2 * D)
        + [dma(112), dma(112), dma(11), dma(11), dma(40), dma(3), pltpu.SemaphoreType.DMA((2, 2))],
        compiler_params=pltpu.CompilerParams(
            collective_id=1, has_side_effects=True, vmem_limit_bytes=BIG
        ),
    )(
        tiles,
        slopes,
        radar,
        dy,
        *vecs,
        qkv.reshape(3, 4, 4, 48, HALF),
        attn,
        up.reshape(4, 4, 48, HIDDEN),
        down,
        gathered,
        gathered.reshape(4, 4, 4, 4, 48, HALF),
        *saved,
        vec,
        *quarters,
        gcr,
        gff,
        gat,
    )


def local(
    radar_tokens,
    optical_tokens,
    out_cotangent,
    tile_sides,
    norm1_gain,
    norm1_bias,
    qkv_weight,
    attn_weight,
    attn_bias,
    norm2_gain,
    norm2_bias,
    up_weight,
    up_bias,
    down_weight,
    down_bias,
    query_gain,
    query_bias,
    cross_query,
    cross_keyval,
    cross_weight,
    cross_bias,
):
    m = lax.axis_index("mp")
    joining = lax.axis_index("pipe") == 1
    slopes = jnp.exp2(-8.0 * (jnp.arange(H, dtype=jnp.int32) + 1).astype(F32) / H)
    vecs = (
        norm1_gain,
        norm1_bias,
        attn_bias,
        norm2_gain,
        norm2_bias,
        up_bias,
        down_bias,
        jnp.stack([query_gain, query_bias, cross_bias]),
    )
    own = (
        qkv_weight[0].transpose(1, 0, 2).reshape(3, 4, 2, 96, HALF),
        attn_weight.reshape(2, 2, 96, D),
        up_weight.reshape(4, 2, 96, HIDDEN),
        down_weight.reshape(2, 4, 2, 96, D),
    )
    cross_own = (
        cross_query.reshape(4, 2, 96, HALF),
        cross_keyval,
        cross_weight.reshape(2, 2, 96, D),
    )
    tokens = (radar_tokens, optical_tokens, out_cotangent)
    results = forward(
        tile_sides, slopes, tokens, vecs, own + cross_own
    )
    gathered, dy0 = results[:2]
    saved = results[2:8]
    gff, gat, gcr, vec, joined_own, back_own, joined_all, back_all = results[8:]
    outs = backward(
        tile_sides,
        slopes,
        radar_tokens,
        dy0,
        vecs,
        own,
        gathered,
        saved,
        vec,
        (joined_all, back_all),
        gcr,
        gff,
        gat,
    )
    _, _, off, oat, ocr, vec, vec_other, radar_own, quarters, ocr_other = outs

    def placed(own_quarter, kind, here):
        mine = jnp.where(here, own_quarter, quarters[kind, 0].astype(F32))
        others = quarters[kind, 1].astype(F32)
        swap = m == 1
        return jnp.stack([jnp.where(swap, others, mine), jnp.where(swap, mine, others)])

    crossed = jnp.where(joining, vec[10:13], vec_other[10:13])
    ocr = jnp.where(joining, ocr[1], ocr_other)
    q, k = oat[0, :, :HALF], oat[0, :, HALF:]
    v, attn = oat[1, :, :HALF], oat[1, :, HALF:]
    cq, ck = ocr[0, :, :HALF], ocr[0, :, HALF:]
    cv, cw = ocr[1, :, :HALF], ocr[1, :, HALF:]
    return (
        placed(joined_own, 0, joining),
        placed(radar_own, 2, jnp.logical_not(joining)),
        placed(back_own, 1, joining),
        vec[0:1],
        vec[1:2],
        jnp.stack([q, k, v], axis=1)[None],
        attn.T[None],
        vec[2:3],
        vec[3:4],
        vec[4:5],
        off[0][None],
        vec[6:10].reshape(1, FF),
        off[1].T[None],
        vec[5:6],
        crossed[0],
        crossed[1],
        cq,
        jnp.stack([ck, cv], axis=1),
        cw.T,
        crossed[2],
    )


def solution(mesh):
    in_specs = (
        P(None, "dp", None),
        P(None, "dp", None),
        P(None, "dp", None),
        P(None, "dp"),
        P("pipe", None),
        P("pipe", None),
        P("pipe", None, None, "mp"),
        P("pipe", "mp", None),
        P("pipe", None),
        P("pipe", None),
        P("pipe", None),
        P("pipe", None, "mp"),
        P("pipe", None),
        P("pipe", "mp", None),
        P("pipe", None),
        P(),
        P(),
        P(None, "mp"),
        P(None, None, "mp"),
        P("mp", None),
        P(),
    )
    out_specs = (
        P(None, ("dp", "mp"), "pipe"),
        P(None, ("dp", "mp"), "pipe"),
        P(None, ("dp", "mp"), "pipe"),
        P("pipe", None),
        P("pipe", None),
        P("pipe", "dp", None, "mp"),
        P("pipe", "mp", "dp"),
        P("pipe", None),
        P("pipe", None),
        P("pipe", None),
        P("pipe", "dp", "mp"),
        P("pipe", None),
        P("pipe", "mp", "dp"),
        P("pipe", None),
        P(),
        P(),
        P(("pipe", "dp"), "mp"),
        P(("pipe", "dp"), None, "mp"),
        P("mp", ("pipe", "dp")),
        P(),
    )
    return jax.shard_map(local, mesh=mesh, in_specs=in_specs, out_specs=out_specs, check_vma=False)
```

```python
import jax
import jax.numpy as jnp
from jax import lax
from jax.experimental import pallas as pl
from jax.experimental.pallas import tpu as pltpu
from jax.sharding import PartitionSpec as P

H = 12
HS = 64
D = 768
FF = 3072
R = 512
HALF = D // 2
HIDDEN = FF // 2
SLOTS = 3
EPSILON = 1e-05
BF = jnp.bfloat16
F32 = jnp.float32
ANY = pl.BlockSpec(memory_space=pl.ANY)
VM = pl.BlockSpec(memory_space=pltpu.VMEM)
SM = pl.BlockSpec(memory_space=pltpu.SMEM)
MESH = pl.DeviceIdType.MESH
BIG = 62 * 1024 * 1024


def shape(dims, kind):
    return jax.ShapeDtypeStruct(dims, kind)


def vmem(shapes):
    return [pltpu.VMEM(dims, kind) for dims, kind in shapes]


def dma(count):
    return pltpu.SemaphoreType.DMA((count,))


class Place:
    def __init__(self):
        dp = lax.axis_index("dp")
        self.dp = dp
        self.pipe = lax.axis_index("pipe")
        self.m = lax.axis_index("mp")
        self.o = 1 - self.m
        self.core = lax.rem(dp, 2)
        self.twin = 1 - self.core
        chip = dp // 2
        self.x = lax.rem(chip, 4)
        self.z = chip // 4
        self.xs = [self.x] + [lax.rem(self.x + i, 4) for i in (1, 2, 3)]
        self.zs = [self.z] + [lax.rem(self.z + i, 4) for i in (1, 2, 3)]
        self.along_x = [self.at(self.z, x, self.core) for x in self.xs]
        self.along_z = [self.at(z, self.x, self.core) for z in self.zs]
        self.sibling = self.at(self.z, self.x, self.twin)
        self.partner = {"mp": self.o}
        self.section = {"pipe": 1 - self.pipe}
        self.crossed = {"pipe": 1 - self.pipe, "mp": self.o}
        self.diagonal = dict(self.sibling, mp=self.o)
        self.ring = [self.along_x[1], self.along_x[3], self.along_z[1], self.along_z[3]]
        self.first = self.pipe == 0
        self.second = self.pipe == 1

    def at(self, z, x, core):
        return {"dp": (z * 4 + x) * 2 + core}

    def signal(self, devices):
        barrier = pltpu.get_barrier_semaphore()
        for device in devices:
            pl.semaphore_signal(barrier, inc=1, device_id=device, device_id_type=MESH)

    def await_all(self, devices):
        pl.semaphore_wait(pltpu.get_barrier_semaphore(), len(devices))


def remote(source, target, sems, i, device):
    return pltpu.make_async_remote_copy(
        src_ref=source,
        dst_ref=target,
        send_sem=sems[0].at[i],
        recv_sem=sems[1].at[i],
        device_id=device,
        device_id_type=MESH,
    )


class Links:
    def __init__(self, *sems):
        self.sems = sems
        self.used = 0

    def prepare(self, source, target, device):
        copy = remote(source, target, self.sems, self.used, device)
        self.used += 1
        return copy


class Loads:
    def __init__(self, sems):
        self.sems = sems
        self.used = 0

    def prepare(self, *pairs):
        copies = []
        for source, target in pairs:
            copies.append(pltpu.make_async_copy(source, target, self.sems.at[self.used]))
            self.used += 1
        return copies

    def start(self, *pairs):
        return start_all(self.prepare(*pairs))


def start_all(copies):
    for copy in copies:
        copy.start()
    return copies


def wait_all(copies):
    for copy in copies:
        copy.wait()


def lanes_at(first, size):
    return pl.ds(pl.multiple_of(first, 128), size)


def rows_at(first, size):
    return pl.ds(pl.multiple_of(first, 16), size)


class Gather:
    def __init__(self, here, links, out, g, sources):
        c, x, z = here.core, here.x, here.z
        xs, zs = here.xs, here.zs
        right, left, up, down = here.ring
        a, b = pl.ds(0, 48), pl.ds(48, 48)
        low, high = pl.ds(0, 2), pl.ds(2, 2)
        at = links.used
        self.begins = [
            (condition, remote(source, out.at[g, z, x, c], links.sems, at, here.partner))
            for condition, source in sources
        ]
        links.used = at + 1

        def same(view, device):
            return links.prepare(view, view, device)

        direct, early = [], []
        for j in (2, 1, 3):
            direct.append(same(out.at[g, z, x, c, a], here.along_x[j]))
            direct.append(same(out.at[g, z, x, c, b], here.along_z[j]))
        for j in (0, 1, 3):
            early.append(same(out.at[g, zs[j], :, c, a], here.sibling))
            early.append(same(out.at[g, :, xs[j], c, b], here.sibling))
        near = [
            same(out.at[g, z, :, c, a], up),
            same(out.at[g, z, :, c, a], down),
            same(out.at[g, :, x, c, b], right),
            same(out.at[g, :, x, c, b], left),
        ]
        relayed = [
            same(out.at[g, zs[3], low, c, a], up),
            same(out.at[g, zs[1], high, c, a], down),
            same(out.at[g, low, xs[3], c, b], right),
            same(out.at[g, high, xs[1], c, b], left),
        ]
        late = [
            same(out.at[g, zs[2], :, c, a], here.sibling),
            same(out.at[g, :, xs[2], c, b], here.sibling),
        ]
        first = [self.begins[-1][1]]
        self.waits = [[], first, direct, near, relayed, early + late]
        self.starts = [[], direct, near, relayed + early, late, []]
        self.all = first + direct + near + relayed + early + late

    def begin(self):
        for condition, copy in self.begins:
            if condition is None:
                copy.start()
            else:
                pl.when(condition)(copy.start)

    def stage(self, i):
        for copy in self.waits[i]:
            copy.wait_recv()
        for copy in self.starts[i]:
            copy.start()

    def drain(self):
        for copy in self.all:
            copy.wait_send()


class Across:
    def __init__(self, here, links, own, out, g):
        c = here.core
        spans = [pl.ds(2 * j, 2) for j in range(2)]
        self.copies = [
            links.prepare(
                own.at[:, :, c, :, pl.ds(j * HALF, HALF)], out.at[g, span, :, c], here.partner
            )
            for j, span in enumerate(spans)
        ]
        self.shared = [
            links.prepare(out.at[g, span, :, c], out.at[g, span, :, c], here.sibling)
            for span in spans
        ]

    def begin(self):
        start_all(self.copies)

    def share(self):
        for copy, onward in zip(self.copies, self.shared):
            copy.wait_recv()
            onward.start()

    def finish(self):
        for copy in self.shared:
            copy.wait_recv()

    def drain(self):
        for copy in self.copies + self.shared:
            copy.wait_send()


def vector_stages(here, links, vec, vbuf, total):
    rounds = [[here.sibling], here.along_x[1:], here.along_z[1:], [here.partner]]
    copies, used = [], 0
    for devices in rounds:
        copies.append(
            [links.prepare(total, vbuf.at[used + i], d) for i, d in enumerate(devices)]
        )
        used += len(devices)

    def begin(i):
        def stage():
            if i == 0:
                total[...] = vec[...]
            else:
                first = sum(len(devices) for devices in rounds[: i - 1])
                for copy in copies[i - 1]:
                    copy.wait()
                value = total[...]
                for j in range(len(rounds[i - 1])):
                    value = value + vbuf[first + j]
                total[...] = value
            if i < len(rounds):
                for copy in copies[i]:
                    copy.start()

        return stage

    return [begin(i) for i in range(len(rounds) + 1)]


def scatter_scratch(cols):
    half = cols // 2
    return [
        pltpu.VMEM((4, 4, 48, cols), BF),
        pltpu.VMEM((2, 2, 2, 48, half), BF),
        pltpu.VMEM((2, 2, 4, 48, half), BF),
        pltpu.VMEM((2, 4, 48, half), BF),
        pltpu.VMEM((2, 3, 48, half), BF),
        pltpu.VMEM((2, 2, 24, half), F32),
        pltpu.VMEM((3, 24, half), F32),
    ]


def scatter_stages(here, links, local_sem, grads, out, own, buffers):
    other, far, near, mid, near2, late, last = buffers
    cols = own.shape[-1]
    half = cols // 2
    c, twin, m, o = here.core, here.twin, here.m, here.o
    xs, zs = here.xs, here.zs
    lanes = [pl.ds(0, half), pl.ds(half, half)]
    low, high = pl.ds(0, 2), pl.ds(2, 2)
    ahead = [here.along_x[1], here.along_z[1]]
    behind = [here.along_x[3], here.along_z[3]]

    def block(ref, way, j):
        if way == 0:
            return ref.at[:, xs[j], :, lanes[0]]
        return ref.at[zs[j], :, :, lanes[1]]

    def part(ref, way, j, span):
        if way == 0:
            return ref.at[span, xs[j], :, lanes[0]]
        return ref.at[zs[j], span, :, lanes[1]]

    def places(way):
        return zs if way == 0 else xs

    order = [(way, j) for j in (2, 1, 3, 0) for way in range(2)]
    local = pltpu.make_async_copy(grads.at[c], own, local_sem)
    exchange = {
        (way, j): links.prepare(
            block(grads.at[twin], way, j), block(other, way, j), here.sibling
        )
        for way, j in order
    }
    one, two, three = [], [], []
    for way in range(2):
        turn = 1 - way
        at = places(way)
        one.append(
            [
                links.prepare(part(own, way, 2, low), far.at[way, 0], ahead[way]),
                links.prepare(part(own, way, 2, high), far.at[way, 1], behind[way]),
                links.prepare(part(own, way, 1, high), near.at[way, 0, high], ahead[way]),
                links.prepare(part(own, way, 3, low), near.at[way, 1, low], behind[way]),
            ]
        )
        two.append(
            [
                links.prepare(part(own, way, 1, low), near.at[way, 0, low], ahead[way]),
                links.prepare(part(own, way, 3, high), near.at[way, 1, high], behind[way]),
            ]
        )
        axis = (here.along_x, here.along_z)[turn]
        three.append(
            [
                links.prepare(mid.at[way, at[j]], near2.at[way, j - 1], axis[j])
                for j in (2, 1, 3)
            ]
        )
    ending = [
        links.prepare(late.at[m, twin], last.at[0], here.sibling),
        links.prepare(late.at[o, c], last.at[1], here.partner),
        links.prepare(late.at[o, twin], last.at[2], here.diagonal),
    ]

    def start():
        local.start()
        for key in order:
            exchange[key].start()

    def add_other(way, j):
        exchange[way, j].wait_recv()
        mine, theirs = block(own, way, j), block(other, way, j)
        for i in range(4):
            mine[i] = mine[i] + theirs[i]

    def ring_one():
        local.wait()
        for way in range(2):
            add_other(way, 2)
            one[way][0].start()
            one[way][1].start()
        for way in range(2):
            add_other(way, 1)
            one[way][2].start()
            add_other(way, 3)
            one[way][3].start()
        for way in range(2):
            add_other(way, 0)

    def ring_two():
        for way in range(2):
            one[way][0].wait_recv()
            target = part(own, way, 1, low)
            for i in range(2):
                target[i] = target[i] + far[way, 0, i]
            two[way][0].start()
            one[way][1].wait_recv()
            target = part(own, way, 3, high)
            for i in range(2):
                target[i] = target[i] + far[way, 1, i]
            two[way][1].start()

    def ring_three():
        for way in range(2):
            for copy in one[way][2:] + two[way]:
                copy.wait_recv()
            mine = block(own, way, 0)
            for i in range(4):
                mid[way, i] = (
                    mine[i].astype(F32) + near[way, 0, i].astype(F32) + near[way, 1, i].astype(F32)
                ).astype(BF)
            for copy in three[way]:
                copy.start()

    def to_owners():
        for way in range(2):
            for copy in three[way]:
                copy.wait_recv()
            total = mid[way, places(way)[0]].astype(F32)
            for j in range(3):
                total = total + near2[way, j].astype(F32)
            late[way, 0] = total[:24]
            late[way, 1] = total[24:]
        for copy in ending:
            copy.start()

    def finish():
        for copy in ending:
            copy.wait_recv()
        out[c] = late[m, c] + last[1]
        out[twin] = last[0] + last[2]
        for key in order:
            exchange[key].wait_send()
        for step in one + two + three + [ending]:
            for copy in step:
                copy.wait_send()

    return [start, ring_one, ring_two, ring_three, to_owners, finish]


def own_scratch(cols):
    return [pltpu.VMEM((4, 4, 48, cols), BF)]


def mm(a, b):
    return lax.dot_general(a, b, (((1,), (0,)), ((), ())), preferred_element_type=F32)


def mmt(a, b):
    return lax.dot_general(a, b, (((1,), (1,)), ((), ())), preferred_element_type=F32)


def tmm(a, b):
    return lax.dot_general(a, b, (((0,), (0,)), ((), ())), preferred_element_type=F32)


def normalize(values):
    centered = values - jnp.mean(values, axis=-1, keepdims=True)
    inverse = lax.rsqrt(jnp.mean(centered * centered, axis=-1, keepdims=True) + EPSILON)
    return centered * inverse, inverse


def norm_grad(upstream, normed, inverse, gain):
    scaled = upstream * gain
    return inverse * (
        scaled
        - jnp.mean(scaled, axis=-1, keepdims=True)
        - normed * jnp.mean(scaled * normed, axis=-1, keepdims=True)
    )


class Geometry:
    def __init__(self, tiles, m, places):
        starts, member = [0], jnp.zeros_like(places)
        for slot in range(SLOTS):
            side = tiles[m, slot]
            starts.append(starts[-1] + side * side)
            member = member + (places >= starts[-1]).astype(jnp.int32)
        first, side = jnp.zeros_like(places), jnp.ones_like(places)
        for slot in range(SLOTS):
            here = member == slot
            first = jnp.where(here, starts[slot], first)
            side = jnp.where(here, jnp.maximum(tiles[m, slot], 1), side)
        first = jnp.where(member == SLOTS, starts[SLOTS], first)
        offset = (places - first).astype(F32)
        side = side.astype(F32)
        self.row = jnp.floor((offset + 0.5) / side)
        self.col = offset - self.row * side
        self.member = member
        self.valid = (member < SLOTS).astype(F32)


def distances(tiles, m, dist, valid):
    down = Geometry(tiles, m, lax.broadcasted_iota(jnp.int32, (R, 1), 0))
    along = Geometry(tiles, m, lax.broadcasted_iota(jnp.int32, (1, R), 1))
    gap_r = down.row - along.row
    gap_c = down.col - along.col
    apart = jnp.sqrt(gap_r * gap_r + gap_c * gap_c)
    dist[...] = jnp.where(down.member == along.member, apart, 1e30)
    valid[...] = jnp.broadcast_to(down.valid, (R, 128))


def head_lanes():
    lane = lax.broadcasted_iota(jnp.int32, (1, 128), 1)
    first = (lane < HS).astype(F32)
    return first.astype(BF), (1.0 - first).astype(BF), first > 0.5, lane


class Heads:
    def __init__(self, q, k, v, o, dist, slopes, lse_lanes, lse_rows):
        self.q, self.k, self.v, self.o = q, k, v, o
        self.dist, self.slopes = dist, slopes
        self.lse_lanes, self.lse_rows = lse_lanes, lse_rows

    def at(self, place, i):
        ref, first = place
        return ref.at[:, lanes_at(first + i * 128, 128)]

    def forward(self, i):
        m0, m1, in_first, lane = head_lanes()
        q, k, v = self.at(self.q, i)[...], self.at(self.k, i)[...], self.at(self.v, i)[...]
        q = q * jnp.asarray(0.125, BF)
        parts = []
        lse = self.lse_lanes
        for j, keep in enumerate((m0, m1)):
            s = mmt(q * keep, k) - self.slopes[2 * i + j] * self.dist[...]
            top = jnp.max(s, axis=-1, keepdims=True)
            raised = jnp.exp(s - top)
            total = jnp.sum(raised, axis=-1, keepdims=True)
            parts.append(mm(raised.astype(BF), v) * (1.0 / total))
            lse[...] = jnp.where(lane == 2 * i + j, top + jnp.log(total), lse[...])
        self.at(self.o, i)[...] = jnp.where(in_first, parts[0], parts[1]).astype(BF)

    def backward(self, i):
        m0, m1, in_first, lane = head_lanes()
        q, k, v = self.at(self.q, i)[...], self.at(self.k, i)[...], self.at(self.v, i)[...]
        do = self.at(self.o, i)[...]
        q = q * jnp.asarray(0.125, BF)
        dqs, dks, dvs = [], [], []
        for j, keep in enumerate((m0, m1)):
            h = 2 * i + j
            s = mmt(k, q * keep) - self.slopes[h] * self.dist[...]
            p = jnp.exp(s - self.lse_rows[pl.ds(h, 1), :])
            dvs.append(mm(p.astype(BF), do))
            ds = (p * (mmt(v, do * keep) - self.inner[pl.ds(h, 1), :])).astype(BF)
            dks.append(mm(ds, q))
            dqs.append(tmm(ds, k))
        self.at(self.q, i)[...] = (jnp.where(in_first, dqs[0], dqs[1]) * 0.125).astype(BF)
        self.at(self.k, i)[...] = jnp.where(in_first, dks[0], dks[1]).astype(BF)
        self.at(self.v, i)[...] = jnp.where(in_first, dvs[0], dvs[1]).astype(BF)

    def prepare(self, merged, inner):
        ref, _ = self.o
        self.inner = inner
        head = lax.broadcasted_iota(jnp.int32, (16, D), 0)
        lane = lax.broadcasted_iota(jnp.int32, (16, D), 1)
        of_head = ((lane >= head * HS) & (lane < head * HS + HS)).astype(F32).astype(BF)
        product = ref[...].astype(F32) * merged[...].astype(F32)
        high = product.astype(BF)
        low = (product - high.astype(F32)).astype(BF)
        inner[...] = mmt(of_head, high) + mmt(of_head, low)

    def each(self, what, first, last):
        def step(i, carry):
            what(i)
            return carry

        lax.fori_loop(first, last, step, 0)

    def finish(self):
        self.lse_rows[...] = self.lse_lanes[...].T[:16]


class Staged:
    def __init__(self, buffers, sems):
        self.buffers, self.sems = buffers, sems
        self.count = buffers.shape[0]
        self.turn = 0
        self.flying = {}

    def put(self, value, targets):
        slot = self.turn % self.count
        self.turn += 1
        wait_all(self.flying.pop(slot, []))
        self.buffers[slot] = value.reshape(self.buffers.shape[1:])
        copies = []
        for i, (first, size, target) in enumerate(targets):
            copy = pltpu.make_async_copy(
                self.buffers.at[slot, :, :, :, pl.ds(first, size)], target, self.sems.at[slot, i]
            )
            copy.start()
            copies.append(copy)
        self.flying[slot] = copies

    def drain(self):
        for copies in self.flying.values():
            wait_all(copies)
        self.flying = {}


def quarter_of(target, j):
    return [(0, D, target.at[j % 2, :, :, :, pl.ds(j // 2 * D, D)])]


def halves(target, which, first):
    return [
        (part * HALF, HALF, target.at[which, :, :, :, pl.ds(part * D + first, HALF)]) for part in range(2)
    ]


class Vectors:
    def __init__(self, refs):
        (
            self.norm1_gain,
            self.norm1_bias,
            self.attn_bias,
            self.norm2_gain,
            self.norm2_bias,
            self.up_bias,
            self.down_bias,
            self.query_gain,
            self.query_bias,
            self.cross_bias,
        ) = list(refs[:7]) + [refs[7].at[pl.ds(i, 1)] for i in range(3)]


def column_sums(values):
    return jnp.sum(values.astype(F32), axis=0, keepdims=True)


def scaled_norm(values, gain, bias):
    normed, _ = normalize(values)
    return (normed * gain[...] + bias[...]).astype(BF)


LAYER_WEIGHTS = [
    ((4, 2, 96, 3 * D), BF),
    ((2, 2, 2, 96, D), BF),
    ((4, 2, 96, FF), BF),
    ((2, 2, 4, 2, 96, D), BF),
]
CROSS_WEIGHTS = [((4, 2, 96, D), BF), ((4, 2, 96, 2 * D), BF), ((2, 2, 2, 96, D), BF)]
CHUNKED = [
    ((4, 4, 48, 3 * D), BF),
    ((2, 2, 2, 96, D), BF),
    ((4, 4, 48, FF), BF),
    ((2, 2, 4, 2, 96, D), BF),
]
SAVED = [((R, 3 * D), BF), ((R, D), BF), ((16, R), F32), ((R, D), F32), ((R, FF), BF), ((R, FF), BF)]
EXTRA = [((R, D), BF), ((R, 2 * D), BF), ((R, D), BF), ((16, R), F32), ((R, D), F32)]
WORK = [
    ((R, D), BF),
    ((R, 128), F32),
    ((R, D), F32),
    ((D, R), BF),
    ((D, R), BF),
    ((R, R), F32),
    ((R, 128), F32),
    ((16, R), F32),
]


def flat(ref, lanes=None):
    value = ref[...] if lanes is None else ref[..., lanes]
    return value.reshape(-1, value.shape[-1])


def down_chunk(wdn, j):
    return flat(wdn.at[j // 2, j % 2])


def column_chunks():
    return [pl.ds(j * D, D) for j in range(4)]


def hidden_units(u):
    phi = 0.5 * (1.0 + lax.erf(u * 0.7071067811865476))
    return u * phi, phi + u * jnp.exp(-0.5 * u * u) * 0.3989422804014327


def forward_kernel(*refs):
    here = Place()
    tiles, slopes, radar, optical, cotangent = refs[:5]
    vecs = Vectors(refs[5:13])
    qkv_own, attn_own, up_own, down_own, cq_own, kv_own, cw_own = refs[13:20]
    refs = refs[20:]
    gathered, arrived = refs[:2]
    saved_out, refs = refs[2:8], refs[8:]
    gdn, gup, gat, gcr, vec_out, joined_own, back_own, joined_all, back_all = refs[:9]
    refs = refs[9:]
    wqkv, wo, wup, wdn, wcq, wkv, wcw = refs[:7]
    saved, refs = refs[7:13], refs[13:]
    qkv, o, lse_rows, x1, g, gp = saved
    query, pairs, merged, lse_cross, x2 = refs[:5]
    a, lse_lanes, acc, et, at, dist, valid, inner = refs[5:13]
    xin, ctx, cot, e1, e2, out_bf, staging = refs[13:20]
    link_send, link_recv, near_send, near_recv, load_sems, save_sems, stage_sems = refs[20:]
    m, oth = here.m, here.o
    first, second = pl.when(here.first), pl.when(here.second)

    peers = here.along_x[1:] + here.along_z[1:] + [here.sibling, here.partner, here.section]
    here.signal(peers)
    loads = Loads(load_sems)
    heads = Heads((qkv, 0), (qkv, D), (qkv, 2 * D), (o, 0), dist, slopes, lse_lanes, lse_rows)
    cross = Heads(
        (query, 0), (pairs, 0), (pairs, D), (merged, 0), dist, slopes, lse_lanes, lse_cross
    )
    own_qkv = loads.start(
        *[(qkv_own.at[j], wqkv.at[:, :, :, lanes_at(j * D + m * HALF, HALF)]) for j in range(3)]
    )
    own_rest = loads.start(
        (attn_own, wo.at[m]),
        (up_own, wup.at[:, :, :, lanes_at(m * HIDDEN, HIDDEN)]),
        (down_own, wdn.at[m]),
    )
    token_loads = loads.start((optical.at[m], ctx), (cotangent.at[m], cot))
    cross_own = loads.start(
        (cq_own, wcq.at[:, :, :, lanes_at(m * HALF, HALF)]), (cw_own, wcw.at[m])
    )

    i = here.dp
    links = Links(link_send, link_recv)
    block, within = i // 8, (lax.rem(i // 2, 4), lax.rem(i, 2))
    tail_lanes = lanes_at(lax.rem(i // 4, 2) * HALF, HALF)
    tail = (lax.rem(i // 2, 2), within[1], slice(None), tail_lanes)
    part = lax.rem(block, 3)
    kv_part = lax.rem(block + 1, 2)

    @second
    def _():
        for j in range(2):
            wkv[:, :, :, lanes_at(j * D + m * HALF, HALF)] = kv_own[:, j, :].reshape(4, 2, 96, HALF)

    in_head, in_query = i < 24, i < 8
    in_tail, in_pairs = i >= 24, jnp.logical_and(i >= 8, i < 24)
    kv_lanes = lanes_at(kv_part * D + m * HALF, HALF)
    rest = slice(None)
    gathers = [
        Gather(here, links, gathered, g, sources)
        for g, sources in (
            (0, [(in_head, qkv_own.at[(part,) + within]), (in_tail, attn_own.at[tail])]),
            (1, [(None, up_own.at[within + (rest, lanes_at(block * HALF, HALF))])]),
            (
                3,
                [
                    (in_query, cq_own.at[within]),
                    (in_pairs, wkv.at[within + (rest, kv_lanes)]),
                    (in_tail, cw_own.at[tail]),
                ],
            ),
        )
    ]
    across = Across(here, links, down_own, gathered, 2)
    distances(tiles, m, dist, valid)

    def project(j, part):
        lanes = lanes_at(j * D + part * HALF, HALF)
        qkv[:, lanes] = mm(a[...], flat(wqkv, lanes)).astype(BF)

    @first
    def _():
        lse_lanes[...] = jnp.zeros_like(lse_lanes)
        copy = pltpu.make_async_copy(radar.at[m], xin, save_sems.at[6])
        copy.start()
        copy.wait()
        x = xin[...].astype(F32) * valid[:, :1]
        a[...] = scaled_norm(x, vecs.norm1_gain, vecs.norm1_bias)
        wait_all(own_qkv)
        for j in range(3):
            project(j, m)

    here.await_all(peers)
    for gather in gathers[:2]:
        gather.begin()

    @second
    def _():
        wait_all(cross_own)
        gathers[2].begin()

    across.begin()

    def stage(i):
        for gather in gathers[:2]:
            gather.stage(i)
        second(lambda: gathers[2].stage(i))

    for j in range(3):
        first(lambda: heads.forward(m * 3 + j))
        stage(j + 1)
    stage(4)
    gathers[0].stage(5)
    other_one = loads.start(
        *[
            (gathered.at[0, j], wqkv.at[:, :, :, lanes_at(j * D + oth * HALF, HALF)])
            for j in range(3)
        ],
        *[
            (gathered.at[0, 3, pl.ds(2 * j, 2)], wo.at[oth, :, :, :, pl.ds(j * HALF, HALF)])
            for j in range(2)
        ],
    )

    @first
    def _():
        wait_all(other_one[:3])
        for j in range(3):
            project(j, oth)

    gathers[1].stage(5)
    other_up = loads.start(
        *[
            (gathered.at[1, j], wup.at[:, :, :, lanes_at(oth * HIDDEN + j * HALF, HALF)])
            for j in range(4)
        ]
    )
    across.share()

    @first
    def _():
        heads.each(heads.forward, oth * 3, oth * 3 + 3)
        heads.finish()

    across.finish()
    other_down = loads.start(
        *[
            (
                gathered.at[2, pl.ds(2 * j, 2)],
                wdn.at[oth, :, :, :, :, pl.ds(j * HALF, HALF)],
            )
            for j in range(2)
        ]
    )

    def feed_forward(source, rows):
        a[rows] = scaled_norm(source[rows], vecs.norm2_gain, vecs.norm2_bias)
        for j, lanes in enumerate(column_chunks()):
            u = mm(a[rows], flat(wup, lanes)) + vecs.up_bias[:, lanes]
            unit, slope = hidden_units(u)
            g[rows, lanes] = unit.astype(BF)
            gp[rows, lanes] = slope.astype(BF)
            term = mm(g[rows, lanes], down_chunk(wdn, j))
            acc[rows] = term if j == 0 else acc[rows] + term

    near = (near_send, near_recv)
    blocks = [pl.ds(0, R // 2), pl.ds(R // 2, R // 2)]
    forth = [remote(out_bf.at[b], xin.at[b], near, i, here.section) for i, b in enumerate(blocks)]
    back = [
        remote(out_bf.at[b], arrived.at[b], near, 2 + i, here.section)
        for i, b in enumerate(blocks)
    ]

    @first
    def _():
        saves = [
            pltpu.make_async_copy(source, target, save_sems.at[i])
            for i, (source, target) in enumerate(zip(saved, saved_out))
        ]
        for copy in saves[:3]:
            copy.start()
        wait_all(own_rest)
        wait_all(other_one[3:])
        x = xin[...].astype(F32) * valid[:, :1]
        x1[...] = x + mm(o[...], flat(wo)) + vecs.attn_bias[...]
        saves[3].start()
        wait_all(other_up)
        wait_all(other_down)
        for rows, copy in zip(blocks, forth):
            feed_forward(x1, rows)
            out_bf[rows] = (x1[rows] + acc[rows] + vecs.down_bias[...]).astype(BF)
            copy.start()
        for copy in saves[4:]:
            copy.start()
        wait_all(saves)
        wait_all(token_loads)
        wait_all(cross_own)
        for copy in forth:
            copy.wait_send()
        for copy in back:
            copy.wait_recv()

    @second
    def _():
        gathers[2].stage(5)
        pairs_cross = [(gathered.at[3, 0], wcq.at[:, :, :, lanes_at(oth * HALF, HALF)])]
        for j in range(2):
            pairs_cross += [
                (gathered.at[3, j + 1], wkv.at[:, :, :, lanes_at(j * D + oth * HALF, HALF)]),
                (
                    gathered.at[3, 3, pl.ds(2 * j, 2)],
                    wcw.at[oth, :, :, :, pl.ds(j * HALF, HALF)],
                ),
            ]
        other_cross = loads.start(*pairs_cross)
        for copies in (own_qkv, own_rest, other_one, other_up, other_down):
            wait_all(copies)
        wait_all(token_loads)
        wait_all(other_cross)
        keep = valid[:, :1]
        ctx[...] = (ctx[...].astype(F32) * keep).astype(BF)
        cot[...] = (cot[...].astype(F32) * keep).astype(BF)
        for j in range(2):
            lanes = pl.ds(j * D, D)
            pairs[:, lanes] = mm(ctx[...], flat(wkv, lanes)).astype(BF)
        lse_lanes[...] = jnp.zeros_like(lse_lanes)
        for copy in forth:
            copy.wait_recv()
        a[...] = scaled_norm(xin[...].astype(F32), vecs.norm1_gain, vecs.norm1_bias)
        for j in range(3):
            lanes = pl.ds(j * D, D)
            qkv[:, lanes] = mm(a[...], flat(wqkv, lanes)).astype(BF)
        heads.each(heads.forward, 0, H // 2)
        heads.finish()
        x1[...] = xin[...].astype(F32) + mm(o[...], flat(wo)) + vecs.attn_bias[...]
        a[...] = scaled_norm(x1[...], vecs.query_gain, vecs.query_bias)
        query[...] = mm(a[...], flat(wcq)).astype(BF)
        cross.each(cross.forward, 0, H // 2)
        cross.finish()
        x2[...] = x1[...] + mm(merged[...], flat(wcw)) + vecs.cross_bias[...]
        feed_forward(x2, pl.ds(0, R))
        acc[...] = (x2[...] + acc[...] + vecs.down_bias[...]) * keep
        joined_own[...] = acc[rows_at(m * (R // 2), R // 2), pl.ds(HALF, HALF)]
        joined_all[...] = acc[...].astype(BF)

        for j, lanes in enumerate(column_chunks()):
            gp[:, lanes] = (mmt(cot[...], down_chunk(wdn, j)) * gp[:, lanes].astype(F32)).astype(BF)
            term = mmt(gp[:, lanes], flat(wup, lanes))
            acc[...] = term if j == 0 else acc[...] + term
        vec_out[...] = jnp.zeros_like(vec_out)
        dm = acc[...]
        normed, inverse = normalize(x2[...])
        vec_out[3:4, :] = column_sums(dm * normed)
        vec_out[4:5, :] = column_sums(dm)
        acc[...] = cot[...].astype(F32) + norm_grad(dm, normed, inverse, vecs.norm2_gain[...])
        e2[...] = acc[...].astype(BF)
        a[...] = mmt(e2[...], flat(wcw)).astype(BF)
        cross_back = Heads(
            (query, 0), (pairs, 0), (pairs, D), (a, 0), dist, slopes, lse_lanes, lse_cross
        )
        cross_back.prepare(merged, inner)
        cross_back.each(cross_back.backward, 0, H // 2)
        dc = mmt(query[...], flat(wcq))
        normed, inverse = normalize(x1[...])
        vec_out[10:11, :] = column_sums(dc * normed)
        vec_out[11:12, :] = column_sums(dc)
        acc[...] = acc[...] + norm_grad(dc, normed, inverse, vecs.query_gain[...])
        e1[...] = acc[...].astype(BF)
        a[...] = mmt(e1[...], flat(wo)).astype(BF)
        self_back = Heads(
            (qkv, 0), (qkv, D), (qkv, 2 * D), (a, 0), dist, slopes, lse_lanes, lse_rows
        )
        self_back.prepare(o, inner)
        self_back.each(self_back.backward, 0, H // 2)
        sums = []
        for rows, copy in zip(blocks, back):
            da = mmt(qkv[rows], flat(wqkv))
            normed, inverse = normalize(xin[rows].astype(F32))
            sums.append((column_sums(da * normed), column_sums(da)))
            out_bf[rows] = (
                acc[rows] + norm_grad(da, normed, inverse, vecs.norm1_gain[...])
            ).astype(BF)
            copy.start()
        vec_out[0:1, :] = sums[0][0] + sums[1][0]
        vec_out[1:2, :] = sums[0][1] + sums[1][1]

        staged = Staged(staging, stage_sems)
        acc[...] = mmt(pairs[...], flat(wkv)) * keep
        back_own[...] = acc[rows_at(m * (R // 2), R // 2), pl.ds(HALF, HALF)]
        back_all[...] = acc[...].astype(BF)
        permute = chunk_order()
        et[...] = mmt(permute, e2[...]).astype(BF)
        staged.put(mm(et[...], merged[...]).astype(BF), halves(gcr, 1, HALF))
        a[...] = scaled_norm(x1[...], vecs.query_gain, vecs.query_bias)
        et[...] = mmt(permute, a[...]).astype(BF)
        staged.put(mm(et[...], query[...]).astype(BF), halves(gcr, 0, 0))
        et[...] = mmt(permute, ctx[...]).astype(BF)
        for j, target in enumerate([(0, HALF), (1, 0)]):
            staged.put(mm(et[...], pairs[:, pl.ds(j * D, D)]).astype(BF), halves(gcr, *target))
        et[...] = cot[...].T
        a[...] = scaled_norm(x2[...], vecs.norm2_gain, vecs.norm2_bias)
        at[...] = a[...].T
        for j, lanes in enumerate(column_chunks()):
            vec_out[6 + j : 7 + j, :] = column_sums(gp[:, lanes])
            staged.put(mm(et[...], g[:, lanes]).astype(BF), quarter_of(gdn, j))
            staged.put(mm(at[...], gp[:, lanes]).astype(BF), quarter_of(gup, j))
        vec_out[2:3, :] = column_sums(e1[...])
        vec_out[5:6, :] = column_sums(cot[...])
        vec_out[12:13, :] = column_sums(e2[...])
        et[...] = e1[...].T
        staged.put(mm(et[...], o[...]).astype(BF), halves(gat, 1, HALF))
        a[...] = scaled_norm(xin[...].astype(F32), vecs.norm1_gain, vecs.norm1_bias)
        at[...] = a[...].T
        for j, target in enumerate([(0, 0), (0, HALF), (1, 0)]):
            staged.put(mm(at[...], qkv[:, pl.ds(j * D, D)]).astype(BF), halves(gat, *target))
        staged.drain()
        for copy in back:
            copy.wait_send()
        gathers[2].drain()

    for gather in gathers[:2] + [across]:
        gather.drain()


def chunk_order():
    r = lax.broadcasted_iota(jnp.int32, (D, 1), 0).astype(F32)
    chunk = jnp.floor((r + 0.5) / 48.0)
    inner = r - chunk * 48.0
    core = (inner >= 24.0).astype(F32)
    inner = inner - 24.0 * core
    section = (inner >= 12.0).astype(F32)
    source = 384.0 * section + 24.0 * chunk + 12.0 * core + inner - 12.0 * section
    columns = lax.broadcasted_iota(jnp.int32, (D, D), 1).astype(F32)
    return (columns == source).astype(F32).astype(BF)


def forward(tiles, slopes, tokens, vecs, own):
    scratch = vmem(
        LAYER_WEIGHTS + CROSS_WEIGHTS + SAVED + EXTRA + WORK + [((R, D), BF)] * 6 + [((2, 4, 4, 48, D), BF)]
    )
    quarter = shape((R // 2, HALF), F32)
    return pl.pallas_call(
        forward_kernel,
        out_shape=[shape((4, 4, 4, 2, 96, HALF), BF), shape((R, D), BF)]
        + [shape(*s) for s in SAVED]
        + [shape((2, 4, 4, 48, 2 * D), BF)] * 4
        + [shape((16, D), F32), quarter, quarter, shape((R, D), BF), shape((R, D), BF)],
        in_specs=[SM, SM] + [ANY] * 3 + [VM] * 8 + [ANY] * 5 + [VM] + [ANY],
        out_specs=[ANY] * 12 + [VM] * 5,
        scratch_shapes=scratch
        + [dma(92), dma(92), dma(4), dma(4), dma(40), dma(7), pltpu.SemaphoreType.DMA((2, 2))],
        compiler_params=pltpu.CompilerParams(
            collective_id=0, has_side_effects=True, vmem_limit_bytes=BIG
        ),
    )(tiles, slopes, *tokens, *vecs, *own)


def backward_kernel(*refs):
    here = Place()
    tiles, slopes, radar, dy_in = refs[:4]
    vecs = Vectors(refs[4:12])
    qkv_own, attn_own, up_own, down_own, gathered, gathered48 = refs[12:18]
    saved_in, refs = refs[18:24], refs[24:]
    vec_in, joined_all, back_all, gcr = refs[:4]
    refs = refs[7:]
    gdn, gup, gat, odn, oup, oat, ocr, vec_total, vec_other, radar_own, quarters, ocr_other = refs[
        :12
    ]
    refs = refs[12:]
    wqkv, wo, wup, wdn = refs[:4]
    saved, refs = refs[4:10], refs[10:]
    qkv, o, lse_rows, x1, g, gp = saved
    a, lse_lanes, acc, et, at, dist, valid, inner = refs[:8]
    xin, out_bf, staging, vec, vbuf = refs[8:13]
    own_at, cross_sums = refs[13:15]
    buffers, refs = [refs[15 + 7 * i : 22 + 7 * i] for i in range(4)], refs[43:]
    link_send, link_recv, far_send, far_recv, load_sems, local_sems, stage_sems = refs
    m, oth = here.m, here.o
    first, second = pl.when(here.first), pl.when(here.second)
    peers = here.ring + [
        here.sibling,
        here.partner,
        here.diagonal,
        here.along_x[2],
        here.along_z[2],
        here.section,
        here.crossed,
    ]
    here.signal(peers)
    loads = Loads(load_sems)
    links = Links(link_send, link_recv)
    far = (far_send, far_recv)
    staged = Staged(staging, stage_sems)
    heads = Heads((qkv, 0), (qkv, D), (qkv, 2 * D), (a, 0), dist, slopes, lse_lanes, lse_rows)
    chunks = column_chunks()

    cotangent = loads.prepare((dy_in, out_bf))
    units = [loads.prepare((saved_in[4].at[:, c], g.at[j % 2])) for j, c in enumerate(chunks)]
    early = loads.prepare((saved_in[3], x1), (radar.at[m], xin))
    copies_down = loads.prepare(
        (down_own, wdn.at[m]),
        *[
            (gathered.at[2, pl.ds(2 * j, 2)], wdn.at[oth, :, :, :, :, pl.ds(j * HALF, HALF)])
            for j in range(2)
        ],
    )
    slopes_of = [loads.prepare((saved_in[5].at[:, c], gp.at[:, c])) for c in chunks]
    copies_up = loads.prepare(
        (up_own, wup.at[:, :, :, lanes_at(m * HIDDEN, HIDDEN)]),
        *[
            (gathered48.at[1, j], wup.at[:, :, :, lanes_at(oth * HIDDEN + j * HALF, HALF)])
            for j in range(4)
        ],
    )
    late = loads.prepare(
        (saved_in[0], qkv),
        (saved_in[1], o),
        (saved_in[2], lse_rows),
        (attn_own, wo.at[m]),
        *[
            (gathered.at[0, 3, pl.ds(2 * j, 2)], wo.at[oth, :, :, :, pl.ds(j * HALF, HALF)])
            for j in range(2)
        ],
    )
    copies_qkv = loads.prepare(
        *[(qkv_own.at[j], wqkv.at[:, :, :, lanes_at(j * D + m * HALF, HALF)]) for j in range(3)],
        *[
            (gathered48.at[0, j], wqkv.at[:, :, :, lanes_at(j * D + oth * HALF, HALF)])
            for j in range(3)
        ],
    )

    @first
    def _():
        for copies in [cotangent] + units[:2] + [early, copies_down] + slopes_of + [copies_up, late]:
            start_all(copies)
        distances(tiles, m, dist, valid)
        vec[...] = jnp.zeros_like(vec)
        wait_all(cotangent)
        e3 = out_bf[...]
        vec[5:6, :] = column_sums(e3)
        et[...] = e3.T
        for j in range(4):
            wait_all(units[j])
            staged.put(mm(et[...], g[j % 2]).astype(BF), quarter_of(gdn, j))
            if j < 2:
                start_all(units[j + 2])
        staged.drain()

    @second
    def _():
        vec[...] = vec_in[...]

    here.await_all(peers)
    low, high = pl.ds(0, 2 * D), pl.ds(2 * D, 2 * D)
    dn = scatter_stages(
        here, links, local_sems.at[0], gdn, odn, wqkv.at[:, :, :, low], buffers[0]
    )
    up = scatter_stages(here, links, local_sems.at[1], gup, oup, wup.at[:, :, :, low], buffers[1])
    mid = scatter_stages(here, links, local_sems.at[2], gat, oat, own_at, buffers[2])
    cross = scatter_stages(
        here, links, local_sems.at[3], gcr, cross_sums, wup.at[:, :, :, high], buffers[3]
    )
    vec_steps = vector_stages(here, links, vec, vbuf, vec_total)

    def quarter_copies(source, kind):
        half_rows = R // 2
        mine, others = rows_at(m * half_rows, half_rows), rows_at(oth * half_rows, half_rows)
        sender, receiver = (0, 1) if kind == 2 else (1, 0)
        same = pl.ds(sender * HALF, HALF)
        over = pl.ds(receiver * HALF, HALF)
        return [
            remote(source.at[mine, over], quarters.at[kind, 0], far, 3 * kind, here.section),
            remote(source.at[others, over], quarters.at[kind, 1], far, 3 * kind + 1, here.crossed),
            remote(source.at[others, same], quarters.at[kind, 1], far, 3 * kind + 2, here.partner),
        ]

    sent = [quarter_copies(s, i) for i, s in enumerate((joined_all, back_all, out_bf))]
    cross_sent = remote(ocr.at[0], ocr_other, far, 9, here.section)
    vec_sent = remote(vec_total, vec_other, far, 10, here.section)

    @second
    def _():
        for copies in sent[:2]:
            for copy in copies:
                copy.start()
        cross[0]()

    dn[0]()
    second(cross[1])

    def chain(j):
        lanes = chunks[j]
        wait_all(slopes_of[j])
        du = (mmt(out_bf[...], down_chunk(wdn, j)) * gp[:, lanes].astype(F32)).astype(BF)
        gp[:, lanes] = du
        vec[6 + j : 7 + j, :] = column_sums(du)
        staged.put(mm(at[...], gp[:, lanes]).astype(BF), quarter_of(gup, j))
        if j == 0:
            wait_all(copies_up)
        term = mmt(gp[:, lanes], flat(wup, lanes))
        acc[...] = term if j == 0 else acc[...] + term

    @first
    def _():
        wait_all(early)
        a[...] = scaled_norm(x1[...], vecs.norm2_gain, vecs.norm2_bias)
        at[...] = a[...].T
        wait_all(copies_down)
        chain(0)
        chain(1)
        staged.drain()

    dn[1]()

    @first
    def _():
        chain(2)
        chain(3)
        wait_all(late)
        staged.drain()

    up[0]()
    second(cross[2])
    dn[2]()

    @first
    def _():
        dm = acc[...]
        normed, inverse = normalize(x1[...])
        vec[3:4, :] = column_sums(dm * normed)
        vec[4:5, :] = column_sums(dm)
        acc[...] = out_bf[...].astype(F32) + norm_grad(dm, normed, inverse, vecs.norm2_gain[...])
        e1 = acc[...].astype(BF)
        vec[2:3, :] = column_sums(e1)
        out_bf[...] = e1
        a[...] = mmt(out_bf[...], flat(wo)).astype(BF)
        heads.prepare(o, inner)

    up[1]()
    second(cross[3])

    @first
    def _():
        et[...] = out_bf[...].T
        staged.put(mm(et[...], o[...]).astype(BF), halves(gat, 1, HALF))
        heads.backward(0)
        staged.drain()

    dn[3]()
    first(lambda: heads.each(heads.backward, 1, 3))
    up[2]()
    second(cross[4])
    dn[4]()
    first(lambda: heads.backward(3))
    up[3]()
    dn[5]()
    second(cross[5])

    @first
    def _():
        start_all(copies_qkv)
        heads.each(heads.backward, 4, 6)

    up[4]()

    @first
    def _():
        x = xin[...].astype(F32) * valid[:, :1]
        a[...] = scaled_norm(x, vecs.norm1_gain, vecs.norm1_bias)
        at[...] = a[...].T
        for j, target in enumerate([(0, 0), (0, HALF), (1, 0)]):
            staged.put(mm(at[...], qkv[:, pl.ds(j * D, D)]).astype(BF), halves(gat, *target))
        staged.drain()
        wait_all(copies_qkv)

    mid[0]()

    @first
    def _():
        da = mmt(qkv[...], flat(wqkv))
        normed, inverse = normalize(xin[...].astype(F32) * valid[:, :1])
        vec[0:1, :] = column_sums(da * normed)
        vec[1:2, :] = column_sums(da)
        acc[...] = (acc[...] + norm_grad(da, normed, inverse, vecs.norm1_gain[...])) * valid[:, :1]
        radar_own[...] = acc[rows_at(m * (R // 2), R // 2), pl.ds(0, HALF)]
        out_bf[...] = acc[...].astype(BF)
        for copy in sent[2]:
            copy.start()

    @second
    def _():
        for section in range(2):
            for which in range(2):
                ocr[section, which] = cross_sums[which][section * 12 : section * 12 + 12]
        cross_sent.start()

    vec_steps[0]()
    mid[1]()
    vec_steps[1]()
    up[5]()
    mid[2]()
    vec_steps[2]()
    mid[3]()
    vec_steps[3]()
    mid[4]()
    vec_steps[4]()

    @second
    def _():
        vec_sent.start()

    mid[5]()

    @first
    def _():
        for copies in sent[:2]:
            copies[0].wait_recv()
            copies[1].wait_recv()
        sent[2][2].wait_recv()
        for copy in sent[2]:
            copy.wait_send()
        cross_sent.wait_recv()
        vec_sent.wait_recv()

    @second
    def _():
        sent[2][0].wait_recv()
        sent[2][1].wait_recv()
        for copies in sent[:2]:
            copies[2].wait_recv()
            for copy in copies:
                copy.wait_send()
        cross_sent.wait_send()
        vec_sent.wait_send()


def backward(tiles, slopes, radar, dy, vecs, own, gathered, saved, vec, quarters, gcr, grads):
    scratch = vmem(
        CHUNKED
        + SAVED[:4]
        + [((2, R, D), BF)]
        + SAVED[5:]
        + WORK
        + [((R, D), BF)] * 2
        + [((2, 4, 4, 48, D), BF), ((16, D), F32), ((8, 16, D), F32)]
    )
    vector = shape((16, D), F32)
    qkv, attn, up, down = own
    return pl.pallas_call(
        backward_kernel,
        out_shape=[
            *[shape(array.shape, BF) for array in grads],
            *[shape((2, 24, D), F32)] * 3,
            shape((2, 2, 12, D), F32),
            vector,
            vector,
            shape((R // 2, HALF), F32),
            shape((3, 2, R // 2, HALF), BF),
            shape((2, 12, D), F32),
        ],
        in_specs=[SM, SM, ANY, ANY] + [VM] * 8 + [ANY] * 12 + [VM] + [ANY] * 6,
        out_specs=[ANY] * 3 + [VM] * 7 + [ANY, VM],
        input_output_aliases={28: 0, 29: 1, 30: 2},
        scratch_shapes=scratch
        + own_scratch(2 * D)
        + [pltpu.VMEM((2, 24, D), F32)]
        + scatter_scratch(2 * D) * 4
        + [dma(124), dma(124), dma(11), dma(11), dma(40), dma(4), pltpu.SemaphoreType.DMA((2, 2))],
        compiler_params=pltpu.CompilerParams(
            collective_id=1, has_side_effects=True, vmem_limit_bytes=BIG
        ),
    )(
        tiles,
        slopes,
        radar,
        dy,
        *vecs,
        qkv.reshape(3, 4, 4, 48, HALF),
        attn,
        up.reshape(4, 4, 48, HIDDEN),
        down,
        gathered,
        gathered.reshape(4, 4, 4, 4, 48, HALF),
        *saved,
        vec,
        *quarters,
        gcr,
        *grads,
    )


def local(
    radar_tokens,
    optical_tokens,
    out_cotangent,
    tile_sides,
    norm1_gain,
    norm1_bias,
    qkv_weight,
    attn_weight,
    attn_bias,
    norm2_gain,
    norm2_bias,
    up_weight,
    up_bias,
    down_weight,
    down_bias,
    query_gain,
    query_bias,
    cross_query,
    cross_keyval,
    cross_weight,
    cross_bias,
):
    m = lax.axis_index("mp")
    joining = lax.axis_index("pipe") == 1
    slopes = jnp.exp2(-8.0 * (jnp.arange(H, dtype=jnp.int32) + 1).astype(F32) / H)
    vecs = (
        norm1_gain,
        norm1_bias,
        attn_bias,
        norm2_gain,
        norm2_bias,
        up_bias,
        down_bias,
        jnp.stack([query_gain, query_bias, cross_bias]),
    )
    own = (
        qkv_weight[0].transpose(1, 0, 2).reshape(3, 4, 2, 96, HALF),
        attn_weight.reshape(2, 2, 96, D),
        up_weight.reshape(4, 2, 96, HIDDEN),
        down_weight.reshape(2, 4, 2, 96, D),
    )
    cross_own = (
        cross_query.reshape(4, 2, 96, HALF),
        cross_keyval,
        cross_weight.reshape(2, 2, 96, D),
    )
    tokens = (radar_tokens, optical_tokens, out_cotangent)
    results = forward(
        tile_sides, slopes, tokens, vecs, own + cross_own
    )
    gathered, dy0 = results[:2]
    saved = results[2:8]
    grads = results[8:11]
    gcr, vec, joined_own, back_own, joined_all, back_all = results[11:]
    outs = backward(
        tile_sides,
        slopes,
        radar_tokens,
        dy0,
        vecs,
        own,
        gathered,
        saved,
        vec,
        (joined_all, back_all),
        gcr,
        grads,
    )
    odn, oup, oat, ocr, vec, vec_other, radar_own, quarters, ocr_other = outs[3:]

    def placed(own_quarter, kind, here):
        mine = jnp.where(here, own_quarter, quarters[kind, 0].astype(F32))
        others = quarters[kind, 1].astype(F32)
        swap = m == 1
        return jnp.stack([jnp.where(swap, others, mine), jnp.where(swap, mine, others)])

    crossed = jnp.where(joining, vec[10:13], vec_other[10:13])
    ocr = jnp.where(joining, ocr[1], ocr_other)
    q, k = oat[0, :, :HALF], oat[0, :, HALF:]
    v, attn = oat[1, :, :HALF], oat[1, :, HALF:]
    cq, ck = ocr[0, :, :HALF], ocr[0, :, HALF:]
    cv, cw = ocr[1, :, :HALF], ocr[1, :, HALF:]
    return (
        placed(joined_own, 0, joining),
        placed(radar_own, 2, jnp.logical_not(joining)),
        placed(back_own, 1, joining),
        vec[0:1],
        vec[1:2],
        jnp.stack([q, k, v], axis=1)[None],
        attn.T[None],
        vec[2:3],
        vec[3:4],
        vec[4:5],
        jnp.concatenate([oup[0], oup[1]], axis=1)[None],
        vec[6:10].reshape(1, FF),
        jnp.concatenate([odn[0].T, odn[1].T])[None],
        vec[5:6],
        crossed[0],
        crossed[1],
        cq,
        jnp.stack([ck, cv], axis=1),
        cw.T,
        crossed[2],
    )


def solution(mesh):
    in_specs = (
        P(None, "dp", None),
        P(None, "dp", None),
        P(None, "dp", None),
        P(None, "dp"),
        P("pipe", None),
        P("pipe", None),
        P("pipe", None, None, "mp"),
        P("pipe", "mp", None),
        P("pipe", None),
        P("pipe", None),
        P("pipe", None),
        P("pipe", None, "mp"),
        P("pipe", None),
        P("pipe", "mp", None),
        P("pipe", None),
        P(),
        P(),
        P(None, "mp"),
        P(None, None, "mp"),
        P("mp", None),
        P(),
    )
    out_specs = (
        P(None, ("dp", "mp"), "pipe"),
        P(None, ("dp", "mp"), "pipe"),
        P(None, ("dp", "mp"), "pipe"),
        P("pipe", None),
        P("pipe", None),
        P("pipe", "dp", None, "mp"),
        P("pipe", "mp", "dp"),
        P("pipe", None),
        P("pipe", None),
        P("pipe", None),
        P("pipe", "dp", "mp"),
        P("pipe", None),
        P("pipe", "mp", "dp"),
        P("pipe", None),
        P(),
        P(),
        P(("pipe", "dp"), "mp"),
        P(("pipe", "dp"), None, "mp"),
        P("mp", ("pipe", "dp")),
        P(),
    )
    return jax.shard_map(local, mesh=mesh, in_specs=in_specs, out_specs=out_specs, check_vma=False)
```

```python
import jax
import jax.numpy as jnp
from jax import lax
from jax.experimental import pallas as pl
from jax.experimental.pallas import tpu as pltpu
from jax.sharding import PartitionSpec as P

H = 12
HS = 64
D = 768
FF = 3072
ROWS = 512
R = 464
HALF = D // 2
HIDDEN = FF // 2
SLOTS = 3
EPSILON = 1e-05
BF = jnp.bfloat16
F32 = jnp.float32
ANY = pl.BlockSpec(memory_space=pl.ANY)
VM = pl.BlockSpec(memory_space=pltpu.VMEM)
SM = pl.BlockSpec(memory_space=pltpu.SMEM)
MESH = pl.DeviceIdType.MESH
BIG = 62 * 1024 * 1024


def shape(dims, kind):
    return jax.ShapeDtypeStruct(dims, kind)


def vmem(shapes):
    return [pltpu.VMEM(dims, kind) for dims, kind in shapes]


def dma(count):
    return pltpu.SemaphoreType.DMA((count,))


class Place:
    def __init__(self):
        dp = lax.axis_index("dp")
        self.dp = dp
        self.pipe = lax.axis_index("pipe")
        self.m = lax.axis_index("mp")
        self.o = 1 - self.m
        self.core = lax.rem(dp, 2)
        self.twin = 1 - self.core
        chip = dp // 2
        self.x = lax.rem(chip, 4)
        self.z = chip // 4
        self.xs = [self.x] + [lax.rem(self.x + i, 4) for i in (1, 2, 3)]
        self.zs = [self.z] + [lax.rem(self.z + i, 4) for i in (1, 2, 3)]
        self.along_x = [self.at(self.z, x, self.core) for x in self.xs]
        self.along_z = [self.at(z, self.x, self.core) for z in self.zs]
        self.sibling = self.at(self.z, self.x, self.twin)
        self.partner = {"mp": self.o}
        self.section = {"pipe": 1 - self.pipe}
        self.crossed = {"pipe": 1 - self.pipe, "mp": self.o}
        self.diagonal = dict(self.sibling, mp=self.o)
        self.ring = [self.along_x[1], self.along_x[3], self.along_z[1], self.along_z[3]]
        self.first = self.pipe == 0
        self.second = self.pipe == 1

    def at(self, z, x, core):
        return {"dp": (z * 4 + x) * 2 + core}

    def signal(self, devices):
        barrier = pltpu.get_barrier_semaphore()
        for device in devices:
            pl.semaphore_signal(barrier, inc=1, device_id=device, device_id_type=MESH)

    def await_all(self, devices):
        pl.semaphore_wait(pltpu.get_barrier_semaphore(), len(devices))


def remote(source, target, sems, i, device):
    return pltpu.make_async_remote_copy(
        src_ref=source,
        dst_ref=target,
        send_sem=sems[0].at[i],
        recv_sem=sems[1].at[i],
        device_id=device,
        device_id_type=MESH,
    )


class Links:
    def __init__(self, *sems):
        self.sems = sems
        self.used = 0

    def prepare(self, source, target, device):
        copy = remote(source, target, self.sems, self.used, device)
        self.used += 1
        return copy


class Loads:
    def __init__(self, sems):
        self.sems = sems
        self.used = 0

    def prepare(self, *pairs):
        copies = []
        for source, target in pairs:
            copies.append(pltpu.make_async_copy(source, target, self.sems.at[self.used]))
            self.used += 1
        return copies

    def start(self, *pairs):
        return start_all(self.prepare(*pairs))


def start_all(copies):
    for copy in copies:
        copy.start()
    return copies


def wait_all(copies):
    for copy in copies:
        copy.wait()


def lanes_at(first, size):
    return pl.ds(pl.multiple_of(first, 128), size)


def rows_at(first, size):
    return pl.ds(pl.multiple_of(first, 16), size)


class Gather:
    def __init__(self, here, links, out, g, sources):
        c, x, z = here.core, here.x, here.z
        xs, zs = here.xs, here.zs
        right, left, up, down = here.ring
        a, b = pl.ds(0, 48), pl.ds(48, 48)
        low, high = pl.ds(0, 2), pl.ds(2, 2)
        at = links.used
        self.begins = [
            (condition, remote(source, out.at[g, z, x, c], links.sems, at, here.partner))
            for condition, source in sources
        ]
        links.used = at + 1

        def same(view, device):
            return links.prepare(view, view, device)

        direct, early = [], []
        for j in (2, 1, 3):
            direct.append(same(out.at[g, z, x, c, a], here.along_x[j]))
            direct.append(same(out.at[g, z, x, c, b], here.along_z[j]))
        for j in (0, 1, 3):
            early.append(same(out.at[g, zs[j], :, c, a], here.sibling))
            early.append(same(out.at[g, :, xs[j], c, b], here.sibling))
        near = [
            same(out.at[g, z, :, c, a], up),
            same(out.at[g, z, :, c, a], down),
            same(out.at[g, :, x, c, b], right),
            same(out.at[g, :, x, c, b], left),
        ]
        relayed = [
            same(out.at[g, zs[3], low, c, a], up),
            same(out.at[g, zs[1], high, c, a], down),
            same(out.at[g, low, xs[3], c, b], right),
            same(out.at[g, high, xs[1], c, b], left),
        ]
        late = [
            same(out.at[g, zs[2], :, c, a], here.sibling),
            same(out.at[g, :, xs[2], c, b], here.sibling),
        ]
        first = [self.begins[-1][1]]
        self.waits = [[], first, direct, near, relayed, early + late]
        self.starts = [[], direct, near, relayed + early, late, []]
        self.all = first + direct + near + relayed + early + late

    def begin(self):
        for condition, copy in self.begins:
            if condition is None:
                copy.start()
            else:
                pl.when(condition)(copy.start)

    def stage(self, i):
        for copy in self.waits[i]:
            copy.wait_recv()
        for copy in self.starts[i]:
            copy.start()

    def drain(self):
        for copy in self.all:
            copy.wait_send()


class Across:
    def __init__(self, here, links, own, out, g):
        c = here.core
        spans = [pl.ds(2 * j, 2) for j in range(2)]
        self.copies = [
            links.prepare(
                own.at[:, :, c, :, pl.ds(j * HALF, HALF)], out.at[g, span, :, c], here.partner
            )
            for j, span in enumerate(spans)
        ]
        self.shared = [
            links.prepare(out.at[g, span, :, c], out.at[g, span, :, c], here.sibling)
            for span in spans
        ]

    def begin(self):
        start_all(self.copies)

    def share(self):
        for copy, onward in zip(self.copies, self.shared):
            copy.wait_recv()
            onward.start()

    def finish(self):
        for copy in self.shared:
            copy.wait_recv()

    def drain(self):
        for copy in self.copies + self.shared:
            copy.wait_send()


def vector_stages(here, links, vec, vbuf, total):
    rounds = [[here.sibling], here.along_x[1:], here.along_z[1:], [here.partner]]
    copies, used = [], 0
    for devices in rounds:
        copies.append(
            [links.prepare(total, vbuf.at[used + i], d) for i, d in enumerate(devices)]
        )
        used += len(devices)

    def begin(i):
        def stage():
            if i == 0:
                total[...] = vec[...]
            else:
                first = sum(len(devices) for devices in rounds[: i - 1])
                for copy in copies[i - 1]:
                    copy.wait()
                value = total[...]
                for j in range(len(rounds[i - 1])):
                    value = value + vbuf[first + j]
                total[...] = value
            if i < len(rounds):
                for copy in copies[i]:
                    copy.start()

        return stage

    return [begin(i) for i in range(len(rounds) + 1)]


def scatter_scratch(cols):
    half = cols // 2
    return [
        pltpu.VMEM((4, 4, 48, cols), BF),
        pltpu.VMEM((2, 2, 2, 48, half), BF),
        pltpu.VMEM((2, 2, 4, 48, half), BF),
        pltpu.VMEM((2, 4, 48, half), BF),
        pltpu.VMEM((2, 3, 48, half), BF),
        pltpu.VMEM((2, 2, 24, half), F32),
        pltpu.VMEM((3, 24, half), F32),
    ]


def scatter_stages(here, links, local_sem, grads, out, own, buffers):
    other, far, near, mid, near2, late, last = buffers
    cols = own.shape[-1]
    half = cols // 2
    c, twin, m, o = here.core, here.twin, here.m, here.o
    xs, zs = here.xs, here.zs
    lanes = [pl.ds(0, half), pl.ds(half, half)]
    low, high = pl.ds(0, 2), pl.ds(2, 2)
    ahead = [here.along_x[1], here.along_z[1]]
    behind = [here.along_x[3], here.along_z[3]]

    def block(ref, way, j):
        if way == 0:
            return ref.at[:, xs[j], :, lanes[0]]
        return ref.at[zs[j], :, :, lanes[1]]

    def part(ref, way, j, span):
        if way == 0:
            return ref.at[span, xs[j], :, lanes[0]]
        return ref.at[zs[j], span, :, lanes[1]]

    def places(way):
        return zs if way == 0 else xs

    order = [(way, j) for j in (2, 1, 3, 0) for way in range(2)]
    local = pltpu.make_async_copy(grads.at[c], own, local_sem)
    exchange = {
        (way, j): links.prepare(
            block(grads.at[twin], way, j), block(other, way, j), here.sibling
        )
        for way, j in order
    }
    one, two, three = [], [], []
    for way in range(2):
        turn = 1 - way
        at = places(way)
        one.append(
            [
                links.prepare(part(own, way, 2, low), far.at[way, 0], ahead[way]),
                links.prepare(part(own, way, 2, high), far.at[way, 1], behind[way]),
                links.prepare(part(own, way, 1, high), near.at[way, 0, high], ahead[way]),
                links.prepare(part(own, way, 3, low), near.at[way, 1, low], behind[way]),
            ]
        )
        two.append(
            [
                links.prepare(part(own, way, 1, low), near.at[way, 0, low], ahead[way]),
                links.prepare(part(own, way, 3, high), near.at[way, 1, high], behind[way]),
            ]
        )
        axis = (here.along_x, here.along_z)[turn]
        three.append(
            [
                links.prepare(mid.at[way, at[j]], near2.at[way, j - 1], axis[j])
                for j in (2, 1, 3)
            ]
        )
    ending = [
        links.prepare(late.at[m, twin], last.at[0], here.sibling),
        links.prepare(late.at[o, c], last.at[1], here.partner),
        links.prepare(late.at[o, twin], last.at[2], here.diagonal),
    ]

    def start():
        local.start()
        for key in order:
            exchange[key].start()

    def add_other(way, j):
        exchange[way, j].wait_recv()
        mine, theirs = block(own, way, j), block(other, way, j)
        for i in range(4):
            mine[i] = mine[i] + theirs[i]

    def ring_one():
        local.wait()
        for way in range(2):
            add_other(way, 2)
            one[way][0].start()
            one[way][1].start()
        for way in range(2):
            add_other(way, 1)
            one[way][2].start()
            add_other(way, 3)
            one[way][3].start()
        for way in range(2):
            add_other(way, 0)

    def ring_two():
        for way in range(2):
            one[way][0].wait_recv()
            target = part(own, way, 1, low)
            for i in range(2):
                target[i] = target[i] + far[way, 0, i]
            two[way][0].start()
            one[way][1].wait_recv()
            target = part(own, way, 3, high)
            for i in range(2):
                target[i] = target[i] + far[way, 1, i]
            two[way][1].start()

    def ring_three():
        for way in range(2):
            for copy in one[way][2:] + two[way]:
                copy.wait_recv()
            mine = block(own, way, 0)
            for i in range(4):
                mid[way, i] = (
                    mine[i].astype(F32) + near[way, 0, i].astype(F32) + near[way, 1, i].astype(F32)
                ).astype(BF)
            for copy in three[way]:
                copy.start()

    def to_owners():
        for way in range(2):
            for copy in three[way]:
                copy.wait_recv()
            total = mid[way, places(way)[0]].astype(F32)
            for j in range(3):
                total = total + near2[way, j].astype(F32)
            late[way, 0] = total[:24]
            late[way, 1] = total[24:]
        for copy in ending:
            copy.start()

    def finish():
        for copy in ending:
            copy.wait_recv()
        out[c] = late[m, c] + last[1]
        out[twin] = last[0] + last[2]
        for key in order:
            exchange[key].wait_send()
        for step in one + two + three + [ending]:
            for copy in step:
                copy.wait_send()

    return [start, ring_one, ring_two, ring_three, to_owners, finish]


def own_scratch(cols):
    return [pltpu.VMEM((4, 4, 48, cols), BF)]


def mm(a, b):
    return lax.dot_general(a, b, (((1,), (0,)), ((), ())), preferred_element_type=F32)


def mmt(a, b):
    return lax.dot_general(a, b, (((1,), (1,)), ((), ())), preferred_element_type=F32)


def tmm(a, b):
    return lax.dot_general(a, b, (((0,), (0,)), ((), ())), preferred_element_type=F32)


def normalize(values):
    centered = values - jnp.mean(values, axis=-1, keepdims=True)
    inverse = lax.rsqrt(jnp.mean(centered * centered, axis=-1, keepdims=True) + EPSILON)
    return centered * inverse, inverse


def norm_grad(upstream, normed, inverse, gain):
    scaled = upstream * gain
    return inverse * (
        scaled
        - jnp.mean(scaled, axis=-1, keepdims=True)
        - normed * jnp.mean(scaled * normed, axis=-1, keepdims=True)
    )


class Geometry:
    def __init__(self, tiles, m, places):
        starts, member = [0], jnp.zeros_like(places)
        for slot in range(SLOTS):
            side = tiles[m, slot]
            starts.append(starts[-1] + side * side)
            member = member + (places >= starts[-1]).astype(jnp.int32)
        first, side = jnp.zeros_like(places), jnp.ones_like(places)
        for slot in range(SLOTS):
            here = member == slot
            first = jnp.where(here, starts[slot], first)
            side = jnp.where(here, jnp.maximum(tiles[m, slot], 1), side)
        first = jnp.where(member == SLOTS, starts[SLOTS], first)
        offset = (places - first).astype(F32)
        side = side.astype(F32)
        self.row = jnp.floor((offset + 0.5) / side)
        self.col = offset - self.row * side
        self.member = member
        self.valid = (member < SLOTS).astype(F32)


def distances(tiles, m, dist, valid):
    down = Geometry(tiles, m, lax.broadcasted_iota(jnp.int32, (R, 1), 0))
    along = Geometry(tiles, m, lax.broadcasted_iota(jnp.int32, (1, R), 1))
    gap_r = down.row - along.row
    gap_c = down.col - along.col
    apart = jnp.sqrt(gap_r * gap_r + gap_c * gap_c)
    dist[...] = jnp.where(down.member == along.member, apart, 1e30)
    valid[...] = jnp.broadcast_to(down.valid, (R, 128))


def head_lanes():
    lane = lax.broadcasted_iota(jnp.int32, (1, 128), 1)
    first = (lane < HS).astype(F32)
    return first.astype(BF), (1.0 - first).astype(BF), first > 0.5, lane


class Heads:
    def __init__(self, q, k, v, o, dist, slopes, lse_lanes, lse_rows):
        self.q, self.k, self.v, self.o = q, k, v, o
        self.dist, self.slopes = dist, slopes
        self.lse_lanes, self.lse_rows = lse_lanes, lse_rows

    def at(self, place, i):
        ref, first = place
        return ref.at[:, lanes_at(first + i * 128, 128)]

    def forward(self, i):
        m0, m1, in_first, lane = head_lanes()
        q, k, v = self.at(self.q, i)[...], self.at(self.k, i)[...], self.at(self.v, i)[...]
        q = q * jnp.asarray(0.125, BF)
        parts = []
        lse = self.lse_lanes
        for j, keep in enumerate((m0, m1)):
            s = mmt(q * keep, k) - self.slopes[2 * i + j] * self.dist[...]
            top = jnp.max(s, axis=-1, keepdims=True)
            raised = jnp.exp(s - top)
            total = jnp.sum(raised, axis=-1, keepdims=True)
            parts.append(mm(raised.astype(BF), v) * (1.0 / total))
            lse[...] = jnp.where(lane == 2 * i + j, top + jnp.log(total), lse[...])
        self.at(self.o, i)[...] = jnp.where(in_first, parts[0], parts[1]).astype(BF)

    def backward(self, i):
        m0, m1, in_first, lane = head_lanes()
        q, k, v = self.at(self.q, i)[...], self.at(self.k, i)[...], self.at(self.v, i)[...]
        do = self.at(self.o, i)[...]
        q = q * jnp.asarray(0.125, BF)
        dqs, dks, dvs = [], [], []
        for j, keep in enumerate((m0, m1)):
            h = 2 * i + j
            s = mmt(k, q * keep) - self.slopes[h] * self.dist[...]
            p = jnp.exp(s - self.lse_rows[pl.ds(h, 1), :])
            dvs.append(mm(p.astype(BF), do))
            ds = (p * (mmt(v, do * keep) - self.inner[pl.ds(h, 1), :])).astype(BF)
            dks.append(mm(ds, q))
            dqs.append(tmm(ds, k))
        self.at(self.q, i)[...] = (jnp.where(in_first, dqs[0], dqs[1]) * 0.125).astype(BF)
        self.at(self.k, i)[...] = jnp.where(in_first, dks[0], dks[1]).astype(BF)
        self.at(self.v, i)[...] = jnp.where(in_first, dvs[0], dvs[1]).astype(BF)

    def prepare(self, merged, inner):
        ref, _ = self.o
        self.inner = inner
        head = lax.broadcasted_iota(jnp.int32, (16, D), 0)
        lane = lax.broadcasted_iota(jnp.int32, (16, D), 1)
        of_head = ((lane >= head * HS) & (lane < head * HS + HS)).astype(F32).astype(BF)
        product = ref[...].astype(F32) * merged[...].astype(F32)
        high = product.astype(BF)
        low = (product - high.astype(F32)).astype(BF)
        inner[...] = mmt(of_head, high) + mmt(of_head, low)

    def each(self, what, first, last):
        def step(i, carry):
            what(i)
            return carry

        lax.fori_loop(first, last, step, 0)

    def finish(self):
        self.lse_rows[...] = self.lse_lanes[...].T[:16]


class Staged:
    def __init__(self, buffers, sems):
        self.buffers, self.sems = buffers, sems
        self.count = buffers.shape[0]
        self.turn = 0
        self.flying = {}

    def put(self, value, targets):
        slot = self.turn % self.count
        self.turn += 1
        self.settle(slot)
        self.buffers[slot] = value.reshape(self.buffers.shape[1:])
        self.flying[slot] = targets
        start_all(self.copies(slot))

    def copies(self, slot):
        return [
            pltpu.make_async_copy(
                self.buffers.at[slot, :, :, :, pl.ds(first, size)], target(), self.sems.at[slot, i]
            )
            for i, (first, size, target) in enumerate(self.flying[slot])
        ]

    def settle(self, slot):
        if slot in self.flying:
            wait_all(self.copies(slot))
            self.flying.pop(slot)

    def drain(self):
        for slot in range(self.count):
            self.settle(slot)


def quarter_of(target, j):
    return [(0, D, lambda: target.at[j % 2, :, :, :, pl.ds(j // 2 * D, D)])]


def halves(target, which, first):
    return [
        (
            part * HALF,
            HALF,
            lambda part=part: target.at[which, :, :, :, pl.ds(part * D + first, HALF)],
        )
        for part in range(2)
    ]


class Vectors:
    def __init__(self, refs):
        (
            self.norm1_gain,
            self.norm1_bias,
            self.attn_bias,
            self.norm2_gain,
            self.norm2_bias,
            self.up_bias,
            self.down_bias,
            self.query_gain,
            self.query_bias,
            self.cross_bias,
        ) = list(refs[:7]) + [refs[7].at[pl.ds(i, 1)] for i in range(3)]


def column_sums(values):
    return jnp.sum(values.astype(F32), axis=0, keepdims=True)


def scaled_norm(values, gain, bias):
    normed, _ = normalize(values)
    return (normed * gain[...] + bias[...]).astype(BF)


LAYER_WEIGHTS = [
    ((4, 2, 96, 3 * D), BF),
    ((2, 2, 2, 96, D), BF),
    ((4, 2, 96, FF), BF),
    ((2, 2, 4, 2, 96, D), BF),
]
CROSS_WEIGHTS = [((4, 2, 96, D), BF), ((4, 2, 96, 2 * D), BF), ((2, 2, 2, 96, D), BF)]
CHUNKED = [
    ((4, 4, 48, 3 * D), BF),
    ((2, 2, 2, 96, D), BF),
    ((4, 4, 48, FF), BF),
    ((2, 2, 4, 2, 96, D), BF),
]
SAVED = [((R, 3 * D), BF), ((R, D), BF), ((16, R), F32), ((R, D), F32), ((R, FF), BF), ((R, FF), BF)]
EXTRA = [((R, D), BF), ((R, 2 * D), BF), ((R, D), BF), ((16, R), F32), ((R, D), F32)]
WORK = [
    ((R, D), BF),
    ((R, 128), F32),
    ((R, D), F32),
    ((D, R), BF),
    ((D, R), BF),
    ((R, R), F32),
    ((R, 128), F32),
    ((16, R), F32),
]


def flat(ref, lanes=None):
    value = ref[...] if lanes is None else ref[..., lanes]
    return value.reshape(-1, value.shape[-1])


def down_chunk(wdn, j):
    return flat(wdn.at[j // 2, j % 2])


def column_chunks():
    return [pl.ds(j * D, D) for j in range(4)]


def hidden_units(u):
    phi = 0.5 * (1.0 + lax.erf(u * 0.7071067811865476))
    return u * phi, phi + u * jnp.exp(-0.5 * u * u) * 0.3989422804014327


def own_quarter(here, values, first, out):
    half, tail = ROWS // 2, R - ROWS // 2
    columns = pl.ds(first, HALF)

    @pl.when(here.m == 0)
    def _():
        out[...] = values[pl.ds(0, half), columns]

    @pl.when(here.m == 1)
    def _():
        out[pl.ds(0, tail)] = values[pl.ds(half, tail), columns]
        out[pl.ds(tail, half - tail)] = jnp.zeros((half - tail, HALF), F32)


def padded(values, out):
    out[pl.ds(0, R)] = values[...].astype(BF)
    out[pl.ds(R, ROWS - R)] = jnp.zeros((ROWS - R, D), BF)


def forward_kernel(*refs):
    here = Place()
    tiles, slopes, radar, optical, cotangent = refs[:5]
    vecs = Vectors(refs[5:13])
    qkv_own, attn_own, up_own, down_own, cq_own, kv_own, cw_own = refs[13:20]
    refs = refs[20:]
    gathered, arrived = refs[:2]
    saved_out, refs = refs[2:8], refs[8:]
    gdn, gup, gat, gcr, vec_out, joined_own, back_own, joined_all, back_all = refs[:9]
    refs = refs[9:]
    wqkv, wo, wup, wdn, wcq, wkv, wcw = refs[:7]
    saved, refs = refs[7:13], refs[13:]
    qkv, o, lse_rows, x1, g, gp = saved
    query, pairs, merged, lse_cross, x2 = refs[:5]
    a, lse_lanes, acc, et, at, dist, valid, inner = refs[5:13]
    xin, ctx, cot, e1, e2, out_bf, staging = refs[13:20]
    link_send, link_recv, near_send, near_recv, load_sems, save_sems, stage_sems = refs[20:]
    m, oth = here.m, here.o
    first, second = pl.when(here.first), pl.when(here.second)

    peers = here.along_x[1:] + here.along_z[1:] + [here.sibling, here.partner, here.section]
    here.signal(peers)
    loads = Loads(load_sems)
    heads = Heads((qkv, 0), (qkv, D), (qkv, 2 * D), (o, 0), dist, slopes, lse_lanes, lse_rows)
    cross = Heads(
        (query, 0), (pairs, 0), (pairs, D), (merged, 0), dist, slopes, lse_lanes, lse_cross
    )
    own_qkv = loads.start(
        *[(qkv_own.at[j], wqkv.at[:, :, :, lanes_at(j * D + m * HALF, HALF)]) for j in range(3)]
    )
    own_rest = loads.start(
        (attn_own, wo.at[m]),
        (up_own, wup.at[:, :, :, lanes_at(m * HIDDEN, HIDDEN)]),
        (down_own, wdn.at[m]),
    )
    token_loads = loads.start(
        (optical.at[m, pl.ds(0, R)], ctx), (cotangent.at[m, pl.ds(0, R)], cot)
    )
    cross_own = loads.start(
        (cq_own, wcq.at[:, :, :, lanes_at(m * HALF, HALF)]), (cw_own, wcw.at[m])
    )

    i = here.dp
    links = Links(link_send, link_recv)
    block, within = i // 8, (lax.rem(i // 2, 4), lax.rem(i, 2))
    tail_lanes = lanes_at(lax.rem(i // 4, 2) * HALF, HALF)
    tail = (lax.rem(i // 2, 2), within[1], slice(None), tail_lanes)
    part = lax.rem(block, 3)
    kv_part = lax.rem(block + 1, 2)

    @second
    def _():
        for j in range(2):
            wkv[:, :, :, lanes_at(j * D + m * HALF, HALF)] = kv_own[:, j, :].reshape(4, 2, 96, HALF)

    in_head, in_query = i < 24, i < 8
    in_tail, in_pairs = i >= 24, jnp.logical_and(i >= 8, i < 24)
    kv_lanes = lanes_at(kv_part * D + m * HALF, HALF)
    rest = slice(None)
    gathers = [
        Gather(here, links, gathered, g, sources)
        for g, sources in (
            (0, [(in_head, qkv_own.at[(part,) + within]), (in_tail, attn_own.at[tail])]),
            (1, [(None, up_own.at[within + (rest, lanes_at(block * HALF, HALF))])]),
            (
                3,
                [
                    (in_query, cq_own.at[within]),
                    (in_pairs, wkv.at[within + (rest, kv_lanes)]),
                    (in_tail, cw_own.at[tail]),
                ],
            ),
        )
    ]
    across = Across(here, links, down_own, gathered, 2)
    distances(tiles, m, dist, valid)

    def project(j, part):
        lanes = lanes_at(j * D + part * HALF, HALF)
        qkv[:, lanes] = mm(a[...], flat(wqkv, lanes)).astype(BF)

    @first
    def _():
        lse_lanes[...] = jnp.zeros_like(lse_lanes)
        copy = pltpu.make_async_copy(radar.at[m, pl.ds(0, R)], xin, save_sems.at[6])
        copy.start()
        copy.wait()
        x = xin[...].astype(F32) * valid[:, :1]
        a[...] = scaled_norm(x, vecs.norm1_gain, vecs.norm1_bias)
        wait_all(own_qkv)
        for j in range(3):
            project(j, m)

    here.await_all(peers)
    for gather in gathers[:2]:
        gather.begin()

    @second
    def _():
        wait_all(cross_own)
        gathers[2].begin()

    across.begin()

    def stage(i):
        for gather in gathers[:2]:
            gather.stage(i)
        second(lambda: gathers[2].stage(i))

    for j in range(3):
        first(lambda: heads.forward(m * 3 + j))
        stage(j + 1)
    stage(4)
    gathers[0].stage(5)
    other_one = loads.start(
        *[
            (gathered.at[0, j], wqkv.at[:, :, :, lanes_at(j * D + oth * HALF, HALF)])
            for j in range(3)
        ],
        *[
            (gathered.at[0, 3, pl.ds(2 * j, 2)], wo.at[oth, :, :, :, pl.ds(j * HALF, HALF)])
            for j in range(2)
        ],
    )

    @first
    def _():
        wait_all(other_one[:3])
        for j in range(3):
            project(j, oth)

    gathers[1].stage(5)
    other_up = loads.start(
        *[
            (gathered.at[1, j], wup.at[:, :, :, lanes_at(oth * HIDDEN + j * HALF, HALF)])
            for j in range(4)
        ]
    )
    across.share()

    @first
    def _():
        heads.each(heads.forward, oth * 3, oth * 3 + 3)
        heads.finish()

    across.finish()
    other_down = loads.start(
        *[
            (
                gathered.at[2, pl.ds(2 * j, 2)],
                wdn.at[oth, :, :, :, :, pl.ds(j * HALF, HALF)],
            )
            for j in range(2)
        ]
    )

    def feed_forward(source, rows):
        a[rows] = scaled_norm(source[rows], vecs.norm2_gain, vecs.norm2_bias)
        for j, lanes in enumerate(column_chunks()):
            u = mm(a[rows], flat(wup, lanes)) + vecs.up_bias[:, lanes]
            unit, slope = hidden_units(u)
            g[rows, lanes] = unit.astype(BF)
            gp[rows, lanes] = slope.astype(BF)
            term = mm(g[rows, lanes], down_chunk(wdn, j))
            acc[rows] = term if j == 0 else acc[rows] + term

    near = (near_send, near_recv)
    blocks = [pl.ds(0, 256), pl.ds(256, R - 256)]
    forth = [remote(out_bf.at[b], xin.at[b], near, i, here.section) for i, b in enumerate(blocks)]
    back = [
        remote(out_bf.at[b], arrived.at[b], near, 2 + i, here.section)
        for i, b in enumerate(blocks)
    ]

    @first
    def _():
        saves = [
            pltpu.make_async_copy(source, target, save_sems.at[i])
            for i, (source, target) in enumerate(zip(saved, saved_out))
        ]
        for copy in saves[:3]:
            copy.start()
        wait_all(own_rest)
        wait_all(other_one[3:])
        x = xin[...].astype(F32) * valid[:, :1]
        x1[...] = x + mm(o[...], flat(wo)) + vecs.attn_bias[...]
        saves[3].start()
        wait_all(other_up)
        wait_all(other_down)
        for rows, copy in zip(blocks, forth):
            feed_forward(x1, rows)
            out_bf[rows] = (x1[rows] + acc[rows] + vecs.down_bias[...]).astype(BF)
            copy.start()
        for copy in saves[4:]:
            copy.start()
        wait_all(saves)
        wait_all(token_loads)
        wait_all(cross_own)
        for copy in forth:
            copy.wait_send()
        for copy in back:
            copy.wait_recv()

    @second
    def _():
        gathers[2].stage(5)
        pairs_cross = [(gathered.at[3, 0], wcq.at[:, :, :, lanes_at(oth * HALF, HALF)])]
        for j in range(2):
            pairs_cross += [
                (gathered.at[3, j + 1], wkv.at[:, :, :, lanes_at(j * D + oth * HALF, HALF)]),
                (
                    gathered.at[3, 3, pl.ds(2 * j, 2)],
                    wcw.at[oth, :, :, :, pl.ds(j * HALF, HALF)],
                ),
            ]
        other_cross = loads.start(*pairs_cross)
        for copies in (own_qkv, own_rest, other_one, other_up, other_down):
            wait_all(copies)
        wait_all(token_loads)
        wait_all(other_cross)
        keep = valid[:, :1]
        ctx[...] = (ctx[...].astype(F32) * keep).astype(BF)
        cot[...] = (cot[...].astype(F32) * keep).astype(BF)
        for j in range(2):
            lanes = pl.ds(j * D, D)
            pairs[:, lanes] = mm(ctx[...], flat(wkv, lanes)).astype(BF)
        lse_lanes[...] = jnp.zeros_like(lse_lanes)
        for copy in forth:
            copy.wait_recv()
        a[...] = scaled_norm(xin[...].astype(F32), vecs.norm1_gain, vecs.norm1_bias)
        for j in range(3):
            lanes = pl.ds(j * D, D)
            qkv[:, lanes] = mm(a[...], flat(wqkv, lanes)).astype(BF)
        heads.each(heads.forward, 0, H // 2)
        heads.finish()
        x1[...] = xin[...].astype(F32) + mm(o[...], flat(wo)) + vecs.attn_bias[...]
        a[...] = scaled_norm(x1[...], vecs.query_gain, vecs.query_bias)
        query[...] = mm(a[...], flat(wcq)).astype(BF)
        cross.each(cross.forward, 0, H // 2)
        cross.finish()
        x2[...] = x1[...] + mm(merged[...], flat(wcw)) + vecs.cross_bias[...]
        feed_forward(x2, pl.ds(0, R))
        acc[...] = (x2[...] + acc[...] + vecs.down_bias[...]) * keep
        own_quarter(here, acc, HALF, joined_own)
        padded(acc, joined_all)

        for j, lanes in enumerate(column_chunks()):
            gp[:, lanes] = (mmt(cot[...], down_chunk(wdn, j)) * gp[:, lanes].astype(F32)).astype(BF)
            term = mmt(gp[:, lanes], flat(wup, lanes))
            acc[...] = term if j == 0 else acc[...] + term
        vec_out[...] = jnp.zeros_like(vec_out)
        dm = acc[...]
        normed, inverse = normalize(x2[...])
        vec_out[3:4, :] = column_sums(dm * normed)
        vec_out[4:5, :] = column_sums(dm)
        acc[...] = cot[...].astype(F32) + norm_grad(dm, normed, inverse, vecs.norm2_gain[...])
        e2[...] = acc[...].astype(BF)
        a[...] = mmt(e2[...], flat(wcw)).astype(BF)
        cross_back = Heads(
            (query, 0), (pairs, 0), (pairs, D), (a, 0), dist, slopes, lse_lanes, lse_cross
        )
        cross_back.prepare(merged, inner)
        cross_back.each(cross_back.backward, 0, H // 2)
        dc = mmt(query[...], flat(wcq))
        normed, inverse = normalize(x1[...])
        vec_out[10:11, :] = column_sums(dc * normed)
        vec_out[11:12, :] = column_sums(dc)
        acc[...] = acc[...] + norm_grad(dc, normed, inverse, vecs.query_gain[...])
        e1[...] = acc[...].astype(BF)
        a[...] = mmt(e1[...], flat(wo)).astype(BF)
        self_back = Heads(
            (qkv, 0), (qkv, D), (qkv, 2 * D), (a, 0), dist, slopes, lse_lanes, lse_rows
        )
        self_back.prepare(o, inner)
        self_back.each(self_back.backward, 0, H // 2)
        sums = []
        for rows, copy in zip(blocks, back):
            da = mmt(qkv[rows], flat(wqkv))
            normed, inverse = normalize(xin[rows].astype(F32))
            sums.append((column_sums(da * normed), column_sums(da)))
            out_bf[rows] = (
                acc[rows] + norm_grad(da, normed, inverse, vecs.norm1_gain[...])
            ).astype(BF)
            copy.start()
        vec_out[0:1, :] = sums[0][0] + sums[1][0]
        vec_out[1:2, :] = sums[0][1] + sums[1][1]

        staged = Staged(staging, stage_sems)
        acc[...] = mmt(pairs[...], flat(wkv)) * keep
        own_quarter(here, acc, HALF, back_own)
        padded(acc, back_all)
        permute = chunk_order()
        et[...] = mmt(permute, e2[...]).astype(BF)
        staged.put(mm(et[...], merged[...]).astype(BF), halves(gcr, 1, HALF))
        a[...] = scaled_norm(x1[...], vecs.query_gain, vecs.query_bias)
        et[...] = mmt(permute, a[...]).astype(BF)
        staged.put(mm(et[...], query[...]).astype(BF), halves(gcr, 0, 0))
        et[...] = mmt(permute, ctx[...]).astype(BF)
        for j, target in enumerate([(0, HALF), (1, 0)]):
            staged.put(mm(et[...], pairs[:, pl.ds(j * D, D)]).astype(BF), halves(gcr, *target))
        et[...] = cot[...].T
        a[...] = scaled_norm(x2[...], vecs.norm2_gain, vecs.norm2_bias)
        at[...] = a[...].T
        for j, lanes in enumerate(column_chunks()):
            vec_out[6 + j : 7 + j, :] = column_sums(gp[:, lanes])
            staged.put(mm(et[...], g[:, lanes]).astype(BF), quarter_of(gdn, j))
            staged.put(mm(at[...], gp[:, lanes]).astype(BF), quarter_of(gup, j))
        vec_out[2:3, :] = column_sums(e1[...])
        vec_out[5:6, :] = column_sums(cot[...])
        vec_out[12:13, :] = column_sums(e2[...])
        et[...] = e1[...].T
        staged.put(mm(et[...], o[...]).astype(BF), halves(gat, 1, HALF))
        a[...] = scaled_norm(xin[...].astype(F32), vecs.norm1_gain, vecs.norm1_bias)
        at[...] = a[...].T
        for j, target in enumerate([(0, 0), (0, HALF), (1, 0)]):
            staged.put(mm(at[...], qkv[:, pl.ds(j * D, D)]).astype(BF), halves(gat, *target))
        staged.drain()
        for copy in back:
            copy.wait_send()
        gathers[2].drain()

    for gather in gathers[:2] + [across]:
        gather.drain()


def chunk_order():
    r = lax.broadcasted_iota(jnp.int32, (D, 1), 0).astype(F32)
    chunk = jnp.floor((r + 0.5) / 48.0)
    inner = r - chunk * 48.0
    core = (inner >= 24.0).astype(F32)
    inner = inner - 24.0 * core
    section = (inner >= 12.0).astype(F32)
    source = 384.0 * section + 24.0 * chunk + 12.0 * core + inner - 12.0 * section
    columns = lax.broadcasted_iota(jnp.int32, (D, D), 1).astype(F32)
    return (columns == source).astype(F32).astype(BF)


def forward(tiles, slopes, tokens, vecs, own):
    scratch = vmem(
        LAYER_WEIGHTS + CROSS_WEIGHTS + SAVED + EXTRA + WORK + [((R, D), BF)] * 6 + [((2, 4, 4, 48, D), BF)]
    )
    quarter = shape((ROWS // 2, HALF), F32)
    return pl.pallas_call(
        forward_kernel,
        out_shape=[shape((4, 4, 4, 2, 96, HALF), BF), shape((R, D), BF)]
        + [shape(*s) for s in SAVED]
        + [shape((2, 4, 4, 48, 2 * D), BF)] * 4
        + [shape((16, D), F32), quarter, quarter, shape((ROWS, D), BF), shape((ROWS, D), BF)],
        in_specs=[SM, SM] + [ANY] * 3 + [VM] * 8 + [ANY] * 5 + [VM] + [ANY],
        out_specs=[ANY] * 12 + [VM] * 5,
        scratch_shapes=scratch
        + [dma(92), dma(92), dma(4), dma(4), dma(40), dma(7), pltpu.SemaphoreType.DMA((2, 2))],
        compiler_params=pltpu.CompilerParams(
            collective_id=0, has_side_effects=True, vmem_limit_bytes=BIG
        ),
    )(tiles, slopes, *tokens, *vecs, *own)


def backward_kernel(*refs):
    here = Place()
    tiles, slopes, radar, dy_in = refs[:4]
    vecs = Vectors(refs[4:12])
    qkv_own, attn_own, up_own, down_own, gathered, gathered48 = refs[12:18]
    saved_in, refs = refs[18:24], refs[24:]
    vec_in, joined_all, back_all, gcr = refs[:4]
    refs = refs[7:]
    gdn, gup, gat, odn, oup, oat, ocr, vec_total, vec_other, radar_own, quarters, ocr_other = refs[
        :12
    ]
    refs = refs[12:]
    wqkv, wo, wup, wdn = refs[:4]
    saved, refs = refs[4:10], refs[10:]
    qkv, o, lse_rows, x1, g, gp = saved
    a, lse_lanes, acc, et, at, dist, valid, inner = refs[:8]
    xin, radar_all, staging, vec, vbuf = refs[8:13]
    out_bf = radar_all.at[pl.ds(0, R)]
    own_at, cross_sums = refs[13:15]
    buffers, refs = [refs[15 + 7 * i : 22 + 7 * i] for i in range(4)], refs[43:]
    link_send, link_recv, far_send, far_recv, load_sems, local_sems, stage_sems = refs
    m, oth = here.m, here.o
    first, second = pl.when(here.first), pl.when(here.second)
    peers = here.ring + [
        here.sibling,
        here.partner,
        here.diagonal,
        here.along_x[2],
        here.along_z[2],
        here.section,
        here.crossed,
    ]
    here.signal(peers)
    loads = Loads(load_sems)
    links = Links(link_send, link_recv)
    far = (far_send, far_recv)
    staged = Staged(staging, stage_sems)
    heads = Heads((qkv, 0), (qkv, D), (qkv, 2 * D), (a, 0), dist, slopes, lse_lanes, lse_rows)
    chunks = column_chunks()

    cotangent = loads.prepare((dy_in, out_bf))
    units = [loads.prepare((saved_in[4].at[:, c], g.at[j % 2])) for j, c in enumerate(chunks)]
    early = loads.prepare((saved_in[3], x1), (radar.at[m, pl.ds(0, R)], xin))
    copies_down = loads.prepare(
        (down_own, wdn.at[m]),
        *[
            (gathered.at[2, pl.ds(2 * j, 2)], wdn.at[oth, :, :, :, :, pl.ds(j * HALF, HALF)])
            for j in range(2)
        ],
    )
    slopes_of = [loads.prepare((saved_in[5].at[:, c], gp.at[:, c])) for c in chunks]
    copies_up = loads.prepare(
        (up_own, wup.at[:, :, :, lanes_at(m * HIDDEN, HIDDEN)]),
        *[
            (gathered48.at[1, j], wup.at[:, :, :, lanes_at(oth * HIDDEN + j * HALF, HALF)])
            for j in range(4)
        ],
    )
    late = loads.prepare(
        (saved_in[0], qkv),
        (saved_in[1], o),
        (saved_in[2], lse_rows),
        (attn_own, wo.at[m]),
        *[
            (gathered.at[0, 3, pl.ds(2 * j, 2)], wo.at[oth, :, :, :, pl.ds(j * HALF, HALF)])
            for j in range(2)
        ],
    )
    copies_qkv = loads.prepare(
        *[(qkv_own.at[j], wqkv.at[:, :, :, lanes_at(j * D + m * HALF, HALF)]) for j in range(3)],
        *[
            (gathered48.at[0, j], wqkv.at[:, :, :, lanes_at(j * D + oth * HALF, HALF)])
            for j in range(3)
        ],
    )

    @first
    def _():
        for copies in [cotangent] + units[:2] + [early, copies_down] + slopes_of + [copies_up, late]:
            start_all(copies)
        distances(tiles, m, dist, valid)
        vec[...] = jnp.zeros_like(vec)
        wait_all(cotangent)
        e3 = out_bf[...]
        vec[5:6, :] = column_sums(e3)
        et[...] = e3.T
        for j in range(4):
            wait_all(units[j])
            staged.put(mm(et[...], g[j % 2]).astype(BF), quarter_of(gdn, j))
            if j < 2:
                start_all(units[j + 2])
        staged.drain()

    @second
    def _():
        vec[...] = vec_in[...]

    here.await_all(peers)
    low, high = pl.ds(0, 2 * D), pl.ds(2 * D, 2 * D)
    dn = scatter_stages(
        here, links, local_sems.at[0], gdn, odn, wqkv.at[:, :, :, low], buffers[0]
    )
    up = scatter_stages(here, links, local_sems.at[1], gup, oup, wup.at[:, :, :, low], buffers[1])
    mid = scatter_stages(here, links, local_sems.at[2], gat, oat, own_at, buffers[2])
    cross = scatter_stages(
        here, links, local_sems.at[3], gcr, cross_sums, wup.at[:, :, :, high], buffers[3]
    )
    vec_steps = vector_stages(here, links, vec, vbuf, vec_total)

    def quarter_copies(source, kind):
        half_rows = ROWS // 2
        mine, others = rows_at(m * half_rows, half_rows), rows_at(oth * half_rows, half_rows)
        sender, receiver = (0, 1) if kind == 2 else (1, 0)
        same = pl.ds(sender * HALF, HALF)
        over = pl.ds(receiver * HALF, HALF)
        return [
            remote(source.at[mine, over], quarters.at[kind, 0], far, 3 * kind, here.section),
            remote(source.at[others, over], quarters.at[kind, 1], far, 3 * kind + 1, here.crossed),
            remote(source.at[others, same], quarters.at[kind, 1], far, 3 * kind + 2, here.partner),
        ]

    sent = [quarter_copies(s, i) for i, s in enumerate((joined_all, back_all, radar_all))]
    cross_sent = remote(ocr.at[0], ocr_other, far, 9, here.section)
    vec_sent = remote(vec_total, vec_other, far, 10, here.section)

    @second
    def _():
        for copies in sent[:2]:
            for copy in copies:
                copy.start()
        cross[0]()

    dn[0]()
    second(cross[1])

    def chain(j):
        lanes = chunks[j]
        wait_all(slopes_of[j])
        du = (mmt(out_bf[...], down_chunk(wdn, j)) * gp[:, lanes].astype(F32)).astype(BF)
        gp[:, lanes] = du
        vec[6 + j : 7 + j, :] = column_sums(du)
        staged.put(mm(at[...], gp[:, lanes]).astype(BF), quarter_of(gup, j))
        if j == 0:
            wait_all(copies_up)
        term = mmt(gp[:, lanes], flat(wup, lanes))
        acc[...] = term if j == 0 else acc[...] + term

    @first
    def _():
        wait_all(early)
        a[...] = scaled_norm(x1[...], vecs.norm2_gain, vecs.norm2_bias)
        at[...] = a[...].T
        wait_all(copies_down)
        chain(0)
        chain(1)

    dn[1]()

    @first
    def _():
        chain(2)
        chain(3)
        staged.drain()
        wait_all(late)

    up[0]()
    second(cross[2])
    dn[2]()

    @first
    def _():
        dm = acc[...]
        normed, inverse = normalize(x1[...])
        vec[3:4, :] = column_sums(dm * normed)
        vec[4:5, :] = column_sums(dm)
        acc[...] = out_bf[...].astype(F32) + norm_grad(dm, normed, inverse, vecs.norm2_gain[...])
        e1 = acc[...].astype(BF)
        vec[2:3, :] = column_sums(e1)
        out_bf[...] = e1
        a[...] = mmt(out_bf[...], flat(wo)).astype(BF)
        heads.prepare(o, inner)

    up[1]()
    second(cross[3])

    @first
    def _():
        et[...] = out_bf[...].T
        staged.put(mm(et[...], o[...]).astype(BF), halves(gat, 1, HALF))
        heads.backward(0)

    dn[3]()
    first(lambda: heads.each(heads.backward, 1, 3))
    up[2]()
    second(cross[4])
    dn[4]()
    first(lambda: heads.backward(3))
    up[3]()
    dn[5]()
    second(cross[5])

    @first
    def _():
        start_all(copies_qkv)
        heads.each(heads.backward, 4, 6)

    up[4]()

    @first
    def _():
        x = xin[...].astype(F32) * valid[:, :1]
        a[...] = scaled_norm(x, vecs.norm1_gain, vecs.norm1_bias)
        at[...] = a[...].T
        for j, target in enumerate([(0, 0), (0, HALF), (1, 0)]):
            staged.put(mm(at[...], qkv[:, pl.ds(j * D, D)]).astype(BF), halves(gat, *target))
        staged.drain()
        wait_all(copies_qkv)

    mid[0]()

    @first
    def _():
        da = mmt(qkv[...], flat(wqkv))
        normed, inverse = normalize(xin[...].astype(F32) * valid[:, :1])
        vec[0:1, :] = column_sums(da * normed)
        vec[1:2, :] = column_sums(da)
        acc[...] = (acc[...] + norm_grad(da, normed, inverse, vecs.norm1_gain[...])) * valid[:, :1]
        own_quarter(here, acc, 0, radar_own)
        padded(acc, radar_all)
        for copy in sent[2]:
            copy.start()

    @second
    def _():
        for section in range(2):
            for which in range(2):
                ocr[section, which] = cross_sums[which][section * 12 : section * 12 + 12]
        cross_sent.start()

    vec_steps[0]()
    mid[1]()
    vec_steps[1]()
    up[5]()
    mid[2]()
    vec_steps[2]()
    mid[3]()
    vec_steps[3]()
    mid[4]()
    vec_steps[4]()

    @second
    def _():
        vec_sent.start()

    mid[5]()

    @first
    def _():
        for copies in sent[:2]:
            copies[0].wait_recv()
            copies[1].wait_recv()
        sent[2][2].wait_recv()
        for copy in sent[2]:
            copy.wait_send()
        cross_sent.wait_recv()
        vec_sent.wait_recv()

    @second
    def _():
        sent[2][0].wait_recv()
        sent[2][1].wait_recv()
        for copies in sent[:2]:
            copies[2].wait_recv()
            for copy in copies:
                copy.wait_send()
        cross_sent.wait_send()
        vec_sent.wait_send()


def backward(tiles, slopes, radar, dy, vecs, own, gathered, saved, vec, quarters, gcr, grads):
    scratch = vmem(
        CHUNKED
        + SAVED[:4]
        + [((2, R, D), BF)]
        + SAVED[5:]
        + WORK
        + [((R, D), BF), ((ROWS, D), BF)]
        + [((2, 4, 4, 48, D), BF), ((16, D), F32), ((8, 16, D), F32)]
    )
    vector = shape((16, D), F32)
    qkv, attn, up, down = own
    return pl.pallas_call(
        backward_kernel,
        out_shape=[
            *[shape(array.shape, BF) for array in grads],
            *[shape((2, 24, D), F32)] * 3,
            shape((2, 2, 12, D), F32),
            vector,
            vector,
            shape((ROWS // 2, HALF), F32),
            shape((3, 2, ROWS // 2, HALF), BF),
            shape((2, 12, D), F32),
        ],
        in_specs=[SM, SM, ANY, ANY] + [VM] * 8 + [ANY] * 12 + [VM] + [ANY] * 6,
        out_specs=[ANY] * 3 + [VM] * 7 + [ANY, VM],
        input_output_aliases={28: 0, 29: 1, 30: 2},
        scratch_shapes=scratch
        + own_scratch(2 * D)
        + [pltpu.VMEM((2, 24, D), F32)]
        + scatter_scratch(2 * D) * 4
        + [dma(124), dma(124), dma(11), dma(11), dma(40), dma(4), pltpu.SemaphoreType.DMA((2, 2))],
        compiler_params=pltpu.CompilerParams(
            collective_id=1, has_side_effects=True, vmem_limit_bytes=BIG
        ),
    )(
        tiles,
        slopes,
        radar,
        dy,
        *vecs,
        qkv.reshape(3, 4, 4, 48, HALF),
        attn,
        up.reshape(4, 4, 48, HIDDEN),
        down,
        gathered,
        gathered.reshape(4, 4, 4, 4, 48, HALF),
        *saved,
        vec,
        *quarters,
        gcr,
        *grads,
    )


def local(
    radar_tokens,
    optical_tokens,
    out_cotangent,
    tile_sides,
    norm1_gain,
    norm1_bias,
    qkv_weight,
    attn_weight,
    attn_bias,
    norm2_gain,
    norm2_bias,
    up_weight,
    up_bias,
    down_weight,
    down_bias,
    query_gain,
    query_bias,
    cross_query,
    cross_keyval,
    cross_weight,
    cross_bias,
):
    m = lax.axis_index("mp")
    joining = lax.axis_index("pipe") == 1
    slopes = jnp.exp2(-8.0 * (jnp.arange(H, dtype=jnp.int32) + 1).astype(F32) / H)
    vecs = (
        norm1_gain,
        norm1_bias,
        attn_bias,
        norm2_gain,
        norm2_bias,
        up_bias,
        down_bias,
        jnp.stack([query_gain, query_bias, cross_bias]),
    )
    own = (
        qkv_weight[0].transpose(1, 0, 2).reshape(3, 4, 2, 96, HALF),
        attn_weight.reshape(2, 2, 96, D),
        up_weight.reshape(4, 2, 96, HIDDEN),
        down_weight.reshape(2, 4, 2, 96, D),
    )
    cross_own = (
        cross_query.reshape(4, 2, 96, HALF),
        cross_keyval,
        cross_weight.reshape(2, 2, 96, D),
    )
    tokens = (radar_tokens, optical_tokens, out_cotangent)
    results = forward(
        tile_sides, slopes, tokens, vecs, own + cross_own
    )
    gathered, dy0 = results[:2]
    saved = results[2:8]
    grads = results[8:11]
    gcr, vec, joined_own, back_own, joined_all, back_all = results[11:]
    outs = backward(
        tile_sides,
        slopes,
        radar_tokens,
        dy0,
        vecs,
        own,
        gathered,
        saved,
        vec,
        (joined_all, back_all),
        gcr,
        grads,
    )
    odn, oup, oat, ocr, vec, vec_other, radar_own, quarters, ocr_other = outs[3:]

    def placed(own_quarter, kind, here):
        mine = jnp.where(here, own_quarter, quarters[kind, 0].astype(F32))
        others = quarters[kind, 1].astype(F32)
        swap = m == 1
        return jnp.stack([jnp.where(swap, others, mine), jnp.where(swap, mine, others)])

    crossed = jnp.where(joining, vec[10:13], vec_other[10:13])
    ocr = jnp.where(joining, ocr[1], ocr_other)
    q, k = oat[0, :, :HALF], oat[0, :, HALF:]
    v, attn = oat[1, :, :HALF], oat[1, :, HALF:]
    cq, ck = ocr[0, :, :HALF], ocr[0, :, HALF:]
    cv, cw = ocr[1, :, :HALF], ocr[1, :, HALF:]
    return (
        placed(joined_own, 0, joining),
        placed(radar_own, 2, jnp.logical_not(joining)),
        placed(back_own, 1, joining),
        vec[0:1],
        vec[1:2],
        jnp.stack([q, k, v], axis=1)[None],
        attn.T[None],
        vec[2:3],
        vec[3:4],
        vec[4:5],
        jnp.concatenate([oup[0], oup[1]], axis=1)[None],
        vec[6:10].reshape(1, FF),
        jnp.concatenate([odn[0].T, odn[1].T])[None],
        vec[5:6],
        crossed[0],
        crossed[1],
        cq,
        jnp.stack([ck, cv], axis=1),
        cw.T,
        crossed[2],
    )


def solution(mesh):
    in_specs = (
        P(None, "dp", None),
        P(None, "dp", None),
        P(None, "dp", None),
        P(None, "dp"),
        P("pipe", None),
        P("pipe", None),
        P("pipe", None, None, "mp"),
        P("pipe", "mp", None),
        P("pipe", None),
        P("pipe", None),
        P("pipe", None),
        P("pipe", None, "mp"),
        P("pipe", None),
        P("pipe", "mp", None),
        P("pipe", None),
        P(),
        P(),
        P(None, "mp"),
        P(None, None, "mp"),
        P("mp", None),
        P(),
    )
    out_specs = (
        P(None, ("dp", "mp"), "pipe"),
        P(None, ("dp", "mp"), "pipe"),
        P(None, ("dp", "mp"), "pipe"),
        P("pipe", None),
        P("pipe", None),
        P("pipe", "dp", None, "mp"),
        P("pipe", "mp", "dp"),
        P("pipe", None),
        P("pipe", None),
        P("pipe", None),
        P("pipe", "dp", "mp"),
        P("pipe", None),
        P("pipe", "mp", "dp"),
        P("pipe", None),
        P(),
        P(),
        P(("pipe", "dp"), "mp"),
        P(("pipe", "dp"), None, "mp"),
        P("mp", ("pipe", "dp")),
        P(),
    )
    return jax.shard_map(local, mesh=mesh, in_specs=in_specs, out_specs=out_specs, check_vma=False)
```

```python
import jax
import jax.numpy as jnp
from jax import lax
from jax.experimental import pallas as pl
from jax.experimental.pallas import tpu as pltpu
from jax.sharding import PartitionSpec as P

H = 12
HS = 64
D = 768
FF = 3072
ROWS = 512
R = 464
HALF = D // 2
HIDDEN = FF // 2
SLOTS = 3
EPSILON = 1e-05
BF = jnp.bfloat16
F32 = jnp.float32
ANY = pl.BlockSpec(memory_space=pl.ANY)
VM = pl.BlockSpec(memory_space=pltpu.VMEM)
SM = pl.BlockSpec(memory_space=pltpu.SMEM)
MESH = pl.DeviceIdType.MESH
BIG = 62 * 1024 * 1024


def shape(dims, kind):
    return jax.ShapeDtypeStruct(dims, kind)


def vmem(shapes):
    return [pltpu.VMEM(dims, kind) for dims, kind in shapes]


def dma(count):
    return pltpu.SemaphoreType.DMA((count,))


class Place:
    def __init__(self):
        dp = lax.axis_index("dp")
        self.dp = dp
        self.pipe = lax.axis_index("pipe")
        self.m = lax.axis_index("mp")
        self.o = 1 - self.m
        self.core = lax.rem(dp, 2)
        self.twin = 1 - self.core
        chip = dp // 2
        self.x = lax.rem(chip, 4)
        self.z = chip // 4
        self.xs = [self.x] + [lax.rem(self.x + i, 4) for i in (1, 2, 3)]
        self.zs = [self.z] + [lax.rem(self.z + i, 4) for i in (1, 2, 3)]
        self.along_x = [self.at(self.z, x, self.core) for x in self.xs]
        self.along_z = [self.at(z, self.x, self.core) for z in self.zs]
        self.sibling = self.at(self.z, self.x, self.twin)
        self.partner = {"mp": self.o}
        self.section = {"pipe": 1 - self.pipe}
        self.crossed = {"pipe": 1 - self.pipe, "mp": self.o}
        self.diagonal = dict(self.sibling, mp=self.o)
        self.ring = [self.along_x[1], self.along_x[3], self.along_z[1], self.along_z[3]]
        self.first = self.pipe == 0
        self.second = self.pipe == 1

    def at(self, z, x, core):
        return {"dp": (z * 4 + x) * 2 + core}

    def signal(self, devices):
        barrier = pltpu.get_barrier_semaphore()
        for device in devices:
            pl.semaphore_signal(barrier, inc=1, device_id=device, device_id_type=MESH)

    def await_all(self, devices):
        pl.semaphore_wait(pltpu.get_barrier_semaphore(), len(devices))


def remote(source, target, sems, i, device):
    return pltpu.make_async_remote_copy(
        src_ref=source,
        dst_ref=target,
        send_sem=sems[0].at[i],
        recv_sem=sems[1].at[i],
        device_id=device,
        device_id_type=MESH,
    )


class Links:
    def __init__(self, *sems):
        self.sems = sems
        self.used = 0

    def prepare(self, source, target, device):
        copy = remote(source, target, self.sems, self.used, device)
        self.used += 1
        return copy


class Loads:
    def __init__(self, sems):
        self.sems = sems
        self.used = 0

    def prepare(self, *pairs):
        copies = []
        for source, target in pairs:
            copies.append(pltpu.make_async_copy(source, target, self.sems.at[self.used]))
            self.used += 1
        return copies

    def start(self, *pairs):
        return start_all(self.prepare(*pairs))


def start_all(copies):
    for copy in copies:
        copy.start()
    return copies


def wait_all(copies):
    for copy in copies:
        copy.wait()


def lanes_at(first, size):
    return pl.ds(pl.multiple_of(first, 128), size)


def rows_at(first, size):
    return pl.ds(pl.multiple_of(first, 16), size)


class Gather:
    def __init__(self, here, links, out, g, sources):
        c, x, z = here.core, here.x, here.z
        xs, zs = here.xs, here.zs
        right, left, up, down = here.ring
        a, b = pl.ds(0, 48), pl.ds(48, 48)
        low, high = pl.ds(0, 2), pl.ds(2, 2)
        at = links.used
        self.begins = [
            (condition, remote(source, out.at[g, z, x, c], links.sems, at, here.partner))
            for condition, source in sources
        ]
        links.used = at + 1

        def same(view, device):
            return links.prepare(view, view, device)

        direct, early = [], []
        for j in (2, 1, 3):
            direct.append(same(out.at[g, z, x, c, a], here.along_x[j]))
            direct.append(same(out.at[g, z, x, c, b], here.along_z[j]))
        for j in (0, 1, 3):
            early.append(same(out.at[g, zs[j], :, c, a], here.sibling))
            early.append(same(out.at[g, :, xs[j], c, b], here.sibling))
        near = [
            same(out.at[g, z, :, c, a], up),
            same(out.at[g, z, :, c, a], down),
            same(out.at[g, :, x, c, b], right),
            same(out.at[g, :, x, c, b], left),
        ]
        relayed = [
            same(out.at[g, zs[3], low, c, a], up),
            same(out.at[g, zs[1], high, c, a], down),
            same(out.at[g, low, xs[3], c, b], right),
            same(out.at[g, high, xs[1], c, b], left),
        ]
        late = [
            same(out.at[g, zs[2], :, c, a], here.sibling),
            same(out.at[g, :, xs[2], c, b], here.sibling),
        ]
        first = [self.begins[-1][1]]
        self.waits = [[], first, direct, near, relayed, early + late]
        self.starts = [[], direct, near, relayed + early, late, []]
        self.all = first + direct + near + relayed + early + late

    def begin(self):
        for condition, copy in self.begins:
            if condition is None:
                copy.start()
            else:
                pl.when(condition)(copy.start)

    def stage(self, i):
        for copy in self.waits[i]:
            copy.wait_recv()
        for copy in self.starts[i]:
            copy.start()

    def drain(self):
        for copy in self.all:
            copy.wait_send()


class Across:
    def __init__(self, here, links, own, out, g):
        c = here.core
        spans = [pl.ds(2 * j, 2) for j in range(2)]
        self.copies = [
            links.prepare(
                own.at[:, :, c, :, pl.ds(j * HALF, HALF)], out.at[g, span, :, c], here.partner
            )
            for j, span in enumerate(spans)
        ]
        self.shared = [
            links.prepare(out.at[g, span, :, c], out.at[g, span, :, c], here.sibling)
            for span in spans
        ]

    def begin(self):
        start_all(self.copies)

    def share(self):
        for copy, onward in zip(self.copies, self.shared):
            copy.wait_recv()
            onward.start()

    def finish(self):
        for copy in self.shared:
            copy.wait_recv()

    def drain(self):
        for copy in self.copies + self.shared:
            copy.wait_send()


def vector_stages(here, links, vec, vbuf, total):
    rounds = [[here.sibling], here.along_x[1:], here.along_z[1:], [here.partner]]
    copies, used = [], 0
    for devices in rounds:
        copies.append(
            [links.prepare(total, vbuf.at[used + i], d) for i, d in enumerate(devices)]
        )
        used += len(devices)

    def begin(i):
        def stage():
            if i == 0:
                total[...] = vec[...]
            else:
                first = sum(len(devices) for devices in rounds[: i - 1])
                for copy in copies[i - 1]:
                    copy.wait()
                value = total[...]
                for j in range(len(rounds[i - 1])):
                    value = value + vbuf[first + j]
                total[...] = value
            if i < len(rounds):
                for copy in copies[i]:
                    copy.start()

        return stage

    return [begin(i) for i in range(len(rounds) + 1)]


def scatter_scratch(cols):
    half = cols // 2
    return [
        pltpu.VMEM((4, 4, 48, cols), BF),
        pltpu.VMEM((2, 2, 2, 48, half), BF),
        pltpu.VMEM((2, 2, 4, 48, half), BF),
        pltpu.VMEM((2, 4, 48, half), BF),
        pltpu.VMEM((2, 3, 48, half), BF),
        pltpu.VMEM((2, 2, 24, half), F32),
        pltpu.VMEM((3, 24, half), F32),
    ]


def scatter_stages(here, links, local_sem, grads, out, own, buffers):
    other, far, near, mid, near2, late, last = buffers
    cols = own.shape[-1]
    half = cols // 2
    c, twin, m, o = here.core, here.twin, here.m, here.o
    xs, zs = here.xs, here.zs
    lanes = [pl.ds(0, half), pl.ds(half, half)]
    low, high = pl.ds(0, 2), pl.ds(2, 2)
    ahead = [here.along_x[1], here.along_z[1]]
    behind = [here.along_x[3], here.along_z[3]]

    def block(ref, way, j):
        if way == 0:
            return ref.at[:, xs[j], :, lanes[0]]
        return ref.at[zs[j], :, :, lanes[1]]

    def part(ref, way, j, span):
        if way == 0:
            return ref.at[span, xs[j], :, lanes[0]]
        return ref.at[zs[j], span, :, lanes[1]]

    def places(way):
        return zs if way == 0 else xs

    order = [(way, j) for j in (2, 1, 3, 0) for way in range(2)]
    local = pltpu.make_async_copy(grads.at[c], own, local_sem)
    exchange = {
        (way, j): links.prepare(
            block(grads.at[twin], way, j), block(other, way, j), here.sibling
        )
        for way, j in order
    }
    one, two, three = [], [], []
    for way in range(2):
        turn = 1 - way
        at = places(way)
        one.append(
            [
                links.prepare(part(own, way, 2, low), far.at[way, 0], ahead[way]),
                links.prepare(part(own, way, 2, high), far.at[way, 1], behind[way]),
                links.prepare(part(own, way, 1, high), near.at[way, 0, high], ahead[way]),
                links.prepare(part(own, way, 3, low), near.at[way, 1, low], behind[way]),
            ]
        )
        two.append(
            [
                links.prepare(part(own, way, 1, low), near.at[way, 0, low], ahead[way]),
                links.prepare(part(own, way, 3, high), near.at[way, 1, high], behind[way]),
            ]
        )
        axis = (here.along_x, here.along_z)[turn]
        three.append(
            [
                links.prepare(mid.at[way, at[j]], near2.at[way, j - 1], axis[j])
                for j in (2, 1, 3)
            ]
        )
    ending = [
        links.prepare(late.at[m, twin], last.at[0], here.sibling),
        links.prepare(late.at[o, c], last.at[1], here.partner),
        links.prepare(late.at[o, twin], last.at[2], here.diagonal),
    ]

    def start():
        local.start()
        for key in order:
            exchange[key].start()

    def add_other(way, j):
        exchange[way, j].wait_recv()
        mine, theirs = block(own, way, j), block(other, way, j)
        for i in range(4):
            mine[i] = mine[i] + theirs[i]

    def ring_one():
        local.wait()
        for way in range(2):
            add_other(way, 2)
            one[way][0].start()
            one[way][1].start()
        for way in range(2):
            add_other(way, 1)
            one[way][2].start()
            add_other(way, 3)
            one[way][3].start()
        for way in range(2):
            add_other(way, 0)

    def ring_two():
        for way in range(2):
            one[way][0].wait_recv()
            target = part(own, way, 1, low)
            for i in range(2):
                target[i] = target[i] + far[way, 0, i]
            two[way][0].start()
            one[way][1].wait_recv()
            target = part(own, way, 3, high)
            for i in range(2):
                target[i] = target[i] + far[way, 1, i]
            two[way][1].start()

    def ring_three():
        for way in range(2):
            for copy in one[way][2:] + two[way]:
                copy.wait_recv()
            mine = block(own, way, 0)
            for i in range(4):
                mid[way, i] = (
                    mine[i].astype(F32) + near[way, 0, i].astype(F32) + near[way, 1, i].astype(F32)
                ).astype(BF)
            for copy in three[way]:
                copy.start()
        for step in one + two:
            for copy in step:
                copy.wait_send()

    def to_owners():
        for way in range(2):
            for copy in three[way]:
                copy.wait_recv()
            total = mid[way, places(way)[0]].astype(F32)
            for j in range(3):
                total = total + near2[way, j].astype(F32)
            late[way, 0] = total[:24]
            late[way, 1] = total[24:]
        for copy in ending:
            copy.start()

    def finish():
        for copy in ending:
            copy.wait_recv()
        out[c] = late[m, c] + last[1]
        out[twin] = last[0] + last[2]
        for key in order:
            exchange[key].wait_send()
        for step in three + [ending]:
            for copy in step:
                copy.wait_send()

    return [start, ring_one, ring_two, ring_three, to_owners, finish]


def own_scratch(cols):
    return [pltpu.VMEM((4, 4, 48, cols), BF)]


def mm(a, b):
    return lax.dot_general(a, b, (((1,), (0,)), ((), ())), preferred_element_type=F32)


def mmt(a, b):
    return lax.dot_general(a, b, (((1,), (1,)), ((), ())), preferred_element_type=F32)


def tmm(a, b):
    return lax.dot_general(a, b, (((0,), (0,)), ((), ())), preferred_element_type=F32)


def normalize(values):
    centered = values - jnp.mean(values, axis=-1, keepdims=True)
    inverse = lax.rsqrt(jnp.mean(centered * centered, axis=-1, keepdims=True) + EPSILON)
    return centered * inverse, inverse


def norm_grad(upstream, normed, inverse, gain):
    scaled = upstream * gain
    return inverse * (
        scaled
        - jnp.mean(scaled, axis=-1, keepdims=True)
        - normed * jnp.mean(scaled * normed, axis=-1, keepdims=True)
    )


class Geometry:
    def __init__(self, tiles, m, places):
        starts, member = [0], jnp.zeros_like(places)
        for slot in range(SLOTS):
            side = tiles[m, slot]
            starts.append(starts[-1] + side * side)
            member = member + (places >= starts[-1]).astype(jnp.int32)
        first, side = jnp.zeros_like(places), jnp.ones_like(places)
        for slot in range(SLOTS):
            here = member == slot
            first = jnp.where(here, starts[slot], first)
            side = jnp.where(here, jnp.maximum(tiles[m, slot], 1), side)
        first = jnp.where(member == SLOTS, starts[SLOTS], first)
        offset = (places - first).astype(F32)
        side = side.astype(F32)
        self.row = jnp.floor((offset + 0.5) / side)
        self.col = offset - self.row * side
        self.member = member
        self.valid = (member < SLOTS).astype(F32)


def distances(tiles, m, dist, valid):
    down = Geometry(tiles, m, lax.broadcasted_iota(jnp.int32, (R, 1), 0))
    along = Geometry(tiles, m, lax.broadcasted_iota(jnp.int32, (1, R), 1))
    gap_r = down.row - along.row
    gap_c = down.col - along.col
    apart = jnp.sqrt(gap_r * gap_r + gap_c * gap_c)
    dist[...] = jnp.where(down.member == along.member, apart, 1e30)
    valid[...] = jnp.broadcast_to(down.valid, (R, 128))


def head_lanes():
    lane = lax.broadcasted_iota(jnp.int32, (1, 128), 1)
    first = (lane < HS).astype(F32)
    return first.astype(BF), (1.0 - first).astype(BF), first > 0.5, lane


class Heads:
    def __init__(self, q, k, v, o, dist, slopes, lse_lanes, lse_rows):
        self.q, self.k, self.v, self.o = q, k, v, o
        self.dist, self.slopes = dist, slopes
        self.lse_lanes, self.lse_rows = lse_lanes, lse_rows

    def at(self, place, i):
        ref, first = place
        return ref.at[:, lanes_at(first + i * 128, 128)]

    def forward(self, i):
        m0, m1, in_first, lane = head_lanes()
        q, k, v = self.at(self.q, i)[...], self.at(self.k, i)[...], self.at(self.v, i)[...]
        q = q * jnp.asarray(0.125, BF)
        parts = []
        lse = self.lse_lanes
        for j, keep in enumerate((m0, m1)):
            s = mmt(q * keep, k) - self.slopes[2 * i + j] * self.dist[...]
            top = jnp.max(s, axis=-1, keepdims=True)
            raised = jnp.exp(s - top)
            total = jnp.sum(raised, axis=-1, keepdims=True)
            parts.append(mm(raised.astype(BF), v) * (1.0 / total))
            lse[...] = jnp.where(lane == 2 * i + j, top + jnp.log(total), lse[...])
        self.at(self.o, i)[...] = jnp.where(in_first, parts[0], parts[1]).astype(BF)

    def backward(self, i):
        m0, m1, in_first, lane = head_lanes()
        q, k, v = self.at(self.q, i)[...], self.at(self.k, i)[...], self.at(self.v, i)[...]
        do = self.at(self.o, i)[...]
        q = q * jnp.asarray(0.125, BF)
        dqs, dks, dvs = [], [], []
        for j, keep in enumerate((m0, m1)):
            h = 2 * i + j
            s = mmt(k, q * keep) - self.slopes[h] * self.dist[...]
            p = jnp.exp(s - self.lse_rows[pl.ds(h, 1), :])
            dvs.append(mm(p.astype(BF), do))
            ds = (p * (mmt(v, do * keep) - self.inner[pl.ds(h, 1), :])).astype(BF)
            dks.append(mm(ds, q))
            dqs.append(tmm(ds, k))
        self.at(self.q, i)[...] = (jnp.where(in_first, dqs[0], dqs[1]) * 0.125).astype(BF)
        self.at(self.k, i)[...] = jnp.where(in_first, dks[0], dks[1]).astype(BF)
        self.at(self.v, i)[...] = jnp.where(in_first, dvs[0], dvs[1]).astype(BF)

    def prepare(self, merged, inner):
        ref, _ = self.o
        self.inner = inner
        head = lax.broadcasted_iota(jnp.int32, (16, D), 0)
        lane = lax.broadcasted_iota(jnp.int32, (16, D), 1)
        of_head = ((lane >= head * HS) & (lane < head * HS + HS)).astype(F32).astype(BF)
        product = ref[...].astype(F32) * merged[...].astype(F32)
        high = product.astype(BF)
        low = (product - high.astype(F32)).astype(BF)
        inner[...] = mmt(of_head, high) + mmt(of_head, low)

    def each(self, what, first, last):
        def step(i, carry):
            what(i)
            return carry

        lax.fori_loop(first, last, step, 0)

    def finish(self):
        self.lse_rows[...] = self.lse_lanes[...].T[:16]


class Staged:
    def __init__(self, buffers, sems):
        self.buffers, self.sems = buffers, sems
        self.count = buffers.shape[0]
        self.turn = 0
        self.flying = {}

    def put(self, value, targets):
        slot = self.turn % self.count
        self.turn += 1
        self.settle(slot)
        self.buffers[slot] = value.reshape(self.buffers.shape[1:])
        self.flying[slot] = targets
        start_all(self.copies(slot))

    def copies(self, slot):
        return [
            pltpu.make_async_copy(
                self.buffers.at[slot, :, :, :, pl.ds(first, size)], target(), self.sems.at[slot, i]
            )
            for i, (first, size, target) in enumerate(self.flying[slot])
        ]

    def settle(self, slot):
        if slot in self.flying:
            wait_all(self.copies(slot))
            self.flying.pop(slot)

    def drain(self):
        for slot in range(self.count):
            self.settle(slot)


def quarter_of(target, j):
    return [(0, D, lambda: target.at[j % 2, :, :, :, pl.ds(j // 2 * D, D)])]


def halves(target, which, first):
    return [
        (
            part * HALF,
            HALF,
            lambda part=part: target.at[which, :, :, :, pl.ds(part * D + first, HALF)],
        )
        for part in range(2)
    ]


class Vectors:
    def __init__(self, refs):
        (
            self.norm1_gain,
            self.norm1_bias,
            self.attn_bias,
            self.norm2_gain,
            self.norm2_bias,
            self.up_bias,
            self.down_bias,
            self.query_gain,
            self.query_bias,
            self.cross_bias,
        ) = refs


def column_sums(values):
    return jnp.sum(values.astype(F32), axis=0, keepdims=True)


def scaled_norm(values, gain, bias):
    normed, _ = normalize(values)
    return (normed * gain[...] + bias[...]).astype(BF)


LAYER_WEIGHTS = [
    ((4, 2, 96, 3 * D), BF),
    ((2, 2, 2, 96, D), BF),
    ((4, 2, 96, FF), BF),
    ((2, 2, 4, 2, 96, D), BF),
]
CROSS_WEIGHTS = [((4, 2, 96, D), BF), ((4, 2, 96, 2 * D), BF), ((2, 2, 2, 96, D), BF)]
CHUNKED = [
    ((4, 4, 48, 3 * D), BF),
    ((2, 2, 2, 96, D), BF),
    ((4, 4, 48, FF), BF),
    ((2, 2, 4, 2, 96, D), BF),
]
SAVED = [((R, 3 * D), BF), ((R, D), BF), ((16, R), F32), ((R, D), F32), ((R, FF), BF), ((R, FF), BF)]
EXTRA = [((R, D), BF), ((R, 2 * D), BF), ((R, D), BF), ((16, R), F32), ((R, D), F32)]
WORK = [
    ((R, D), BF),
    ((R, 128), F32),
    ((R, D), F32),
    ((D, R), BF),
    ((D, R), BF),
    ((R, R), F32),
    ((R, 128), F32),
    ((16, R), F32),
]


def flat(ref, lanes=None):
    value = ref[...] if lanes is None else ref[..., lanes]
    return value.reshape(-1, value.shape[-1])


def down_chunk(wdn, j):
    return flat(wdn.at[j // 2, j % 2])


def column_chunks():
    return [pl.ds(j * D, D) for j in range(4)]


def hidden_units(u):
    phi = 0.5 * (1.0 + lax.erf(u * 0.7071067811865476))
    return u * phi, phi + u * jnp.exp(-0.5 * u * u) * 0.3989422804014327


def own_quarter(here, values, first, out):
    half, tail = ROWS // 2, R - ROWS // 2
    columns = pl.ds(first, HALF)

    @pl.when(here.m == 0)
    def _():
        out[...] = values[pl.ds(0, half), columns]

    @pl.when(here.m == 1)
    def _():
        out[pl.ds(0, tail)] = values[pl.ds(half, tail), columns]
        out[pl.ds(tail, half - tail)] = jnp.zeros((half - tail, HALF), F32)


def padded(values, out):
    out[pl.ds(0, R)] = values[...].astype(BF)
    out[pl.ds(R, ROWS - R)] = jnp.zeros((ROWS - R, D), BF)


def forward_kernel(*refs):
    here = Place()
    tiles, slopes, radar, optical, cotangent = refs[:5]
    vecs = Vectors(refs[5:15])
    qkv_own, attn_own, up_own, down_own, cq_own, kv_own, cw_own = refs[15:22]
    refs = refs[22:]
    gathered, arrived = refs[:2]
    saved_out, refs = refs[2:8], refs[8:]
    gdn, gup, gat, gcr, vec_out, joined_own, back_own, joined_all, back_all = refs[:9]
    refs = refs[9:]
    wqkv, wo, wup, wdn, wcq, wkv, wcw = refs[:7]
    saved, refs = refs[7:13], refs[13:]
    qkv, o, lse_rows, x1, g, gp = saved
    query, pairs, merged, lse_cross, x2 = refs[:5]
    a, lse_lanes, acc, et, at, dist, valid, inner = refs[5:13]
    xin, ctx, cot, e1, e2, out_bf, staging = refs[13:20]
    link_send, link_recv, near_send, near_recv, load_sems, save_sems, stage_sems = refs[20:]
    m, oth = here.m, here.o
    first, second = pl.when(here.first), pl.when(here.second)

    peers = here.along_x[1:] + here.along_z[1:] + [here.sibling, here.partner, here.section]
    here.signal(peers)
    loads = Loads(load_sems)
    heads = Heads((qkv, 0), (qkv, D), (qkv, 2 * D), (o, 0), dist, slopes, lse_lanes, lse_rows)
    cross = Heads(
        (query, 0), (pairs, 0), (pairs, D), (merged, 0), dist, slopes, lse_lanes, lse_cross
    )
    own_qkv = loads.start(
        *[(qkv_own.at[j], wqkv.at[:, :, :, lanes_at(j * D + m * HALF, HALF)]) for j in range(3)]
    )
    own_rest = loads.start(
        (attn_own, wo.at[m]),
        (up_own, wup.at[:, :, :, lanes_at(m * HIDDEN, HIDDEN)]),
        (down_own, wdn.at[m]),
    )
    token_loads = loads.start(
        (optical.at[m, pl.ds(0, R)], ctx), (cotangent.at[m, pl.ds(0, R)], cot)
    )
    cross_own = loads.start(
        (cq_own, wcq.at[:, :, :, lanes_at(m * HALF, HALF)]), (cw_own, wcw.at[m])
    )

    i = here.dp
    links = Links(link_send, link_recv)
    block, within = i // 8, (lax.rem(i // 2, 4), lax.rem(i, 2))
    tail_lanes = lanes_at(lax.rem(i // 4, 2) * HALF, HALF)
    tail = (lax.rem(i // 2, 2), within[1], slice(None), tail_lanes)
    part = lax.rem(block, 3)
    kv_part = lax.rem(block + 1, 2)

    @second
    def _():
        for j in range(2):
            wkv[:, :, :, lanes_at(j * D + m * HALF, HALF)] = kv_own[:, j, :].reshape(4, 2, 96, HALF)

    in_head, in_query = i < 24, i < 8
    in_tail, in_pairs = i >= 24, jnp.logical_and(i >= 8, i < 24)
    kv_lanes = lanes_at(kv_part * D + m * HALF, HALF)
    rest = slice(None)
    gathers = [
        Gather(here, links, gathered, g, sources)
        for g, sources in (
            (0, [(in_head, qkv_own.at[(part,) + within]), (in_tail, attn_own.at[tail])]),
            (1, [(None, up_own.at[within + (rest, lanes_at(block * HALF, HALF))])]),
            (
                3,
                [
                    (in_query, cq_own.at[within]),
                    (in_pairs, wkv.at[within + (rest, kv_lanes)]),
                    (in_tail, cw_own.at[tail]),
                ],
            ),
        )
    ]
    across = Across(here, links, down_own, gathered, 2)
    distances(tiles, m, dist, valid)

    def project(j, part):
        lanes = lanes_at(j * D + part * HALF, HALF)
        qkv[:, lanes] = mm(a[...], flat(wqkv, lanes)).astype(BF)

    @first
    def _():
        lse_lanes[...] = jnp.zeros_like(lse_lanes)
        copy = pltpu.make_async_copy(radar.at[m, pl.ds(0, R)], xin, save_sems.at[6])
        copy.start()
        copy.wait()
        x = xin[...].astype(F32) * valid[:, :1]
        a[...] = scaled_norm(x, vecs.norm1_gain, vecs.norm1_bias)
        wait_all(own_qkv)
        for j in range(3):
            project(j, m)

    here.await_all(peers)
    for gather in gathers[:2]:
        gather.begin()

    @second
    def _():
        wait_all(cross_own)
        gathers[2].begin()

    across.begin()

    def stage(i):
        for gather in gathers[:2]:
            gather.stage(i)
        second(lambda: gathers[2].stage(i))

    for j in range(3):
        first(lambda: heads.forward(m * 3 + j))
        stage(j + 1)
    stage(4)
    gathers[0].stage(5)
    other_one = loads.start(
        *[
            (gathered.at[0, j], wqkv.at[:, :, :, lanes_at(j * D + oth * HALF, HALF)])
            for j in range(3)
        ],
        *[
            (gathered.at[0, 3, pl.ds(2 * j, 2)], wo.at[oth, :, :, :, pl.ds(j * HALF, HALF)])
            for j in range(2)
        ],
    )

    @first
    def _():
        wait_all(other_one[:3])
        for j in range(3):
            project(j, oth)

    gathers[1].stage(5)
    other_up = loads.start(
        *[
            (gathered.at[1, j], wup.at[:, :, :, lanes_at(oth * HIDDEN + j * HALF, HALF)])
            for j in range(4)
        ]
    )
    across.share()

    @first
    def _():
        heads.each(heads.forward, oth * 3, oth * 3 + 3)
        heads.finish()

    across.finish()
    other_down = loads.start(
        *[
            (
                gathered.at[2, pl.ds(2 * j, 2)],
                wdn.at[oth, :, :, :, :, pl.ds(j * HALF, HALF)],
            )
            for j in range(2)
        ]
    )

    def feed_forward(source, rows):
        a[rows] = scaled_norm(source[rows], vecs.norm2_gain, vecs.norm2_bias)
        for j, lanes in enumerate(column_chunks()):
            u = mm(a[rows], flat(wup, lanes)) + vecs.up_bias[:, lanes]
            unit, slope = hidden_units(u)
            g[rows, lanes] = unit.astype(BF)
            gp[rows, lanes] = slope.astype(BF)
            term = mm(g[rows, lanes], down_chunk(wdn, j))
            acc[rows] = term if j == 0 else acc[rows] + term

    near = (near_send, near_recv)
    blocks = [pl.ds(0, 256), pl.ds(256, R - 256)]
    forth = [remote(out_bf.at[b], xin.at[b], near, i, here.section) for i, b in enumerate(blocks)]
    back = [
        remote(out_bf.at[b], arrived.at[b], near, 2 + i, here.section)
        for i, b in enumerate(blocks)
    ]

    @first
    def _():
        saves = [
            pltpu.make_async_copy(source, target, save_sems.at[i])
            for i, (source, target) in enumerate(zip(saved, saved_out))
        ]
        for copy in saves[:3]:
            copy.start()
        wait_all(own_rest)
        wait_all(other_one[3:])
        x = xin[...].astype(F32) * valid[:, :1]
        x1[...] = x + mm(o[...], flat(wo)) + vecs.attn_bias[...]
        saves[3].start()
        wait_all(other_up)
        wait_all(other_down)
        for rows, copy in zip(blocks, forth):
            feed_forward(x1, rows)
            out_bf[rows] = (x1[rows] + acc[rows] + vecs.down_bias[...]).astype(BF)
            copy.start()
        for copy in saves[4:]:
            copy.start()
        wait_all(saves)
        wait_all(token_loads)
        wait_all(cross_own)
        for copy in forth:
            copy.wait_send()
        for copy in back:
            copy.wait_recv()

    @second
    def _():
        gathers[2].stage(5)
        pairs_cross = [(gathered.at[3, 0], wcq.at[:, :, :, lanes_at(oth * HALF, HALF)])]
        for j in range(2):
            pairs_cross += [
                (gathered.at[3, j + 1], wkv.at[:, :, :, lanes_at(j * D + oth * HALF, HALF)]),
                (
                    gathered.at[3, 3, pl.ds(2 * j, 2)],
                    wcw.at[oth, :, :, :, pl.ds(j * HALF, HALF)],
                ),
            ]
        other_cross = loads.start(*pairs_cross)
        for copies in (own_qkv, own_rest, other_one, other_up, other_down):
            wait_all(copies)
        wait_all(token_loads)
        wait_all(other_cross)
        keep = valid[:, :1]
        ctx[...] = (ctx[...].astype(F32) * keep).astype(BF)
        cot[...] = (cot[...].astype(F32) * keep).astype(BF)
        for j in range(2):
            lanes = pl.ds(j * D, D)
            pairs[:, lanes] = mm(ctx[...], flat(wkv, lanes)).astype(BF)
        lse_lanes[...] = jnp.zeros_like(lse_lanes)
        for copy in forth:
            copy.wait_recv()
        a[...] = scaled_norm(xin[...].astype(F32), vecs.norm1_gain, vecs.norm1_bias)
        for j in range(3):
            lanes = pl.ds(j * D, D)
            qkv[:, lanes] = mm(a[...], flat(wqkv, lanes)).astype(BF)
        heads.each(heads.forward, 0, H // 2)
        heads.finish()
        x1[...] = xin[...].astype(F32) + mm(o[...], flat(wo)) + vecs.attn_bias[...]
        a[...] = scaled_norm(x1[...], vecs.query_gain, vecs.query_bias)
        query[...] = mm(a[...], flat(wcq)).astype(BF)
        cross.each(cross.forward, 0, H // 2)
        cross.finish()
        x2[...] = x1[...] + mm(merged[...], flat(wcw)) + vecs.cross_bias[...]
        feed_forward(x2, pl.ds(0, R))
        acc[...] = (x2[...] + acc[...] + vecs.down_bias[...]) * keep
        own_quarter(here, acc, HALF, joined_own)
        padded(acc, joined_all)

        for j, lanes in enumerate(column_chunks()):
            gp[:, lanes] = (mmt(cot[...], down_chunk(wdn, j)) * gp[:, lanes].astype(F32)).astype(BF)
            term = mmt(gp[:, lanes], flat(wup, lanes))
            acc[...] = term if j == 0 else acc[...] + term
        vec_out[...] = jnp.zeros_like(vec_out)
        dm = acc[...]
        normed, inverse = normalize(x2[...])
        vec_out[3:4, :] = column_sums(dm * normed)
        vec_out[4:5, :] = column_sums(dm)
        acc[...] = cot[...].astype(F32) + norm_grad(dm, normed, inverse, vecs.norm2_gain[...])
        e2[...] = acc[...].astype(BF)
        a[...] = mmt(e2[...], flat(wcw)).astype(BF)
        cross_back = Heads(
            (query, 0), (pairs, 0), (pairs, D), (a, 0), dist, slopes, lse_lanes, lse_cross
        )
        cross_back.prepare(merged, inner)
        cross_back.each(cross_back.backward, 0, H // 2)
        dc = mmt(query[...], flat(wcq))
        normed, inverse = normalize(x1[...])
        vec_out[10:11, :] = column_sums(dc * normed)
        vec_out[11:12, :] = column_sums(dc)
        acc[...] = acc[...] + norm_grad(dc, normed, inverse, vecs.query_gain[...])
        e1[...] = acc[...].astype(BF)
        a[...] = mmt(e1[...], flat(wo)).astype(BF)
        self_back = Heads(
            (qkv, 0), (qkv, D), (qkv, 2 * D), (a, 0), dist, slopes, lse_lanes, lse_rows
        )
        self_back.prepare(o, inner)
        self_back.each(self_back.backward, 0, H // 2)
        sums = []
        for rows, copy in zip(blocks, back):
            da = mmt(qkv[rows], flat(wqkv))
            normed, inverse = normalize(xin[rows].astype(F32))
            sums.append((column_sums(da * normed), column_sums(da)))
            out_bf[rows] = (
                acc[rows] + norm_grad(da, normed, inverse, vecs.norm1_gain[...])
            ).astype(BF)
            copy.start()
        vec_out[0:1, :] = sums[0][0] + sums[1][0]
        vec_out[1:2, :] = sums[0][1] + sums[1][1]

        staged = Staged(staging, stage_sems)
        acc[...] = mmt(pairs[...], flat(wkv)) * keep
        own_quarter(here, acc, HALF, back_own)
        padded(acc, back_all)
        permute = chunk_order()
        et[...] = mmt(permute, e2[...]).astype(BF)
        staged.put(mm(et[...], merged[...]).astype(BF), halves(gcr, 1, HALF))
        a[...] = scaled_norm(x1[...], vecs.query_gain, vecs.query_bias)
        et[...] = mmt(permute, a[...]).astype(BF)
        staged.put(mm(et[...], query[...]).astype(BF), halves(gcr, 0, 0))
        et[...] = mmt(permute, ctx[...]).astype(BF)
        for j, target in enumerate([(0, HALF), (1, 0)]):
            staged.put(mm(et[...], pairs[:, pl.ds(j * D, D)]).astype(BF), halves(gcr, *target))
        et[...] = cot[...].T
        a[...] = scaled_norm(x2[...], vecs.norm2_gain, vecs.norm2_bias)
        at[...] = a[...].T
        for j, lanes in enumerate(column_chunks()):
            vec_out[6 + j : 7 + j, :] = column_sums(gp[:, lanes])
            staged.put(mm(et[...], g[:, lanes]).astype(BF), quarter_of(gdn, j))
            staged.put(mm(at[...], gp[:, lanes]).astype(BF), quarter_of(gup, j))
        vec_out[2:3, :] = column_sums(e1[...])
        vec_out[5:6, :] = column_sums(cot[...])
        vec_out[12:13, :] = column_sums(e2[...])
        et[...] = e1[...].T
        staged.put(mm(et[...], o[...]).astype(BF), halves(gat, 1, HALF))
        a[...] = scaled_norm(xin[...].astype(F32), vecs.norm1_gain, vecs.norm1_bias)
        at[...] = a[...].T
        for j, target in enumerate([(0, 0), (0, HALF), (1, 0)]):
            staged.put(mm(at[...], qkv[:, pl.ds(j * D, D)]).astype(BF), halves(gat, *target))
        staged.drain()
        for copy in back:
            copy.wait_send()
        gathers[2].drain()

    for gather in gathers[:2] + [across]:
        gather.drain()


def chunk_order():
    r = lax.broadcasted_iota(jnp.int32, (D, 1), 0).astype(F32)
    chunk = jnp.floor((r + 0.5) / 48.0)
    inner = r - chunk * 48.0
    core = (inner >= 24.0).astype(F32)
    inner = inner - 24.0 * core
    section = (inner >= 12.0).astype(F32)
    source = 384.0 * section + 24.0 * chunk + 12.0 * core + inner - 12.0 * section
    columns = lax.broadcasted_iota(jnp.int32, (D, D), 1).astype(F32)
    return (columns == source).astype(F32).astype(BF)


def forward(tiles, slopes, tokens, vecs, own):
    scratch = vmem(
        LAYER_WEIGHTS + CROSS_WEIGHTS + SAVED + EXTRA + WORK + [((R, D), BF)] * 6 + [((2, 4, 4, 48, D), BF)]
    )
    quarter = shape((ROWS // 2, HALF), F32)
    return pl.pallas_call(
        forward_kernel,
        out_shape=[shape((4, 4, 4, 2, 96, HALF), BF), shape((R, D), BF)]
        + [shape(*s) for s in SAVED]
        + [shape((2, 4, 4, 48, 2 * D), BF)] * 4
        + [shape((16, D), F32), quarter, quarter, shape((ROWS, D), BF), shape((ROWS, D), BF)],
        in_specs=[SM, SM] + [ANY] * 3 + [VM] * 10 + [ANY] * 5 + [VM] + [ANY],
        out_specs=[ANY] * 12 + [VM] * 5,
        scratch_shapes=scratch
        + [dma(92), dma(92), dma(4), dma(4), dma(40), dma(7), pltpu.SemaphoreType.DMA((2, 2))],
        compiler_params=pltpu.CompilerParams(
            collective_id=0, has_side_effects=True, vmem_limit_bytes=BIG
        ),
    )(tiles, slopes, *tokens, *vecs, *own)


def backward_kernel(*refs):
    here = Place()
    tiles, slopes, radar, dy_in = refs[:4]
    vecs = Vectors(refs[4:14])
    qkv_own, attn_own, up_own, down_own, gathered, gathered48 = refs[14:20]
    saved_in, refs = refs[20:26], refs[26:]
    vec_in, joined_all, back_all, gcr = refs[:4]
    refs = refs[7:]
    gdn, gup, gat, odn, oup, oat, ocr, vec_total, vec_other, radar_own, quarters, ocr_other = refs[
        :12
    ]
    refs = refs[12:]
    wqkv, wo, wup, wdn = refs[:4]
    saved, refs = refs[4:10], refs[10:]
    qkv, o, lse_rows, x1, g, gp = saved
    a, lse_lanes, acc, et, at, dist, valid, inner = refs[:8]
    xin, radar_all, staging, vec, vbuf = refs[8:13]
    out_bf = radar_all.at[pl.ds(0, R)]
    own_at, cross_sums = refs[13:15]
    buffers, refs = [refs[15 + 7 * i : 22 + 7 * i] for i in range(4)], refs[43:]
    link_send, link_recv, far_send, far_recv, load_sems, local_sems, stage_sems = refs
    m, oth = here.m, here.o
    first, second = pl.when(here.first), pl.when(here.second)
    peers = here.ring + [
        here.sibling,
        here.partner,
        here.diagonal,
        here.along_x[2],
        here.along_z[2],
        here.section,
        here.crossed,
    ]
    here.signal(peers)
    loads = Loads(load_sems)
    links = Links(link_send, link_recv)
    far = (far_send, far_recv)
    staged = Staged(staging, stage_sems)
    heads = Heads((qkv, 0), (qkv, D), (qkv, 2 * D), (a, 0), dist, slopes, lse_lanes, lse_rows)
    chunks = column_chunks()

    cotangent = loads.prepare((dy_in, out_bf))
    units = [loads.prepare((saved_in[4].at[:, c], g.at[j % 2])) for j, c in enumerate(chunks)]
    early = loads.prepare((saved_in[3], x1), (radar.at[m, pl.ds(0, R)], xin))
    copies_down = loads.prepare(
        (down_own, wdn.at[m]),
        *[
            (gathered.at[2, pl.ds(2 * j, 2)], wdn.at[oth, :, :, :, :, pl.ds(j * HALF, HALF)])
            for j in range(2)
        ],
    )
    slopes_of = [loads.prepare((saved_in[5].at[:, c], gp.at[:, c])) for c in chunks]
    copies_up = loads.prepare(
        (up_own, wup.at[:, :, :, lanes_at(m * HIDDEN, HIDDEN)]),
        *[
            (gathered48.at[1, j], wup.at[:, :, :, lanes_at(oth * HIDDEN + j * HALF, HALF)])
            for j in range(4)
        ],
    )
    late = loads.prepare(
        (saved_in[0], qkv),
        (saved_in[1], o),
        (saved_in[2], lse_rows),
        (attn_own, wo.at[m]),
        *[
            (gathered.at[0, 3, pl.ds(2 * j, 2)], wo.at[oth, :, :, :, pl.ds(j * HALF, HALF)])
            for j in range(2)
        ],
    )
    copies_qkv = loads.prepare(
        *[(qkv_own.at[j], wqkv.at[:, :, :, lanes_at(j * D + m * HALF, HALF)]) for j in range(3)],
        *[
            (gathered48.at[0, j], wqkv.at[:, :, :, lanes_at(j * D + oth * HALF, HALF)])
            for j in range(3)
        ],
    )

    @first
    def _():
        for copies in [cotangent] + units[:2] + [early, copies_down] + slopes_of + [copies_up, late]:
            start_all(copies)
        distances(tiles, m, dist, valid)
        vec[...] = jnp.zeros_like(vec)
        wait_all(cotangent)
        e3 = out_bf[...]
        vec[5:6, :] = column_sums(e3)
        et[...] = e3.T
        for j in range(4):
            wait_all(units[j])
            staged.put(mm(et[...], g[j % 2]).astype(BF), quarter_of(gdn, j))
            if j < 2:
                start_all(units[j + 2])
        staged.drain()

    @second
    def _():
        vec[...] = vec_in[...]

    here.await_all(peers)
    low, high = pl.ds(0, 2 * D), pl.ds(2 * D, 2 * D)
    dn = scatter_stages(
        here, links, local_sems.at[0], gdn, odn, wqkv.at[:, :, :, low], buffers[0]
    )
    up = scatter_stages(here, links, local_sems.at[1], gup, oup, wup.at[:, :, :, low], buffers[1])
    mid = scatter_stages(here, links, local_sems.at[2], gat, oat, own_at, buffers[2])
    cross = scatter_stages(
        here, links, local_sems.at[3], gcr, cross_sums, wup.at[:, :, :, high], buffers[3]
    )
    vec_steps = vector_stages(here, links, vec, vbuf, vec_total)

    def quarter_copies(source, kind):
        half_rows = ROWS // 2
        mine, others = rows_at(m * half_rows, half_rows), rows_at(oth * half_rows, half_rows)
        sender, receiver = (0, 1) if kind == 2 else (1, 0)
        same = pl.ds(sender * HALF, HALF)
        over = pl.ds(receiver * HALF, HALF)
        return [
            remote(source.at[mine, over], quarters.at[kind, 0], far, 3 * kind, here.section),
            remote(source.at[others, over], quarters.at[kind, 1], far, 3 * kind + 1, here.crossed),
            remote(source.at[others, same], quarters.at[kind, 1], far, 3 * kind + 2, here.partner),
        ]

    sent = [quarter_copies(s, i) for i, s in enumerate((joined_all, back_all, radar_all))]
    cross_sent = remote(ocr.at[0], ocr_other, far, 9, here.section)
    vec_sent = remote(vec_total, vec_other, far, 10, here.section)

    @second
    def _():
        for copies in sent[:2]:
            for copy in copies:
                copy.start()
        cross[0]()

    dn[0]()
    second(cross[1])

    def chain(j):
        lanes = chunks[j]
        wait_all(slopes_of[j])
        du = (mmt(out_bf[...], down_chunk(wdn, j)) * gp[:, lanes].astype(F32)).astype(BF)
        gp[:, lanes] = du
        vec[6 + j : 7 + j, :] = column_sums(du)
        staged.put(mm(at[...], gp[:, lanes]).astype(BF), quarter_of(gup, j))
        if j == 0:
            wait_all(copies_up)
        term = mmt(gp[:, lanes], flat(wup, lanes))
        acc[...] = term if j == 0 else acc[...] + term

    @first
    def _():
        wait_all(early)
        a[...] = scaled_norm(x1[...], vecs.norm2_gain, vecs.norm2_bias)
        at[...] = a[...].T
        wait_all(copies_down)
        chain(0)
        chain(1)

    dn[1]()

    @first
    def _():
        chain(2)
        chain(3)
        staged.drain()
        wait_all(late)

    up[0]()
    second(cross[2])

    @first
    def _():
        dm = acc[...]
        normed, inverse = normalize(x1[...])
        vec[3:4, :] = column_sums(dm * normed)
        vec[4:5, :] = column_sums(dm)
        acc[...] = out_bf[...].astype(F32) + norm_grad(dm, normed, inverse, vecs.norm2_gain[...])
        e1 = acc[...].astype(BF)
        vec[2:3, :] = column_sums(e1)
        out_bf[...] = e1
        a[...] = mmt(out_bf[...], flat(wo)).astype(BF)
        heads.prepare(o, inner)

    second(cross[3])

    @first
    def _():
        et[...] = out_bf[...].T
        staged.put(mm(et[...], o[...]).astype(BF), halves(gat, 1, HALF))
        heads.backward(0)

    dn[2]()
    up[1]()
    second(cross[4])
    first(lambda: heads.each(heads.backward, 1, 6))
    dn[3]()
    second(cross[5])
    first(lambda: start_all(copies_qkv) and None)

    @first
    def _():
        x = xin[...].astype(F32) * valid[:, :1]
        a[...] = scaled_norm(x, vecs.norm1_gain, vecs.norm1_bias)
        at[...] = a[...].T
        for j, target in enumerate([(0, 0), (0, HALF), (1, 0)]):
            staged.put(mm(at[...], qkv[:, pl.ds(j * D, D)]).astype(BF), halves(gat, *target))
        staged.drain()
        wait_all(copies_qkv)

    mid[0]()

    @first
    def _():
        da = mmt(qkv[...], flat(wqkv))
        normed, inverse = normalize(xin[...].astype(F32) * valid[:, :1])
        vec[0:1, :] = column_sums(da * normed)
        vec[1:2, :] = column_sums(da)
        acc[...] = (acc[...] + norm_grad(da, normed, inverse, vecs.norm1_gain[...])) * valid[:, :1]
        own_quarter(here, acc, 0, radar_own)
        padded(acc, radar_all)
        for copy in sent[2]:
            copy.start()

    @second
    def _():
        for section in range(2):
            for which in range(2):
                ocr[section, which] = cross_sums[which][section * 12 : section * 12 + 12]
        cross_sent.start()

    mid[1]()
    vec_steps[0]()
    vec_steps[1]()
    dn[4]()
    vec_steps[2]()
    up[2]()
    mid[2]()
    vec_steps[3]()
    dn[5]()
    up[3]()
    vec_steps[4]()

    @second
    def _():
        vec_sent.start()

    mid[3]()
    up[4]()
    mid[4]()
    up[5]()
    mid[5]()

    @first
    def _():
        for copies in sent[:2]:
            copies[0].wait_recv()
            copies[1].wait_recv()
        sent[2][2].wait_recv()
        for copy in sent[2]:
            copy.wait_send()
        cross_sent.wait_recv()
        vec_sent.wait_recv()

    @second
    def _():
        sent[2][0].wait_recv()
        sent[2][1].wait_recv()
        for copies in sent[:2]:
            copies[2].wait_recv()
            for copy in copies:
                copy.wait_send()
        cross_sent.wait_send()
        vec_sent.wait_send()


def backward(tiles, slopes, radar, dy, vecs, own, gathered, saved, vec, quarters, gcr, grads):
    scratch = vmem(
        CHUNKED
        + SAVED[:4]
        + [((2, R, D), BF)]
        + SAVED[5:]
        + WORK
        + [((R, D), BF), ((ROWS, D), BF)]
        + [((2, 4, 4, 48, D), BF), ((16, D), F32), ((8, 16, D), F32)]
    )
    vector = shape((16, D), F32)
    qkv, attn, up, down = own
    return pl.pallas_call(
        backward_kernel,
        out_shape=[
            *[shape(array.shape, BF) for array in grads],
            *[shape((2, 24, D), F32)] * 3,
            shape((2, 2, 12, D), F32),
            vector,
            vector,
            shape((ROWS // 2, HALF), F32),
            shape((3, 2, ROWS // 2, HALF), BF),
            shape((2, 12, D), F32),
        ],
        in_specs=[SM, SM, ANY, ANY] + [VM] * 10 + [ANY] * 12 + [VM] + [ANY] * 6,
        out_specs=[ANY] * 3 + [VM] * 7 + [ANY, VM],
        input_output_aliases={30: 0, 31: 1, 32: 2},
        scratch_shapes=scratch
        + own_scratch(2 * D)
        + [pltpu.VMEM((2, 24, D), F32)]
        + scatter_scratch(2 * D) * 4
        + [dma(124), dma(124), dma(11), dma(11), dma(40), dma(4), pltpu.SemaphoreType.DMA((2, 2))],
        compiler_params=pltpu.CompilerParams(
            collective_id=1, has_side_effects=True, vmem_limit_bytes=BIG
        ),
    )(
        tiles,
        slopes,
        radar,
        dy,
        *vecs,
        qkv.reshape(3, 4, 4, 48, HALF),
        attn,
        up.reshape(4, 4, 48, HIDDEN),
        down,
        gathered,
        gathered.reshape(4, 4, 4, 4, 48, HALF),
        *saved,
        vec,
        *quarters,
        gcr,
        *grads,
    )


def local(
    radar_tokens,
    optical_tokens,
    out_cotangent,
    tile_sides,
    norm1_gain,
    norm1_bias,
    qkv_weight,
    attn_weight,
    attn_bias,
    norm2_gain,
    norm2_bias,
    up_weight,
    up_bias,
    down_weight,
    down_bias,
    query_gain,
    query_bias,
    cross_query,
    cross_keyval,
    cross_weight,
    cross_bias,
):
    m = lax.axis_index("mp")
    joining = lax.axis_index("pipe") == 1
    slopes = jnp.exp2(-8.0 * (jnp.arange(H, dtype=jnp.int32) + 1).astype(F32) / H)
    vecs = (
        norm1_gain,
        norm1_bias,
        attn_bias,
        norm2_gain,
        norm2_bias,
        up_bias,
        down_bias,
        query_gain,
        query_bias,
        cross_bias,
    )
    own = (
        qkv_weight[0].transpose(1, 0, 2).reshape(3, 4, 2, 96, HALF),
        attn_weight.reshape(2, 2, 96, D),
        up_weight.reshape(4, 2, 96, HIDDEN),
        down_weight.reshape(2, 4, 2, 96, D),
    )
    cross_own = (
        cross_query.reshape(4, 2, 96, HALF),
        cross_keyval,
        cross_weight.reshape(2, 2, 96, D),
    )
    tokens = (radar_tokens, optical_tokens, out_cotangent)
    results = forward(
        tile_sides, slopes, tokens, vecs, own + cross_own
    )
    gathered, dy0 = results[:2]
    saved = results[2:8]
    grads = results[8:11]
    gcr, vec, joined_own, back_own, joined_all, back_all = results[11:]
    outs = backward(
        tile_sides,
        slopes,
        radar_tokens,
        dy0,
        vecs,
        own,
        gathered,
        saved,
        vec,
        (joined_all, back_all),
        gcr,
        grads,
    )
    odn, oup, oat, ocr, vec, vec_other, radar_own, quarters, ocr_other = outs[3:]

    def placed(own_quarter, kind, here):
        mine = jnp.where(here, own_quarter, quarters[kind, 0].astype(F32))
        others = quarters[kind, 1].astype(F32)
        swap = m == 1
        return jnp.stack([jnp.where(swap, others, mine), jnp.where(swap, mine, others)])

    crossed = jnp.where(joining, vec[10:13], vec_other[10:13])
    ocr = jnp.where(joining, ocr[1], ocr_other)
    q, k = oat[0, :, :HALF], oat[0, :, HALF:]
    v, attn = oat[1, :, :HALF], oat[1, :, HALF:]
    cq, ck = ocr[0, :, :HALF], ocr[0, :, HALF:]
    cv, cw = ocr[1, :, :HALF], ocr[1, :, HALF:]
    return (
        placed(joined_own, 0, joining),
        placed(radar_own, 2, jnp.logical_not(joining)),
        placed(back_own, 1, joining),
        vec[0:1],
        vec[1:2],
        jnp.stack([q, k, v], axis=1)[None],
        attn.T[None],
        vec[2:3],
        vec[3:4],
        vec[4:5],
        jnp.concatenate([oup[0], oup[1]], axis=1)[None],
        vec[6:10].reshape(1, FF),
        jnp.concatenate([odn[0].T, odn[1].T])[None],
        vec[5:6],
        crossed[0],
        crossed[1],
        cq,
        jnp.stack([ck, cv], axis=1),
        cw.T,
        crossed[2],
    )


def solution(mesh):
    in_specs = (
        P(None, "dp", None),
        P(None, "dp", None),
        P(None, "dp", None),
        P(None, "dp"),
        P("pipe", None),
        P("pipe", None),
        P("pipe", None, None, "mp"),
        P("pipe", "mp", None),
        P("pipe", None),
        P("pipe", None),
        P("pipe", None),
        P("pipe", None, "mp"),
        P("pipe", None),
        P("pipe", "mp", None),
        P("pipe", None),
        P(),
        P(),
        P(None, "mp"),
        P(None, None, "mp"),
        P("mp", None),
        P(),
    )
    out_specs = (
        P(None, ("dp", "mp"), "pipe"),
        P(None, ("dp", "mp"), "pipe"),
        P(None, ("dp", "mp"), "pipe"),
        P("pipe", None),
        P("pipe", None),
        P("pipe", "dp", None, "mp"),
        P("pipe", "mp", "dp"),
        P("pipe", None),
        P("pipe", None),
        P("pipe", None),
        P("pipe", "dp", "mp"),
        P("pipe", None),
        P("pipe", "mp", "dp"),
        P("pipe", None),
        P(),
        P(),
        P(("pipe", "dp"), "mp"),
        P(("pipe", "dp"), None, "mp"),
        P("mp", ("pipe", "dp")),
        P(),
    )
    return jax.shard_map(local, mesh=mesh, in_specs=in_specs, out_specs=out_specs, check_vma=False)
```

```python
import jax
import jax.numpy as jnp
from jax import lax
from jax.experimental import pallas as pl
from jax.experimental.pallas import tpu as pltpu
from jax.sharding import PartitionSpec as P

H = 12
HS = 64
D = 768
FF = 3072
ROWS = 512
R = 464
HALF = D // 2
HIDDEN = FF // 2
SLOTS = 3
EPSILON = 1e-05
BF = jnp.bfloat16
F32 = jnp.float32
ANY = pl.BlockSpec(memory_space=pl.ANY)
VM = pl.BlockSpec(memory_space=pltpu.VMEM)
SM = pl.BlockSpec(memory_space=pltpu.SMEM)
MESH = pl.DeviceIdType.MESH
BIG = 62 * 1024 * 1024


def shape(dims, kind):
    return jax.ShapeDtypeStruct(dims, kind)


def vmem(shapes):
    return [pltpu.VMEM(dims, kind) for dims, kind in shapes]


def dma(count):
    return pltpu.SemaphoreType.DMA((count,))


class Place:
    def __init__(self):
        dp = lax.axis_index("dp")
        self.dp = dp
        self.pipe = lax.axis_index("pipe")
        self.m = lax.axis_index("mp")
        self.o = 1 - self.m
        self.core = lax.rem(dp, 2)
        self.twin = 1 - self.core
        chip = dp // 2
        self.x = lax.rem(chip, 4)
        self.z = chip // 4
        self.xs = [self.x] + [lax.rem(self.x + i, 4) for i in (1, 2, 3)]
        self.zs = [self.z] + [lax.rem(self.z + i, 4) for i in (1, 2, 3)]
        self.along_x = [self.at(self.z, x, self.core) for x in self.xs]
        self.along_z = [self.at(z, self.x, self.core) for z in self.zs]
        self.sibling = self.at(self.z, self.x, self.twin)
        self.partner = {"mp": self.o}
        self.section = {"pipe": 1 - self.pipe}
        self.crossed = {"pipe": 1 - self.pipe, "mp": self.o}
        self.diagonal = dict(self.sibling, mp=self.o)
        self.ring = [self.along_x[1], self.along_x[3], self.along_z[1], self.along_z[3]]
        self.first = self.pipe == 0
        self.second = self.pipe == 1

    def at(self, z, x, core):
        return {"dp": (z * 4 + x) * 2 + core}

    def signal(self, devices):
        barrier = pltpu.get_barrier_semaphore()
        for device in devices:
            pl.semaphore_signal(barrier, inc=1, device_id=device, device_id_type=MESH)

    def await_all(self, devices):
        pl.semaphore_wait(pltpu.get_barrier_semaphore(), len(devices))


def remote(source, target, sems, i, device):
    return pltpu.make_async_remote_copy(
        src_ref=source,
        dst_ref=target,
        send_sem=sems[0].at[i],
        recv_sem=sems[1].at[i],
        device_id=device,
        device_id_type=MESH,
    )


class Links:
    def __init__(self, *sems):
        self.sems = sems
        self.used = 0

    def prepare(self, source, target, device):
        copy = remote(source, target, self.sems, self.used, device)
        self.used += 1
        return copy


class Loads:
    def __init__(self, sems):
        self.sems = sems
        self.used = 0

    def prepare(self, *pairs):
        copies = []
        for source, target in pairs:
            copies.append(pltpu.make_async_copy(source, target, self.sems.at[self.used]))
            self.used += 1
        return copies

    def start(self, *pairs):
        return start_all(self.prepare(*pairs))


def start_all(copies):
    for copy in copies:
        copy.start()
    return copies


def wait_all(copies):
    for copy in copies:
        copy.wait()


def lanes_at(first, size):
    return pl.ds(pl.multiple_of(first, 128), size)


def rows_at(first, size):
    return pl.ds(pl.multiple_of(first, 16), size)


class Gather:
    def __init__(self, here, links, out, g, sources):
        c, x, z = here.core, here.x, here.z
        xs, zs = here.xs, here.zs
        right, left, up, down = here.ring
        a, b = pl.ds(0, 48), pl.ds(48, 48)
        low, high = pl.ds(0, 2), pl.ds(2, 2)
        at = links.used
        self.begins = [
            (condition, remote(source, out.at[g, z, x, c], links.sems, at, here.partner))
            for condition, source in sources
        ]
        links.used = at + 1

        def same(view, device):
            return links.prepare(view, view, device)

        direct, early = [], []
        for j in (2, 1, 3):
            direct.append(same(out.at[g, z, x, c, a], here.along_x[j]))
            direct.append(same(out.at[g, z, x, c, b], here.along_z[j]))
        for j in (0, 1, 3):
            early.append(same(out.at[g, zs[j], :, c, a], here.sibling))
            early.append(same(out.at[g, :, xs[j], c, b], here.sibling))
        near = [
            same(out.at[g, z, :, c, a], up),
            same(out.at[g, z, :, c, a], down),
            same(out.at[g, :, x, c, b], right),
            same(out.at[g, :, x, c, b], left),
        ]
        relayed = [
            same(out.at[g, zs[3], low, c, a], up),
            same(out.at[g, zs[1], high, c, a], down),
            same(out.at[g, low, xs[3], c, b], right),
            same(out.at[g, high, xs[1], c, b], left),
        ]
        late = [
            same(out.at[g, zs[2], :, c, a], here.sibling),
            same(out.at[g, :, xs[2], c, b], here.sibling),
        ]
        first = [self.begins[-1][1]]
        self.waits = [[], first, direct, near, relayed, early + late]
        self.starts = [[], direct, near, relayed + early, late, []]
        self.all = first + direct + near + relayed + early + late

    def begin(self):
        for condition, copy in self.begins:
            if condition is None:
                copy.start()
            else:
                pl.when(condition)(copy.start)

    def stage(self, i):
        for copy in self.waits[i]:
            copy.wait_recv()
        for copy in self.starts[i]:
            copy.start()

    def drain(self):
        for copy in self.all:
            copy.wait_send()


class Across:
    def __init__(self, here, links, own, out, g):
        c = here.core
        spans = [pl.ds(2 * j, 2) for j in range(2)]
        self.copies = [
            links.prepare(
                own.at[:, :, c, :, pl.ds(j * HALF, HALF)], out.at[g, span, :, c], here.partner
            )
            for j, span in enumerate(spans)
        ]
        self.shared = [
            links.prepare(out.at[g, span, :, c], out.at[g, span, :, c], here.sibling)
            for span in spans
        ]

    def begin(self):
        start_all(self.copies)

    def share(self):
        for copy, onward in zip(self.copies, self.shared):
            copy.wait_recv()
            onward.start()

    def finish(self):
        for copy in self.shared:
            copy.wait_recv()

    def drain(self):
        for copy in self.copies + self.shared:
            copy.wait_send()


def vector_stages(here, links, vec, vbuf, total):
    rounds = [[here.sibling], here.along_x[1:], here.along_z[1:], [here.partner]]
    copies, used = [], 0
    for devices in rounds:
        copies.append(
            [links.prepare(total, vbuf.at[used + i], d) for i, d in enumerate(devices)]
        )
        used += len(devices)

    def begin(i):
        def stage():
            if i == 0:
                total[...] = vec[...]
            else:
                first = sum(len(devices) for devices in rounds[: i - 1])
                for copy in copies[i - 1]:
                    copy.wait()
                value = total[...]
                for j in range(len(rounds[i - 1])):
                    value = value + vbuf[first + j]
                total[...] = value
            if i < len(rounds):
                for copy in copies[i]:
                    copy.start()

        return stage

    return [begin(i) for i in range(len(rounds) + 1)]


def scatter_scratch(cols):
    half = cols // 2
    return [
        pltpu.VMEM((4, 4, 48, cols), BF),
        pltpu.VMEM((2, 2, 2, 48, half), BF),
        pltpu.VMEM((2, 2, 4, 48, half), BF),
        pltpu.VMEM((2, 4, 48, half), BF),
        pltpu.VMEM((2, 3, 48, half), BF),
        pltpu.VMEM((2, 2, 24, half), F32),
        pltpu.VMEM((3, 24, half), F32),
    ]


def scatter_stages(here, links, local_sem, grads, out, own, buffers):
    other, far, near, mid, near2, late, last = buffers
    cols = own.shape[-1]
    half = cols // 2
    c, twin, m, o = here.core, here.twin, here.m, here.o
    xs, zs = here.xs, here.zs
    lanes = [pl.ds(0, half), pl.ds(half, half)]
    low, high = pl.ds(0, 2), pl.ds(2, 2)
    ahead = [here.along_x[1], here.along_z[1]]
    behind = [here.along_x[3], here.along_z[3]]

    def block(ref, way, j):
        if way == 0:
            return ref.at[:, xs[j], :, lanes[0]]
        return ref.at[zs[j], :, :, lanes[1]]

    def part(ref, way, j, span):
        if way == 0:
            return ref.at[span, xs[j], :, lanes[0]]
        return ref.at[zs[j], span, :, lanes[1]]

    def places(way):
        return zs if way == 0 else xs

    order = [(way, j) for j in (2, 1, 3, 0) for way in range(2)]
    local = pltpu.make_async_copy(grads.at[c], own, local_sem)
    exchange = {
        (way, j): links.prepare(
            block(grads.at[twin], way, j), block(other, way, j), here.sibling
        )
        for way, j in order
    }
    one, two, three = [], [], []
    for way in range(2):
        turn = 1 - way
        at = places(way)
        one.append(
            [
                links.prepare(part(own, way, 2, low), far.at[way, 0], ahead[way]),
                links.prepare(part(own, way, 2, high), far.at[way, 1], behind[way]),
                links.prepare(part(own, way, 1, high), near.at[way, 0, high], ahead[way]),
                links.prepare(part(own, way, 3, low), near.at[way, 1, low], behind[way]),
            ]
        )
        two.append(
            [
                links.prepare(part(own, way, 1, low), near.at[way, 0, low], ahead[way]),
                links.prepare(part(own, way, 3, high), near.at[way, 1, high], behind[way]),
            ]
        )
        axis = (here.along_x, here.along_z)[turn]
        three.append(
            [
                links.prepare(mid.at[way, at[j]], near2.at[way, j - 1], axis[j])
                for j in (2, 1, 3)
            ]
        )
    ending = [
        links.prepare(late.at[m, twin], last.at[0], here.sibling),
        links.prepare(late.at[o, c], last.at[1], here.partner),
        links.prepare(late.at[o, twin], last.at[2], here.diagonal),
    ]

    def start():
        local.start()
        for key in order:
            exchange[key].start()

    def add_other(way, j):
        exchange[way, j].wait_recv()
        mine, theirs = block(own, way, j), block(other, way, j)
        for i in range(4):
            mine[i] = mine[i] + theirs[i]

    def ring_one():
        local.wait()
        for way in range(2):
            add_other(way, 2)
            one[way][0].start()
            one[way][1].start()
        for way in range(2):
            add_other(way, 1)
            one[way][2].start()
            add_other(way, 3)
            one[way][3].start()
        for way in range(2):
            add_other(way, 0)

    def ring_two():
        for way in range(2):
            one[way][0].wait_recv()
            target = part(own, way, 1, low)
            for i in range(2):
                target[i] = target[i] + far[way, 0, i]
            two[way][0].start()
            one[way][1].wait_recv()
            target = part(own, way, 3, high)
            for i in range(2):
                target[i] = target[i] + far[way, 1, i]
            two[way][1].start()

    def ring_three():
        for way in range(2):
            for copy in one[way][2:] + two[way]:
                copy.wait_recv()
            mine = block(own, way, 0)
            for i in range(4):
                mid[way, i] = (
                    mine[i].astype(F32) + near[way, 0, i].astype(F32) + near[way, 1, i].astype(F32)
                ).astype(BF)
            for copy in three[way]:
                copy.start()
        for step in one + two:
            for copy in step:
                copy.wait_send()

    def to_owners():
        for way in range(2):
            for copy in three[way]:
                copy.wait_recv()
            total = mid[way, places(way)[0]].astype(F32)
            for j in range(3):
                total = total + near2[way, j].astype(F32)
            late[way, 0] = total[:24]
            late[way, 1] = total[24:]
        for copy in ending:
            copy.start()

    def finish():
        for copy in ending:
            copy.wait_recv()
        out[c] = late[m, c] + last[1]
        out[twin] = last[0] + last[2]
        for key in order:
            exchange[key].wait_send()
        for step in three + [ending]:
            for copy in step:
                copy.wait_send()

    return [start, ring_one, ring_two, ring_three, to_owners, finish]


def own_scratch(cols):
    return [pltpu.VMEM((4, 4, 48, cols), BF)]


def mm(a, b):
    return lax.dot_general(a, b, (((1,), (0,)), ((), ())), preferred_element_type=F32)


def mmt(a, b):
    return lax.dot_general(a, b, (((1,), (1,)), ((), ())), preferred_element_type=F32)


def tmm(a, b):
    return lax.dot_general(a, b, (((0,), (0,)), ((), ())), preferred_element_type=F32)


def normalize(values):
    centered = values - jnp.mean(values, axis=-1, keepdims=True)
    inverse = lax.rsqrt(jnp.mean(centered * centered, axis=-1, keepdims=True) + EPSILON)
    return centered * inverse, inverse


def norm_grad(upstream, normed, inverse, gain):
    scaled = upstream * gain
    return inverse * (
        scaled
        - jnp.mean(scaled, axis=-1, keepdims=True)
        - normed * jnp.mean(scaled * normed, axis=-1, keepdims=True)
    )


class Geometry:
    def __init__(self, tiles, m, places):
        starts, member = [0], jnp.zeros_like(places)
        for slot in range(SLOTS):
            side = tiles[m, slot]
            starts.append(starts[-1] + side * side)
            member = member + (places >= starts[-1]).astype(jnp.int32)
        first, side = jnp.zeros_like(places), jnp.ones_like(places)
        for slot in range(SLOTS):
            here = member == slot
            first = jnp.where(here, starts[slot], first)
            side = jnp.where(here, jnp.maximum(tiles[m, slot], 1), side)
        first = jnp.where(member == SLOTS, starts[SLOTS], first)
        offset = (places - first).astype(F32)
        side = side.astype(F32)
        self.row = jnp.floor((offset + 0.5) / side)
        self.col = offset - self.row * side
        self.member = member
        self.valid = (member < SLOTS).astype(F32)


def distances(tiles, m, dist, valid):
    down = Geometry(tiles, m, lax.broadcasted_iota(jnp.int32, (R, 1), 0))
    along = Geometry(tiles, m, lax.broadcasted_iota(jnp.int32, (1, R), 1))
    gap_r = down.row - along.row
    gap_c = down.col - along.col
    apart = jnp.sqrt(gap_r * gap_r + gap_c * gap_c)
    dist[...] = jnp.where(down.member == along.member, apart, 1e30)
    valid[...] = jnp.broadcast_to(down.valid, (R, 128))


def head_lanes():
    lane = lax.broadcasted_iota(jnp.int32, (1, 128), 1)
    first = (lane < HS).astype(F32)
    return first.astype(BF), (1.0 - first).astype(BF), first > 0.5, lane


class Heads:
    def __init__(self, q, k, v, o, dist, slopes, lse_lanes, lse_rows):
        self.q, self.k, self.v, self.o = q, k, v, o
        self.dist, self.slopes = dist, slopes
        self.lse_lanes, self.lse_rows = lse_lanes, lse_rows

    def at(self, place, i):
        ref, first = place
        return ref.at[:, lanes_at(first + i * 128, 128)]

    def forward(self, i):
        m0, m1, in_first, lane = head_lanes()
        q, k, v = self.at(self.q, i)[...], self.at(self.k, i)[...], self.at(self.v, i)[...]
        q = q * jnp.asarray(0.125, BF)
        parts = []
        lse = self.lse_lanes
        for j, keep in enumerate((m0, m1)):
            s = mmt(q * keep, k) - self.slopes[2 * i + j] * self.dist[...]
            top = jnp.max(s, axis=-1, keepdims=True)
            raised = jnp.exp(s - top)
            total = jnp.sum(raised, axis=-1, keepdims=True)
            parts.append(mm(raised.astype(BF), v) * (1.0 / total))
            lse[...] = jnp.where(lane == 2 * i + j, top + jnp.log(total), lse[...])
        self.at(self.o, i)[...] = jnp.where(in_first, parts[0], parts[1]).astype(BF)

    def backward(self, i):
        m0, m1, in_first, lane = head_lanes()
        q, k, v = self.at(self.q, i)[...], self.at(self.k, i)[...], self.at(self.v, i)[...]
        do = self.at(self.o, i)[...]
        q = q * jnp.asarray(0.125, BF)
        dqs, dks, dvs = [], [], []
        for j, keep in enumerate((m0, m1)):
            h = 2 * i + j
            s = mmt(k, q * keep) - self.slopes[h] * self.dist[...]
            p = jnp.exp(s - self.lse_rows[pl.ds(h, 1), :])
            dvs.append(mm(p.astype(BF), do))
            ds = (p * (mmt(v, do * keep) - self.inner[pl.ds(h, 1), :])).astype(BF)
            dks.append(mm(ds, q))
            dqs.append(tmm(ds, k))
        self.at(self.q, i)[...] = (jnp.where(in_first, dqs[0], dqs[1]) * 0.125).astype(BF)
        self.at(self.k, i)[...] = jnp.where(in_first, dks[0], dks[1]).astype(BF)
        self.at(self.v, i)[...] = jnp.where(in_first, dvs[0], dvs[1]).astype(BF)

    def prepare(self, merged, inner):
        ref, _ = self.o
        self.inner = inner
        head = lax.broadcasted_iota(jnp.int32, (16, D), 0)
        lane = lax.broadcasted_iota(jnp.int32, (16, D), 1)
        of_head = ((lane >= head * HS) & (lane < head * HS + HS)).astype(F32).astype(BF)
        product = ref[...].astype(F32) * merged[...].astype(F32)
        high = product.astype(BF)
        low = (product - high.astype(F32)).astype(BF)
        inner[...] = mmt(of_head, high) + mmt(of_head, low)

    def each(self, what, first, last):
        def step(i, carry):
            what(i)
            return carry

        lax.fori_loop(first, last, step, 0)

    def finish(self):
        self.lse_rows[...] = self.lse_lanes[...].T[:16]


class Staged:
    def __init__(self, buffers, sems):
        self.buffers, self.sems = buffers, sems
        self.count = buffers.shape[0]
        self.turn = 0
        self.flying = {}

    def put(self, value, targets):
        slot = self.turn % self.count
        self.turn += 1
        self.settle(slot)
        self.buffers[slot] = value.reshape(self.buffers.shape[1:])
        self.flying[slot] = targets
        start_all(self.copies(slot))

    def copies(self, slot):
        return [
            pltpu.make_async_copy(
                self.buffers.at[slot, :, :, :, pl.ds(first, size)], target(), self.sems.at[slot, i]
            )
            for i, (first, size, target) in enumerate(self.flying[slot])
        ]

    def settle(self, slot):
        if slot in self.flying:
            wait_all(self.copies(slot))
            self.flying.pop(slot)

    def drain(self):
        for slot in range(self.count):
            self.settle(slot)


def quarter_of(target, j):
    return [(0, D, lambda: target.at[j % 2, :, :, :, pl.ds(j // 2 * D, D)])]


def halves(target, which, first):
    return [
        (
            part * HALF,
            HALF,
            lambda part=part: target.at[which, :, :, :, pl.ds(part * D + first, HALF)],
        )
        for part in range(2)
    ]


class Vectors:
    def __init__(self, refs):
        (
            self.norm1_gain,
            self.norm1_bias,
            self.attn_bias,
            self.norm2_gain,
            self.norm2_bias,
            self.up_bias,
            self.down_bias,
            self.query_gain,
            self.query_bias,
            self.cross_bias,
        ) = refs


def column_sums(values):
    return jnp.sum(values.astype(F32), axis=0, keepdims=True)


def scaled_norm(values, gain, bias):
    normed, _ = normalize(values)
    return (normed * gain[...] + bias[...]).astype(BF)


LAYER_WEIGHTS = [
    ((4, 2, 96, 3 * D), BF),
    ((2, 2, 2, 96, D), BF),
    ((4, 2, 96, FF), BF),
    ((2, 2, 4, 2, 96, D), BF),
]
CROSS_WEIGHTS = [((4, 2, 96, D), BF), ((4, 2, 96, 2 * D), BF), ((2, 2, 2, 96, D), BF)]
CHUNKED = [
    ((4, 4, 48, 3 * D), BF),
    ((2, 2, 2, 96, D), BF),
    ((4, 4, 48, FF), BF),
    ((2, 2, 4, 2, 96, D), BF),
]
SAVED = [((R, 3 * D), BF), ((R, D), BF), ((16, R), F32), ((R, D), F32), ((R, FF), BF), ((R, FF), BF)]
EXTRA = [((R, D), BF), ((R, 2 * D), BF), ((R, D), BF), ((16, R), F32), ((R, D), F32)]
WORK = [
    ((R, D), BF),
    ((R, 128), F32),
    ((R, D), F32),
    ((D, R), BF),
    ((D, R), BF),
    ((R, R), F32),
    ((R, 128), F32),
    ((16, R), F32),
]


def flat(ref, lanes=None):
    value = ref[...] if lanes is None else ref[..., lanes]
    return value.reshape(-1, value.shape[-1])


def down_chunk(wdn, j):
    return flat(wdn.at[j // 2, j % 2])


def column_chunks():
    return [pl.ds(j * D, D) for j in range(4)]


def hidden_units(u):
    phi = 0.5 * (1.0 + lax.erf(u * 0.7071067811865476))
    return u * phi, phi + u * jnp.exp(-0.5 * u * u) * 0.3989422804014327


def own_quarter(here, values, first, out):
    half, tail = ROWS // 2, R - ROWS // 2
    columns = pl.ds(first, HALF)

    @pl.when(here.m == 0)
    def _():
        out[...] = values[pl.ds(0, half), columns]

    @pl.when(here.m == 1)
    def _():
        out[pl.ds(0, tail)] = values[pl.ds(half, tail), columns]
        out[pl.ds(tail, half - tail)] = jnp.zeros((half - tail, HALF), F32)


def padded(values, out):
    out[pl.ds(0, R)] = values[...].astype(BF)
    out[pl.ds(R, ROWS - R)] = jnp.zeros((ROWS - R, D), BF)


def forward_kernel(*refs):
    here = Place()
    tiles, slopes, radar, optical, cotangent = refs[:5]
    vecs = Vectors(refs[5:15])
    qkv_own, attn_own, up_own, down_own, cq_own, kv_own, cw_own = refs[15:22]
    refs = refs[22:]
    gathered, arrived = refs[:2]
    saved_out, refs = refs[2:8], refs[8:]
    gdn, gup, gat, gcr, vec_out, joined_own, back_own, joined_all, back_all = refs[:9]
    refs = refs[9:]
    wqkv, wo, wup, wdn, wcq, wkv, wcw = refs[:7]
    saved, refs = refs[7:13], refs[13:]
    qkv, o, lse_rows, x1, g, gp = saved
    query, pairs, merged, lse_cross, x2 = refs[:5]
    a, lse_lanes, acc, et, at, dist, valid, inner = refs[5:13]
    xin, ctx, cot, e1, e2, out_bf, staging = refs[13:20]
    link_send, link_recv, near_send, near_recv, load_sems, save_sems, stage_sems = refs[20:]
    m, oth = here.m, here.o
    first, second = pl.when(here.first), pl.when(here.second)

    peers = here.along_x[1:] + here.along_z[1:] + [here.sibling, here.partner, here.section]
    here.signal(peers)
    loads = Loads(load_sems)
    heads = Heads((qkv, 0), (qkv, D), (qkv, 2 * D), (o, 0), dist, slopes, lse_lanes, lse_rows)
    cross = Heads(
        (query, 0), (pairs, 0), (pairs, D), (merged, 0), dist, slopes, lse_lanes, lse_cross
    )
    own_qkv = loads.start(
        *[(qkv_own.at[j], wqkv.at[:, :, :, lanes_at(j * D + m * HALF, HALF)]) for j in range(3)]
    )
    own_rest = loads.start(
        (attn_own, wo.at[m]),
        (up_own, wup.at[:, :, :, lanes_at(m * HIDDEN, HIDDEN)]),
        (down_own, wdn.at[m]),
    )
    token_loads = loads.start(
        (optical.at[m, pl.ds(0, R)], ctx), (cotangent.at[m, pl.ds(0, R)], cot)
    )
    cross_own = loads.start(
        (cq_own, wcq.at[:, :, :, lanes_at(m * HALF, HALF)]), (cw_own, wcw.at[m])
    )

    i = here.dp
    links = Links(link_send, link_recv)
    block, within = i // 8, (lax.rem(i // 2, 4), lax.rem(i, 2))
    tail_lanes = lanes_at(lax.rem(i // 4, 2) * HALF, HALF)
    tail = (lax.rem(i // 2, 2), within[1], slice(None), tail_lanes)
    part = lax.rem(block, 3)
    kv_part = lax.rem(block + 1, 2)

    @second
    def _():
        for j in range(2):
            wkv[:, :, :, lanes_at(j * D + m * HALF, HALF)] = kv_own[:, j, :].reshape(4, 2, 96, HALF)

    in_head, in_query = i < 24, i < 8
    in_tail, in_pairs = i >= 24, jnp.logical_and(i >= 8, i < 24)
    kv_lanes = lanes_at(kv_part * D + m * HALF, HALF)
    rest = slice(None)
    gathers = [
        Gather(here, links, gathered, g, sources)
        for g, sources in (
            (0, [(in_head, qkv_own.at[(part,) + within]), (in_tail, attn_own.at[tail])]),
            (1, [(None, up_own.at[within + (rest, lanes_at(block * HALF, HALF))])]),
            (
                3,
                [
                    (in_query, cq_own.at[within]),
                    (in_pairs, wkv.at[within + (rest, kv_lanes)]),
                    (in_tail, cw_own.at[tail]),
                ],
            ),
        )
    ]
    across = Across(here, links, down_own, gathered, 2)
    distances(tiles, m, dist, valid)

    def project(j, part):
        lanes = lanes_at(j * D + part * HALF, HALF)
        qkv[:, lanes] = mm(a[...], flat(wqkv, lanes)).astype(BF)

    @first
    def _():
        lse_lanes[...] = jnp.zeros_like(lse_lanes)
        copy = pltpu.make_async_copy(radar.at[m, pl.ds(0, R)], xin, save_sems.at[6])
        copy.start()
        copy.wait()
        x = xin[...].astype(F32) * valid[:, :1]
        a[...] = scaled_norm(x, vecs.norm1_gain, vecs.norm1_bias)
        wait_all(own_qkv)
        for j in range(3):
            project(j, m)

    here.await_all(peers)
    for gather in gathers[:2]:
        gather.begin()

    @second
    def _():
        wait_all(cross_own)
        gathers[2].begin()

    across.begin()

    def stage(i):
        for gather in gathers[:2]:
            gather.stage(i)
        second(lambda: gathers[2].stage(i))

    for j in range(3):
        first(lambda: heads.forward(m * 3 + j))
        stage(j + 1)
    stage(4)
    gathers[0].stage(5)
    other_one = loads.start(
        *[
            (gathered.at[0, j], wqkv.at[:, :, :, lanes_at(j * D + oth * HALF, HALF)])
            for j in range(3)
        ],
        *[
            (gathered.at[0, 3, pl.ds(2 * j, 2)], wo.at[oth, :, :, :, pl.ds(j * HALF, HALF)])
            for j in range(2)
        ],
    )

    @first
    def _():
        wait_all(other_one[:3])
        for j in range(3):
            project(j, oth)

    gathers[1].stage(5)
    other_up = loads.start(
        *[
            (gathered.at[1, j], wup.at[:, :, :, lanes_at(oth * HIDDEN + j * HALF, HALF)])
            for j in range(4)
        ]
    )
    across.share()

    @first
    def _():
        heads.each(heads.forward, oth * 3, oth * 3 + 3)
        heads.finish()

    across.finish()
    other_down = loads.start(
        *[
            (
                gathered.at[2, pl.ds(2 * j, 2)],
                wdn.at[oth, :, :, :, :, pl.ds(j * HALF, HALF)],
            )
            for j in range(2)
        ]
    )

    def feed_forward(source, rows):
        a[rows] = scaled_norm(source[rows], vecs.norm2_gain, vecs.norm2_bias)
        for j, lanes in enumerate(column_chunks()):
            u = mm(a[rows], flat(wup, lanes)) + vecs.up_bias[:, lanes]
            unit, slope = hidden_units(u)
            g[rows, lanes] = unit.astype(BF)
            gp[rows, lanes] = slope.astype(BF)
            term = mm(g[rows, lanes], down_chunk(wdn, j))
            acc[rows] = term if j == 0 else acc[rows] + term

    near = (near_send, near_recv)
    blocks = [pl.ds(0, 160), pl.ds(160, 160), pl.ds(320, R - 320)]
    forth = [remote(out_bf.at[b], xin.at[b], near, i, here.section) for i, b in enumerate(blocks)]
    back = [
        remote(out_bf.at[b], arrived.at[b], near, 3 + i, here.section)
        for i, b in enumerate(blocks)
    ]

    @first
    def _():
        saves = [
            pltpu.make_async_copy(source, target, save_sems.at[i])
            for i, (source, target) in enumerate(zip(saved, saved_out))
        ]
        for copy in saves[:3]:
            copy.start()
        wait_all(own_rest)
        wait_all(other_one[3:])
        x = xin[...].astype(F32) * valid[:, :1]
        x1[...] = x + mm(o[...], flat(wo)) + vecs.attn_bias[...]
        saves[3].start()
        wait_all(other_up)
        wait_all(other_down)
        for rows, copy in zip(blocks, forth):
            feed_forward(x1, rows)
            out_bf[rows] = (x1[rows] + acc[rows] + vecs.down_bias[...]).astype(BF)
            copy.start()
        for copy in saves[4:]:
            copy.start()
        wait_all(saves)
        wait_all(token_loads)
        wait_all(cross_own)
        for copy in forth:
            copy.wait_send()
        for copy in back:
            copy.wait_recv()

    @second
    def _():
        gathers[2].stage(5)
        pairs_cross = [(gathered.at[3, 0], wcq.at[:, :, :, lanes_at(oth * HALF, HALF)])]
        for j in range(2):
            pairs_cross += [
                (gathered.at[3, j + 1], wkv.at[:, :, :, lanes_at(j * D + oth * HALF, HALF)]),
                (
                    gathered.at[3, 3, pl.ds(2 * j, 2)],
                    wcw.at[oth, :, :, :, pl.ds(j * HALF, HALF)],
                ),
            ]
        other_cross = loads.start(*pairs_cross)
        for copies in (own_qkv, own_rest, other_one, other_up, other_down):
            wait_all(copies)
        wait_all(token_loads)
        wait_all(other_cross)
        keep = valid[:, :1]
        ctx[...] = (ctx[...].astype(F32) * keep).astype(BF)
        cot[...] = (cot[...].astype(F32) * keep).astype(BF)
        for j in range(2):
            lanes = pl.ds(j * D, D)
            pairs[:, lanes] = mm(ctx[...], flat(wkv, lanes)).astype(BF)
        lse_lanes[...] = jnp.zeros_like(lse_lanes)
        for copy in forth:
            copy.wait_recv()
        a[...] = scaled_norm(xin[...].astype(F32), vecs.norm1_gain, vecs.norm1_bias)
        for j in range(3):
            lanes = pl.ds(j * D, D)
            qkv[:, lanes] = mm(a[...], flat(wqkv, lanes)).astype(BF)
        heads.each(heads.forward, 0, H // 2)
        heads.finish()
        x1[...] = xin[...].astype(F32) + mm(o[...], flat(wo)) + vecs.attn_bias[...]
        a[...] = scaled_norm(x1[...], vecs.query_gain, vecs.query_bias)
        query[...] = mm(a[...], flat(wcq)).astype(BF)
        cross.each(cross.forward, 0, H // 2)
        cross.finish()
        x2[...] = x1[...] + mm(merged[...], flat(wcw)) + vecs.cross_bias[...]
        feed_forward(x2, pl.ds(0, R))
        acc[...] = (x2[...] + acc[...] + vecs.down_bias[...]) * keep
        own_quarter(here, acc, HALF, joined_own)
        padded(acc, joined_all)

        for j, lanes in enumerate(column_chunks()):
            gp[:, lanes] = (mmt(cot[...], down_chunk(wdn, j)) * gp[:, lanes].astype(F32)).astype(BF)
            term = mmt(gp[:, lanes], flat(wup, lanes))
            acc[...] = term if j == 0 else acc[...] + term
        vec_out[...] = jnp.zeros_like(vec_out)
        dm = acc[...]
        normed, inverse = normalize(x2[...])
        vec_out[3:4, :] = column_sums(dm * normed)
        vec_out[4:5, :] = column_sums(dm)
        acc[...] = cot[...].astype(F32) + norm_grad(dm, normed, inverse, vecs.norm2_gain[...])
        e2[...] = acc[...].astype(BF)
        a[...] = mmt(e2[...], flat(wcw)).astype(BF)
        cross_back = Heads(
            (query, 0), (pairs, 0), (pairs, D), (a, 0), dist, slopes, lse_lanes, lse_cross
        )
        cross_back.prepare(merged, inner)
        cross_back.each(cross_back.backward, 0, H // 2)
        dc = mmt(query[...], flat(wcq))
        normed, inverse = normalize(x1[...])
        vec_out[10:11, :] = column_sums(dc * normed)
        vec_out[11:12, :] = column_sums(dc)
        acc[...] = acc[...] + norm_grad(dc, normed, inverse, vecs.query_gain[...])
        e1[...] = acc[...].astype(BF)
        a[...] = mmt(e1[...], flat(wo)).astype(BF)
        self_back = Heads(
            (qkv, 0), (qkv, D), (qkv, 2 * D), (a, 0), dist, slopes, lse_lanes, lse_rows
        )
        self_back.prepare(o, inner)
        self_back.each(self_back.backward, 0, H // 2)
        sums = []
        for rows, copy in zip(blocks, back):
            da = mmt(qkv[rows], flat(wqkv))
            normed, inverse = normalize(xin[rows].astype(F32))
            sums.append((column_sums(da * normed), column_sums(da)))
            out_bf[rows] = (
                acc[rows] + norm_grad(da, normed, inverse, vecs.norm1_gain[...])
            ).astype(BF)
            copy.start()
        vec_out[0:1, :] = sums[0][0] + sums[1][0] + sums[2][0]
        vec_out[1:2, :] = sums[0][1] + sums[1][1] + sums[2][1]

        staged = Staged(staging, stage_sems)
        acc[...] = mmt(pairs[...], flat(wkv)) * keep
        own_quarter(here, acc, HALF, back_own)
        padded(acc, back_all)
        permute = chunk_order()
        et[...] = mmt(permute, e2[...]).astype(BF)
        staged.put(mm(et[...], merged[...]).astype(BF), halves(gcr, 1, HALF))
        a[...] = scaled_norm(x1[...], vecs.query_gain, vecs.query_bias)
        et[...] = mmt(permute, a[...]).astype(BF)
        staged.put(mm(et[...], query[...]).astype(BF), halves(gcr, 0, 0))
        et[...] = mmt(permute, ctx[...]).astype(BF)
        for j, target in enumerate([(0, HALF), (1, 0)]):
            staged.put(mm(et[...], pairs[:, pl.ds(j * D, D)]).astype(BF), halves(gcr, *target))
        et[...] = cot[...].T
        a[...] = scaled_norm(x2[...], vecs.norm2_gain, vecs.norm2_bias)
        at[...] = a[...].T
        for j, lanes in enumerate(column_chunks()):
            vec_out[6 + j : 7 + j, :] = column_sums(gp[:, lanes])
            staged.put(mm(et[...], g[:, lanes]).astype(BF), quarter_of(gdn, j))
            staged.put(mm(at[...], gp[:, lanes]).astype(BF), quarter_of(gup, j))
        vec_out[2:3, :] = column_sums(e1[...])
        vec_out[5:6, :] = column_sums(cot[...])
        vec_out[12:13, :] = column_sums(e2[...])
        et[...] = e1[...].T
        staged.put(mm(et[...], o[...]).astype(BF), halves(gat, 1, HALF))
        a[...] = scaled_norm(xin[...].astype(F32), vecs.norm1_gain, vecs.norm1_bias)
        at[...] = a[...].T
        for j, target in enumerate([(0, 0), (0, HALF), (1, 0)]):
            staged.put(mm(at[...], qkv[:, pl.ds(j * D, D)]).astype(BF), halves(gat, *target))
        staged.drain()
        for copy in back:
            copy.wait_send()
        gathers[2].drain()

    for gather in gathers[:2] + [across]:
        gather.drain()


def chunk_order():
    r = lax.broadcasted_iota(jnp.int32, (D, 1), 0).astype(F32)
    chunk = jnp.floor((r + 0.5) / 48.0)
    inner = r - chunk * 48.0
    core = (inner >= 24.0).astype(F32)
    inner = inner - 24.0 * core
    section = (inner >= 12.0).astype(F32)
    source = 384.0 * section + 24.0 * chunk + 12.0 * core + inner - 12.0 * section
    columns = lax.broadcasted_iota(jnp.int32, (D, D), 1).astype(F32)
    return (columns == source).astype(F32).astype(BF)


def forward(tiles, slopes, tokens, vecs, own):
    scratch = vmem(
        LAYER_WEIGHTS + CROSS_WEIGHTS + SAVED + EXTRA + WORK + [((R, D), BF)] * 6 + [((2, 4, 4, 48, D), BF)]
    )
    quarter = shape((ROWS // 2, HALF), F32)
    return pl.pallas_call(
        forward_kernel,
        out_shape=[shape((4, 4, 4, 2, 96, HALF), BF), shape((R, D), BF)]
        + [shape(*s) for s in SAVED]
        + [shape((2, 4, 4, 48, 2 * D), BF)] * 4
        + [shape((16, D), F32), quarter, quarter, shape((ROWS, D), BF), shape((ROWS, D), BF)],
        in_specs=[SM, SM] + [ANY] * 3 + [VM] * 10 + [ANY] * 5 + [VM] + [ANY],
        out_specs=[ANY] * 12 + [VM] * 5,
        scratch_shapes=scratch
        + [dma(92), dma(92), dma(6), dma(6), dma(40), dma(7), pltpu.SemaphoreType.DMA((2, 2))],
        compiler_params=pltpu.CompilerParams(
            collective_id=0, has_side_effects=True, vmem_limit_bytes=BIG
        ),
    )(tiles, slopes, *tokens, *vecs, *own)


def backward_kernel(*refs):
    here = Place()
    tiles, slopes, radar, dy_in = refs[:4]
    vecs = Vectors(refs[4:14])
    qkv_own, attn_own, up_own, down_own, gathered, gathered48 = refs[14:20]
    saved_in, refs = refs[20:26], refs[26:]
    vec_in, joined_all, back_all, gcr = refs[:4]
    refs = refs[7:]
    gdn, gup, gat, odn, oup, oat, ocr, vec_total, vec_other, radar_own, quarters, ocr_other = refs[
        :12
    ]
    refs = refs[12:]
    wqkv, wo, wup, wdn = refs[:4]
    saved, refs = refs[4:10], refs[10:]
    qkv, o, lse_rows, x1, g, gp = saved
    a, lse_lanes, acc, et, at, dist, valid, inner = refs[:8]
    xin, radar_all, staging, vec, vbuf = refs[8:13]
    out_bf = radar_all.at[pl.ds(0, R)]
    own_at, cross_sums = refs[13:15]
    buffers, refs = [refs[15 + 7 * i : 22 + 7 * i] for i in range(4)], refs[43:]
    link_send, link_recv, far_send, far_recv, load_sems, local_sems, stage_sems = refs
    m, oth = here.m, here.o
    first, second = pl.when(here.first), pl.when(here.second)
    peers = here.ring + [
        here.sibling,
        here.partner,
        here.diagonal,
        here.along_x[2],
        here.along_z[2],
        here.section,
        here.crossed,
    ]
    here.signal(peers)
    loads = Loads(load_sems)
    links = Links(link_send, link_recv)
    far = (far_send, far_recv)
    staged = Staged(staging, stage_sems)
    heads = Heads((qkv, 0), (qkv, D), (qkv, 2 * D), (a, 0), dist, slopes, lse_lanes, lse_rows)
    chunks = column_chunks()

    cotangent = loads.prepare((dy_in, out_bf))
    units = [loads.prepare((saved_in[4].at[:, c], g.at[j % 2])) for j, c in enumerate(chunks)]
    early = loads.prepare((saved_in[3], x1), (radar.at[m, pl.ds(0, R)], xin))
    copies_down = loads.prepare(
        (down_own, wdn.at[m]),
        *[
            (gathered.at[2, pl.ds(2 * j, 2)], wdn.at[oth, :, :, :, :, pl.ds(j * HALF, HALF)])
            for j in range(2)
        ],
    )
    slopes_of = [loads.prepare((saved_in[5].at[:, c], gp.at[:, c])) for c in chunks]
    copies_up = loads.prepare(
        (up_own, wup.at[:, :, :, lanes_at(m * HIDDEN, HIDDEN)]),
        *[
            (gathered48.at[1, j], wup.at[:, :, :, lanes_at(oth * HIDDEN + j * HALF, HALF)])
            for j in range(4)
        ],
    )
    late = loads.prepare(
        (saved_in[0], qkv),
        (saved_in[1], o),
        (saved_in[2], lse_rows),
        (attn_own, wo.at[m]),
        *[
            (gathered.at[0, 3, pl.ds(2 * j, 2)], wo.at[oth, :, :, :, pl.ds(j * HALF, HALF)])
            for j in range(2)
        ],
    )
    copies_qkv = loads.prepare(
        *[(qkv_own.at[j], wqkv.at[:, :, :, lanes_at(j * D + m * HALF, HALF)]) for j in range(3)],
        *[
            (gathered48.at[0, j], wqkv.at[:, :, :, lanes_at(j * D + oth * HALF, HALF)])
            for j in range(3)
        ],
    )

    @first
    def _():
        for copies in [cotangent] + units[:2] + [early, copies_down] + slopes_of + [copies_up, late]:
            start_all(copies)
        distances(tiles, m, dist, valid)
        vec[...] = jnp.zeros_like(vec)
        wait_all(cotangent)
        e3 = out_bf[...]
        vec[5:6, :] = column_sums(e3)
        et[...] = e3.T
        for j in range(4):
            wait_all(units[j])
            staged.put(mm(et[...], g[j % 2]).astype(BF), quarter_of(gdn, j))
            if j < 2:
                start_all(units[j + 2])
        staged.drain()

    @second
    def _():
        vec[...] = vec_in[...]

    here.await_all(peers)
    low, high = pl.ds(0, 2 * D), pl.ds(2 * D, 2 * D)
    dn = scatter_stages(
        here, links, local_sems.at[0], gdn, odn, wqkv.at[:, :, :, low], buffers[0]
    )
    up = scatter_stages(here, links, local_sems.at[1], gup, oup, wup.at[:, :, :, low], buffers[1])
    mid = scatter_stages(here, links, local_sems.at[2], gat, oat, own_at, buffers[2])
    cross = scatter_stages(
        here, links, local_sems.at[3], gcr, cross_sums, wup.at[:, :, :, high], buffers[3]
    )
    vec_steps = vector_stages(here, links, vec, vbuf, vec_total)

    def quarter_copies(source, kind):
        half_rows = ROWS // 2
        mine, others = rows_at(m * half_rows, half_rows), rows_at(oth * half_rows, half_rows)
        sender, receiver = (0, 1) if kind == 2 else (1, 0)
        same = pl.ds(sender * HALF, HALF)
        over = pl.ds(receiver * HALF, HALF)
        return [
            remote(source.at[mine, over], quarters.at[kind, 0], far, 3 * kind, here.section),
            remote(source.at[others, over], quarters.at[kind, 1], far, 3 * kind + 1, here.crossed),
            remote(source.at[others, same], quarters.at[kind, 1], far, 3 * kind + 2, here.partner),
        ]

    sent = [quarter_copies(s, i) for i, s in enumerate((joined_all, back_all, radar_all))]
    cross_sent = remote(ocr.at[0], ocr_other, far, 9, here.section)
    vec_sent = remote(vec_total, vec_other, far, 10, here.section)

    @second
    def _():
        for copies in sent[:2]:
            for copy in copies:
                copy.start()
        cross[0]()

    dn[0]()
    second(cross[1])

    def chain(j):
        lanes = chunks[j]
        wait_all(slopes_of[j])
        du = (mmt(out_bf[...], down_chunk(wdn, j)) * gp[:, lanes].astype(F32)).astype(BF)
        gp[:, lanes] = du
        vec[6 + j : 7 + j, :] = column_sums(du)
        staged.put(mm(at[...], gp[:, lanes]).astype(BF), quarter_of(gup, j))
        if j == 0:
            wait_all(copies_up)
        term = mmt(gp[:, lanes], flat(wup, lanes))
        acc[...] = term if j == 0 else acc[...] + term

    @first
    def _():
        wait_all(early)
        a[...] = scaled_norm(x1[...], vecs.norm2_gain, vecs.norm2_bias)
        at[...] = a[...].T
        wait_all(copies_down)
        chain(0)
        chain(1)

    dn[1]()

    @first
    def _():
        chain(2)
        chain(3)
        staged.drain()
        wait_all(late)

    up[0]()
    second(cross[2])

    @first
    def _():
        dm = acc[...]
        normed, inverse = normalize(x1[...])
        vec[3:4, :] = column_sums(dm * normed)
        vec[4:5, :] = column_sums(dm)
        acc[...] = out_bf[...].astype(F32) + norm_grad(dm, normed, inverse, vecs.norm2_gain[...])
        e1 = acc[...].astype(BF)
        vec[2:3, :] = column_sums(e1)
        out_bf[...] = e1
        a[...] = mmt(out_bf[...], flat(wo)).astype(BF)
        heads.prepare(o, inner)

    second(cross[3])

    @first
    def _():
        et[...] = out_bf[...].T
        staged.put(mm(et[...], o[...]).astype(BF), halves(gat, 1, HALF))
        heads.backward(0)

    dn[2]()
    up[1]()
    second(cross[4])
    first(lambda: heads.each(heads.backward, 1, 6))
    dn[3]()
    second(cross[5])
    first(lambda: start_all(copies_qkv) and None)

    @first
    def _():
        x = xin[...].astype(F32) * valid[:, :1]
        a[...] = scaled_norm(x, vecs.norm1_gain, vecs.norm1_bias)
        at[...] = a[...].T
        for j, target in enumerate([(0, 0), (0, HALF), (1, 0)]):
            staged.put(mm(at[...], qkv[:, pl.ds(j * D, D)]).astype(BF), halves(gat, *target))
        staged.drain()
        wait_all(copies_qkv)

    mid[0]()

    @first
    def _():
        da = mmt(qkv[...], flat(wqkv))
        normed, inverse = normalize(xin[...].astype(F32) * valid[:, :1])
        vec[0:1, :] = column_sums(da * normed)
        vec[1:2, :] = column_sums(da)
        acc[...] = (acc[...] + norm_grad(da, normed, inverse, vecs.norm1_gain[...])) * valid[:, :1]
        own_quarter(here, acc, 0, radar_own)
        padded(acc, radar_all)
        for copy in sent[2]:
            copy.start()

    @second
    def _():
        for section in range(2):
            for which in range(2):
                ocr[section, which] = cross_sums[which][section * 12 : section * 12 + 12]
        cross_sent.start()

    mid[1]()
    vec_steps[0]()
    vec_steps[1]()
    dn[4]()
    vec_steps[2]()
    up[2]()
    mid[2]()
    vec_steps[3]()
    dn[5]()
    up[3]()
    vec_steps[4]()

    @second
    def _():
        vec_sent.start()

    mid[3]()
    up[4]()
    mid[4]()
    up[5]()
    mid[5]()

    @first
    def _():
        for copies in sent[:2]:
            copies[0].wait_recv()
            copies[1].wait_recv()
        sent[2][2].wait_recv()
        for copy in sent[2]:
            copy.wait_send()
        cross_sent.wait_recv()
        vec_sent.wait_recv()

    @second
    def _():
        sent[2][0].wait_recv()
        sent[2][1].wait_recv()
        for copies in sent[:2]:
            copies[2].wait_recv()
            for copy in copies:
                copy.wait_send()
        cross_sent.wait_send()
        vec_sent.wait_send()


def backward(tiles, slopes, radar, dy, vecs, own, gathered, saved, vec, quarters, gcr, grads):
    scratch = vmem(
        CHUNKED
        + SAVED[:4]
        + [((2, R, D), BF)]
        + SAVED[5:]
        + WORK
        + [((R, D), BF), ((ROWS, D), BF)]
        + [((2, 4, 4, 48, D), BF), ((16, D), F32), ((8, 16, D), F32)]
    )
    vector = shape((16, D), F32)
    qkv, attn, up, down = own
    return pl.pallas_call(
        backward_kernel,
        out_shape=[
            *[shape(array.shape, BF) for array in grads],
            *[shape((2, 24, D), F32)] * 3,
            shape((2, 2, 12, D), F32),
            vector,
            vector,
            shape((ROWS // 2, HALF), F32),
            shape((3, 2, ROWS // 2, HALF), BF),
            shape((2, 12, D), F32),
        ],
        in_specs=[SM, SM, ANY, ANY] + [VM] * 10 + [ANY] * 12 + [VM] + [ANY] * 6,
        out_specs=[ANY] * 3 + [VM] * 7 + [ANY, VM],
        input_output_aliases={30: 0, 31: 1, 32: 2},
        scratch_shapes=scratch
        + own_scratch(2 * D)
        + [pltpu.VMEM((2, 24, D), F32)]
        + scatter_scratch(2 * D) * 4
        + [dma(124), dma(124), dma(11), dma(11), dma(40), dma(4), pltpu.SemaphoreType.DMA((2, 2))],
        compiler_params=pltpu.CompilerParams(
            collective_id=1, has_side_effects=True, vmem_limit_bytes=BIG
        ),
    )(
        tiles,
        slopes,
        radar,
        dy,
        *vecs,
        qkv.reshape(3, 4, 4, 48, HALF),
        attn,
        up.reshape(4, 4, 48, HIDDEN),
        down,
        gathered,
        gathered.reshape(4, 4, 4, 4, 48, HALF),
        *saved,
        vec,
        *quarters,
        gcr,
        *grads,
    )


def local(
    radar_tokens,
    optical_tokens,
    out_cotangent,
    tile_sides,
    norm1_gain,
    norm1_bias,
    qkv_weight,
    attn_weight,
    attn_bias,
    norm2_gain,
    norm2_bias,
    up_weight,
    up_bias,
    down_weight,
    down_bias,
    query_gain,
    query_bias,
    cross_query,
    cross_keyval,
    cross_weight,
    cross_bias,
):
    m = lax.axis_index("mp")
    joining = lax.axis_index("pipe") == 1
    slopes = jnp.exp2(-8.0 * (jnp.arange(H, dtype=jnp.int32) + 1).astype(F32) / H)
    vecs = (
        norm1_gain,
        norm1_bias,
        attn_bias,
        norm2_gain,
        norm2_bias,
        up_bias,
        down_bias,
        query_gain,
        query_bias,
        cross_bias,
    )
    own = (
        qkv_weight[0].transpose(1, 0, 2).reshape(3, 4, 2, 96, HALF),
        attn_weight.reshape(2, 2, 96, D),
        up_weight.reshape(4, 2, 96, HIDDEN),
        down_weight.reshape(2, 4, 2, 96, D),
    )
    cross_own = (
        cross_query.reshape(4, 2, 96, HALF),
        cross_keyval,
        cross_weight.reshape(2, 2, 96, D),
    )
    tokens = (radar_tokens, optical_tokens, out_cotangent)
    results = forward(
        tile_sides, slopes, tokens, vecs, own + cross_own
    )
    gathered, dy0 = results[:2]
    saved = results[2:8]
    grads = results[8:11]
    gcr, vec, joined_own, back_own, joined_all, back_all = results[11:]
    outs = backward(
        tile_sides,
        slopes,
        radar_tokens,
        dy0,
        vecs,
        own,
        gathered,
        saved,
        vec,
        (joined_all, back_all),
        gcr,
        grads,
    )
    odn, oup, oat, ocr, vec, vec_other, radar_own, quarters, ocr_other = outs[3:]

    def placed(own_quarter, kind, here):
        mine = jnp.where(here, own_quarter, quarters[kind, 0].astype(F32))
        others = quarters[kind, 1].astype(F32)
        swap = m == 1
        return jnp.stack([jnp.where(swap, others, mine), jnp.where(swap, mine, others)])

    crossed = jnp.where(joining, vec[10:13], vec_other[10:13])
    ocr = jnp.where(joining, ocr[1], ocr_other)
    q, k = oat[0, :, :HALF], oat[0, :, HALF:]
    v, attn = oat[1, :, :HALF], oat[1, :, HALF:]
    cq, ck = ocr[0, :, :HALF], ocr[0, :, HALF:]
    cv, cw = ocr[1, :, :HALF], ocr[1, :, HALF:]
    return (
        placed(joined_own, 0, joining),
        placed(radar_own, 2, jnp.logical_not(joining)),
        placed(back_own, 1, joining),
        vec[0:1],
        vec[1:2],
        jnp.stack([q, k, v], axis=1)[None],
        attn.T[None],
        vec[2:3],
        vec[3:4],
        vec[4:5],
        jnp.concatenate([oup[0], oup[1]], axis=1)[None],
        vec[6:10].reshape(1, FF),
        jnp.concatenate([odn[0].T, odn[1].T])[None],
        vec[5:6],
        crossed[0],
        crossed[1],
        cq,
        jnp.stack([ck, cv], axis=1),
        cw.T,
        crossed[2],
    )


def solution(mesh):
    in_specs = (
        P(None, "dp", None),
        P(None, "dp", None),
        P(None, "dp", None),
        P(None, "dp"),
        P("pipe", None),
        P("pipe", None),
        P("pipe", None, None, "mp"),
        P("pipe", "mp", None),
        P("pipe", None),
        P("pipe", None),
        P("pipe", None),
        P("pipe", None, "mp"),
        P("pipe", None),
        P("pipe", "mp", None),
        P("pipe", None),
        P(),
        P(),
        P(None, "mp"),
        P(None, None, "mp"),
        P("mp", None),
        P(),
    )
    out_specs = (
        P(None, ("dp", "mp"), "pipe"),
        P(None, ("dp", "mp"), "pipe"),
        P(None, ("dp", "mp"), "pipe"),
        P("pipe", None),
        P("pipe", None),
        P("pipe", "dp", None, "mp"),
        P("pipe", "mp", "dp"),
        P("pipe", None),
        P("pipe", None),
        P("pipe", None),
        P("pipe", "dp", "mp"),
        P("pipe", None),
        P("pipe", "mp", "dp"),
        P("pipe", None),
        P(),
        P(),
        P(("pipe", "dp"), "mp"),
        P(("pipe", "dp"), None, "mp"),
        P("mp", ("pipe", "dp")),
        P(),
    )
    return jax.shard_map(local, mesh=mesh, in_specs=in_specs, out_specs=out_specs, check_vma=False)
```
